128 devices in a mesh: tile: 32 (over x, z, core), spare: 4 (over y).
Axes of the slice: x: 4, y: 4, z: 4, core: 2. Of those that a mesh axis runs over, the one named last changes fastest.
Arguments:
- observed: bfloat16 [128, 32, 128, 128], P('tile', 'spare'), may hold values from -6 to 6
- frame_pick: int32 [128, 32], P('tile', 'spare'), may hold values from 0 to 127, as said below
- frame_count: int32 [128], P('tile'), may hold values from 5 to 32, as said below
- incoming: int32 [128], P('tile'), may hold values from 0 to 127, as said below
- start_coefficients: float32 [128, 36], replicated, may hold values from -1.5 to 1.5
- mode_basis: float32 [36, 128, 128], replicated, may hold values from -6 to 6
Outputs:
- restored: float32 [128, 128, 128], P('tile')
- coefficients: float32 [128, 36], replicated
The draws below stay inside these ranges and needn't reach their ends.
Inputs may be any that keep to these rules, and one draw needn't show every extreme that they name: `frame_pick`: the slots of one patch name distinct frames. `frame_count`: patch 0 uses all 32 slots. `incoming`: A permutation of the patches. Position q (tile index q // 4) takes a patch of the same tile index or of a neighbouring one, with tile indices wrapping around; at most one patch crosses each boundary between neighbouring tile indices in each direction, and when one crosses, one crosses back; the boundary after tile index 0 is crossed in every draw.
All inputs are finite; a program needn't handle non-finite values.
Results may differ from the reference program's by a relative error of at most 0.0003.
Values may be sent and summed in bfloat16 or wider, within the bound.
A program may use at most 128 MiB of HBM per device.

```python
import math
import jax
import jax.numpy as jnp
from jax import lax

NPIX = 128
MODES = 36
FRAMES = 128
PATCH_DEV = 4
ITERS = 2
PATCHES = 128
SLOTS = 32
N_SPARE = 4


def draw_frame_pick(key, part):
    key = jax.random.fold_in(key, 11)
    keys = jax.random.split(key, PATCHES)
    orders = jax.vmap(lambda one_key: jax.random.permutation(one_key, FRAMES))(keys)
    return orders[:, :SLOTS].astype(jnp.int32)


def draw_frame_count(key, part):
    key = jax.random.fold_in(key, 12)
    lowest = max(1, SLOTS // 6)
    counts = jax.random.randint(key, (PATCHES,), lowest, SLOTS + 1)
    return jnp.where(jnp.arange(PATCHES) == 0, SLOTS, counts).astype(jnp.int32)


def draw_incoming(key, part):
    key = jax.random.fold_in(key, 13)
    tiles = PATCHES // PATCH_DEV
    key_swap, key_right, key_apart = jax.random.split(key, 3)
    crossing = jax.random.randint(key_swap, (tiles,), 0, 2)
    crossing = jnp.where(jnp.arange(tiles) == 0, 1, crossing)
    go_right = jax.random.randint(key_right, (tiles,), 0, PATCH_DEV)
    apart = jax.random.randint(key_apart, (tiles,), 1, PATCH_DEV)
    go_left = (go_right + apart) % PATCH_DEV
    places = jnp.arange(tiles)
    after = (places + 1) % tiles
    before = (places - 1) % tiles
    slot_ids = jnp.arange(PATCH_DEV)
    staying = places[:, None] * PATCH_DEV + slot_ids[None, :]
    from_after = (crossing[:, None] == 1) & (slot_ids[None, :] == go_right[:, None])
    from_before = (crossing[before][:, None] == 1) & (slot_ids[None, :] == go_left[:, None])
    arrive_after = (after * PATCH_DEV + go_left[after])[:, None]
    arrive_before = (before * PATCH_DEV + go_right[before])[:, None]
    result = jnp.where(from_after, arrive_after, jnp.where(from_before, arrive_before, staying))
    return result.reshape(-1).astype(jnp.int32)


def steps_of(stream_key, shape, shards, low, high):
    def one(position, shards_of):
        heights = jax.random.uniform(jax.random.fold_in(jax.random.fold_in(stream_key, 6), position), (shards_of,), jnp.float32, low / len(shards), high / len(shards))
        return jnp.repeat(jnp.exp(heights), shape[position] // shards_of).reshape((-1,) + (1,) * (len(shape) - position - 1))

    gain = one(*shards[0])
    for cut in shards[1:]:
        gain = gain * one(*cut)
    return gain


def centred(stream_key, shape, scale, limit, cuts=(), kind=jnp.bfloat16):
    entries = jax.random.normal(stream_key, shape, jnp.float32) * scale
    if len(cuts) > 0:
        entries = steps_of(stream_key, shape, cuts, -0.22, 0.18) * entries
    return jnp.clip(entries, min=-limit, max=limit).astype(kind)


def setup_inputs(seed: int = 0) -> dict:
    arg_keys = jax.random.split(jax.random.key(seed), 7)
    observed = centred(arg_keys[0], (PATCHES, SLOTS, NPIX, NPIX), 1.0, 6.0, ((0, 32), (1, 4)))
    frame_pick = draw_frame_pick(jax.random.fold_in(arg_keys[6], 71), 0)
    frame_count = draw_frame_count(jax.random.fold_in(arg_keys[6], 71), 0)
    incoming = draw_incoming(jax.random.fold_in(arg_keys[6], 71), 0)
    start_coefficients = centred(arg_keys[4], (FRAMES, MODES), 0.25, 1.5, (), jnp.float32)
    mode_basis = centred(arg_keys[5], (MODES, NPIX, NPIX), 1.0, 6.0, (), jnp.float32)
    return {"observed": observed, "frame_pick": frame_pick, "frame_count": frame_count, "incoming": incoming, "start_coefficients": start_coefficients, "mode_basis": mode_basis}


GAMMA = 0.5
STEP = 0.25
EPS = 1e-06
FINE = lax.Precision.HIGHEST

def dft_tables(pixels):
    indices = jnp.arange(pixels, dtype=jnp.int32)
    products = indices[:, None] * indices[None, :] % pixels
    angles = products.astype(jnp.float32) * (2.0 * math.pi / pixels)
    cosine = jnp.cos(angles)
    sine = jnp.sin(angles)
    forward_left = jnp.stack([jnp.stack([cosine, sine]), jnp.stack([-sine, cosine])])
    forward_right = jnp.stack([jnp.stack([cosine, -sine]), jnp.stack([sine, cosine])])
    real_left = jnp.stack([cosine, -sine])
    inverse_left = jnp.stack([jnp.stack([cosine, -sine]), jnp.stack([sine, cosine])])
    inverse_right = jnp.stack([jnp.stack([cosine, sine]), jnp.stack([-sine, cosine])])
    return (forward_left, forward_right, real_left, inverse_left, inverse_right)

def pupil_mask(pixels):
    offsets = jnp.arange(pixels, dtype=jnp.int32) - pixels // 2
    radial = offsets[:, None] ** 2 + offsets[None, :] ** 2
    return (radial <= (pixels // 4) ** 2).astype(jnp.float32)

def complex_transform(fields, left_op, right_op, factor):
    halfway = jnp.einsum('jkuv,nkvy->njuy', left_op, fields, precision=FINE)
    return jnp.einsum('nkxy,kjyz->njxz', halfway, right_op, precision=FINE) * factor

def real_transform(images, real_left, right_op, factor):
    halfway = jnp.einsum('juv,nvy->njuy', real_left, images, precision=FINE)
    return jnp.einsum('nkxy,kjyz->njxz', halfway, right_op, precision=FINE) * factor

def frame_terms(coef_rows, basis_flat, spectra, tables, aperture):
    pixels = aperture.shape[0]
    phases = jnp.dot(coef_rows, basis_flat, precision=FINE).reshape(-1, pixels, pixels)
    fields = jnp.stack([aperture * jnp.cos(phases), aperture * jnp.sin(phases)], axis=1)
    amplitude = complex_transform(fields, tables[0], tables[1], 1.0 / pixels)
    spread = (amplitude[:, 0] ** 2 + amplitude[:, 1] ** 2) / jnp.sum(aperture)
    transfer = real_transform(spread, tables[2], tables[1], 1.0)
    crossed = jnp.stack([spectra[:, 0] * transfer[:, 0] + spectra[:, 1] * transfer[:, 1], spectra[:, 1] * transfer[:, 0] - spectra[:, 0] * transfer[:, 1]], axis=1)
    powers = transfer[:, 0] ** 2 + transfer[:, 1] ** 2
    return (crossed, powers)

def patch_loss(numer, denom):
    return -jnp.sum((numer[..., 0, :, :] ** 2 + numer[..., 1, :, :] ** 2) / (GAMMA + denom))

def object_image(numer, denom, tables):
    pixels = numer.shape[-1]
    ratio = numer / (GAMMA + denom)[:, None, :, :]
    return complex_transform(ratio, tables[3], tables[4], 1.0 / pixels)[:, 0]

def patch_sums(coef, images, picks, count, basis_flat, tables, aperture):
    slots = picks.shape[0]
    per_spare = slots // N_SPARE
    pixels = aperture.shape[0]
    order = jnp.arange(slots, dtype=jnp.int32)
    weights = (order % per_spare * N_SPARE + order // per_spare < count).astype(jnp.float32)
    spectra = real_transform(images.astype(jnp.float32), tables[2], tables[1], 1.0 / pixels)
    select = (picks[:, None] == jnp.arange(coef.shape[0], dtype=jnp.int32)[None, :]).astype(jnp.float32)
    coef_rows = jnp.dot(select, coef, precision=FINE)
    crossed, powers = frame_terms(coef_rows, basis_flat, spectra, tables, aperture)
    numer = jnp.einsum('k,kjxy->jxy', weights, crossed, precision=FINE)
    denom = jnp.einsum('k,kxy->xy', weights, powers, precision=FINE)
    return (numer, denom)

def reference(observed, frame_pick, frame_count, incoming, start_coefficients, mode_basis):
    pixels = observed.shape[-1]
    tables = dft_tables(pixels)
    aperture = pupil_mask(pixels)
    basis_flat = mode_basis.reshape(mode_basis.shape[0], pixels * pixels)

    def total_loss(coef):

        def one_patch(items):
            numer, denom = patch_sums(coef, items[0], items[1], items[2], basis_flat, tables, aperture)
            return patch_loss(numer, denom)
        return jnp.sum(lax.map(jax.checkpoint(one_patch), (observed, frame_pick, frame_count)))
    coef = start_coefficients
    for iteration in range(ITERS):
        gradient = jax.grad(total_loss)(coef)
        spread = jnp.sqrt(jnp.mean(gradient * gradient) + EPS)
        coef = coef - STEP * gradient / spread

    def one_object(items):
        numer, denom = patch_sums(coef, items[0], items[1], items[2], basis_flat, tables, aperture)
        return object_image(numer[None], denom[None], tables)[0]
    objects = lax.map(one_object, (observed, frame_pick, frame_count))
    return (jnp.take(objects, incoming, axis=0), coef)
```

```python
import math

import jax
import jax.numpy as jnp
import ml_dtypes
import numpy as np
from jax import lax
from jax.experimental import pallas as pl
from jax.experimental.pallas import tpu as pltpu
from jax.sharding import PartitionSpec as P

MESH = pl.DeviceIdType.MESH
F32 = jnp.float32
BF16 = jnp.bfloat16
NPIX = 128
ITERS = 2
GAMMA = 0.5
STEP = 0.25
EPS = 1e-06
X0, XN = 32, 72
MROWS = 40
FR = 32
QUADS = 8
TILES = 17


def host_tables():
    index = np.arange(NPIX)
    angle = 2.0 * np.pi * (index[:, None] * index[None, :] % NPIX) / NPIX
    c, s = np.cos(angle), np.sin(angle)
    w1 = np.block([[c, -s], [s, c]]) / NPIX
    ma = np.block([[c, s], [-s, c]])
    rows = X0 + np.arange(XN)
    rows[65] = NPIX // 2
    ma = np.concatenate([ma[:, rows], ma[:, NPIX + rows]], axis=1)
    w1 = np.concatenate([w1[32:96], w1[160:224]], axis=0)
    w1t = np.concatenate([w1[64:].T, -w1[:64].T], axis=1)
    ch, sh = c[:, :64], -s[:, :64].copy()
    sh[:, 0] = c[:, 64]
    zero = np.zeros((NPIX, 64))
    rt = np.block([[ch, zero, sh, zero], [zero, ch, zero, sh]])
    m2 = np.block([[c, s], [-s, c]])

    def parts(table, axis):
        high = table.astype(ml_dtypes.bfloat16)
        low = (table - high.astype(np.float64)).astype(ml_dtypes.bfloat16)
        return np.concatenate([high, high, low], axis=axis)

    out = [parts(one, 0) for one in (w1, rt, rt.T, w1t)] + [parts(one, 1) for one in (m2, m2.T, ma, ma.T)]
    off = index - NPIX // 2
    disc = (off[:, None] ** 2 + off[None, :] ** 2 <= (NPIX // 4) ** 2).astype(np.float32)
    mask = np.zeros((XN, 64), np.float32)
    mask[:65] = disc[X0 : X0 + 65, 32:96]
    mask[65, 0] = disc[64, 96]
    mask = np.concatenate([mask, mask], axis=1)
    weight = np.full((NPIX, NPIX), 4.0, np.float32)
    weight[:, 0] = 2.0
    weight[:, 64] = 2.0
    weight[64, 1] = 2.0
    weight[64, 65] = 2.0
    return out, mask, weight, float(disc.sum())


def split(x):
    high = x.astype(BF16)
    return high, (x - high.astype(F32)).astype(BF16)


def split3(x):
    high = x.astype(BF16).astype(F32)
    rest = x - high
    mid = rest.astype(BF16).astype(F32)
    return high, mid, rest - mid


def mm(a, b):
    return jnp.dot(a, b, preferred_element_type=F32)


def mm_nt(a, b):
    return lax.dot_general(a, b, (((1,), (1,)), ((), ())), preferred_element_type=F32)


def right_mul(x, table):
    high, low = split(x)
    return mm(jnp.concatenate([high, low, high], axis=1), table[...])


def left_mul(table, x):
    high, low = split(x)
    return mm(table[...], jnp.concatenate([high, low, high], axis=0))


COS_POLY = (1.0, -4.93480214, 4.05870915, -1.33521195, 0.23493707, -0.02439593)


def horner(poly, z):
    total = poly[-1]
    for one in poly[-2::-1]:
        total = total * z + one
    return total


def unit_field(half_turns, mask):
    k = jnp.floor(half_turns + 0.5)
    r = half_turns - k
    signed = mask * (1.0 - 2.0 * k + 4.0 * jnp.floor(0.5 * k))
    return signed * horner(COS_POLY, r * r)


def lane_mask(width, first):
    lane = lax.broadcasted_iota(jnp.int32, (8, width), 1)
    return (lane % 64) == first


def rows64(arr, fix):
    return jnp.concatenate([arr[:64], fix(arr[64:72]), arr[72:]], axis=0)


def half_spectra(d_pairs):
    real, imag, lone = [], [], []
    at0 = lane_mask(128, 0)[:1]
    for d in d_pairs:
        di = d[:, 128:]
        total = jnp.sum(di, axis=0, keepdims=True)
        lone.append(pltpu.roll(jnp.broadcast_to(total, (8, 128)), 1, 1))
        real.append(d[:, :128])
        imag.append(jnp.where(at0, 0.0, di))
    return (
        jnp.concatenate([jnp.concatenate(real, axis=1), jnp.concatenate(imag, axis=1)], axis=0),
        jnp.concatenate(lone, axis=1),
    )


def put_lone(t, lone):
    row = lax.broadcasted_iota(jnp.int32, (8, 256), 0)
    here = lane_mask(256, 1) & (row == 0)
    return (
        rows64(t[:128], lambda v: jnp.where(here, lone, v)),
        rows64(t[128:], lambda v: jnp.where(here, 0.0, v)),
    )


def adjoint_images(gr, gi, m2t, rtt):
    row = lax.broadcasted_iota(jnp.int32, (8, 256), 0)
    here = lane_mask(256, 1) & (row == 0)
    lone = jnp.where(here, gr[64:72], 0.0)
    gr = rows64(gr, lambda v: jnp.where(here, 0.0, v))
    gi = rows64(gi, lambda v: jnp.where(here, 0.0, v))
    d = left_mul(m2t, jnp.concatenate([gr, gi], axis=0))
    at0 = lane_mask(128, 0)[:1]
    parts = []
    for i in range(2):
        back = pltpu.roll(lone[:, 128 * i : 128 * i + 128], 127, 1)[:1]
        di = jnp.where(at0, back, d[128:, 128 * i : 128 * i + 128])
        parts.append(jnp.concatenate([d[:128, 128 * i : 128 * i + 128], di], axis=1))
    return right_mul(jnp.concatenate(parts, axis=0), rtt)


def frames_of(g):
    pp, kk = g // 4, g % 4
    return [[(2 * pp + h) * 8 + 2 * kk + i for h in range(2)] for i in range(2)]


def h_frame(h, i, half):
    return (2 * (h // 2) + half) * 8 + 4 * (h % 2) + i


def make_kernel(area):
    inv_area = float(np.float32(1.0 / area))

    def prep_spectra(g, observed, rt, m2, spec):
        pairs = []
        for left, right in frames_of(g):
            image = jnp.concatenate([observed[left], observed[right]], axis=1)
            pairs.append(mm(jnp.concatenate([image, image], axis=1), rt[256:768]) * (1.0 / NPIX))
        side, lone = half_spectra(pairs)
        real, imag = put_lone(left_mul(m2, side), lone)
        spec[g, :128, :] = real
        spec[g, 128:, :] = imag

    def prep_basis(i, basis, basis6, last=False):
        lane = lax.broadcasted_iota(jnp.int32, (MROWS, 128), 1)
        halves = []
        for j in range(2):
            if last:
                rows = pltpu.roll(basis[pl.ds(64 - 32 * j, MROWS, stride=XN), :], 96 - 64 * j, 1)
            else:
                one = pltpu.roll(basis[pl.ds(2 * i + j, MROWS, stride=XN), :], 96, 1)
                other = pltpu.roll(basis[pl.ds(2 * i + j + 32, MROWS, stride=XN), :], 32, 1)
                rows = jnp.where(lane < 64, one, other)
            high, mid, low = split3(rows)
            halves.append(
                jnp.concatenate([high, mid, high, low, mid, high, jnp.zeros((16, NPIX), F32)], axis=0)
            )
        basis6[i] = jnp.concatenate(halves, axis=1).astype(BF16)

    def coef_six(coef, onehot):
        high, mid, low = split3(coef[...] * (1.0 / math.pi))
        stack = jnp.concatenate([high, high, mid, high, mid, low, jnp.zeros((16, NPIX), F32)], axis=0)
        return mm_nt(onehot[...].astype(BF16), stack.astype(BF16)).astype(BF16)

    def phases(six, basis6, phi):
        for i in range(TILES):
            both = mm(six[...], basis6[i])
            phi[pl.ds(2 * i * FR, FR), :] = both[:, :128]
            phi[pl.ds((2 * i + 1) * FR, FR), :] = both[:, 128:]

    def frame_field(f, phi, mask):
        lane = lax.broadcasted_iota(jnp.int32, (8, 128), 1)[:1]
        packed = phi[pl.ds(f, 40, stride=FR), :]
        turned = pltpu.roll(packed, 64, 1)
        phase = jnp.concatenate(
            [jnp.where(lane < 64, packed, turned), jnp.where(lane < 64, turned[:32], packed[:32])], axis=0
        )
        phase = jnp.concatenate([phase[:32], phase[40:], phase[32:40]], axis=0)
        return unit_field(phase - jnp.where(lane < 64, 0.0, 0.5), mask[...])

    def modes(dphi, basis6):
        total = None
        for i in range(TILES):
            a = dphi[pl.ds(2 * i * FR, FR), :]
            b = dphi[pl.ds((2 * i + 1) * FR, FR), :]
            high, low = split(jnp.concatenate([a, b], axis=1))
            part = mm_nt(basis6[i, 0 : 2 * MROWS, :], jnp.concatenate([high, low], axis=0))
            total = part if total is None else total + part
        return total

    def forward(h, it, phi, mask, flip, w1, ma, rt, m2, spec, used, field, amp, trans, sums):
        pp = h // 2
        stack = []
        for i in range(4):
            for half in range(2):
                f = h_frame(h, i, half)
                one = frame_field(f, phi, mask)
                field[f] = one
                stack.append(one)
        b = right_mul(jnp.concatenate(stack, axis=0), w1)
        spreads = []
        for i in range(4):
            parts = []
            for half in range(2):
                one = b[XN * (2 * i + half) : XN * (2 * i + half + 1)]
                parts.append(jnp.concatenate([one[:64], one[64:] * flip[...]], axis=0))
            side = jnp.concatenate(
                [
                    jnp.concatenate([parts[0][:, :128], parts[1][:, :128]], axis=1),
                    jnp.concatenate([parts[0][:, 128:], parts[1][:, 128:]], axis=1),
                ],
                axis=0,
            )
            a = left_mul(ma, side)
            amp[4 * h + i] = a
            spreads.append((a[:128] * a[:128] + a[128:] * a[128:]) * inv_area)
        d = right_mul(jnp.concatenate(spreads, axis=0), rt)
        total = [None] * 3
        for j in range(2):
            g = 2 * h + j
            side, lone = half_spectra([d[256 * j : 256 * j + 128], d[256 * j + 128 : 256 * j + 256]])
            tr, ti = put_lone(left_mul(m2, side), lone)
            trans[g, :128, :] = tr
            trans[g, 128:, :] = ti
            sr, si = spec[g, :128, :], spec[g, 128:, :]
            row = 8 * pp + 4 * (h % 2) + 2 * j
            ua, ub = used[pl.ds(row, 1), :], used[pl.ds(row + 1, 1), :]
            for n, v in enumerate((sr * tr + si * ti, si * tr - sr * ti, tr * tr + ti * ti)):
                one = v[:, :128] * ua + v[:, 128:] * ub
                total[n] = one if j == 0 else total[n] + one
        first = h % 2 == 0
        for n in range(3):
            sums[it, pp, n] = jnp.where(first, 0.0, sums[it, pp, n]) + total[n]

    def backward(h, cot, spec, trans, used, flip, m2t, rtt, mat, w1t, amp, field, dphi):
        pp = h // 2
        images = []
        for j in range(2):
            g = 2 * h + j
            row = 8 * pp + 4 * (h % 2) + 2 * j
            u = jnp.concatenate([used[pl.ds(row, 1), :], used[pl.ds(row + 1, 1), :]], axis=1)
            qr, qi, qq = [jnp.concatenate([cot[pp, n], cot[pp, n]], axis=1) for n in range(3)]
            tr, ti = trans[g, :128, :], trans[g, 128:, :]
            sr, si = spec[g, :128, :], spec[g, 128:, :]
            gr = u * (qq * tr - qr * sr - qi * si)
            gi = u * (qi * sr - qr * si + qq * ti)
            images.append(adjoint_images(gr, gi, m2t, rtt))
        stack = []
        for i in range(4):
            a = amp[4 * h + i]
            one = images[i // 2][128 * (i % 2) : 128 * (i % 2) + 128] * (2.0 * inv_area)
            db = left_mul(mat, jnp.concatenate([a[:128] * one, a[128:] * one], axis=0))
            for half in range(2):
                cols = slice(128 * half, 128 * half + 128)
                one = jnp.concatenate([db[:XN, cols], db[XN:, cols]], axis=1)
                stack += [one[:64], one[64:] * flip[...]]
        d = right_mul(jnp.concatenate(stack, axis=0), w1t)
        lane = lax.broadcasted_iota(jnp.int32, (8, 128), 1)[:1]
        for i in range(4):
            for half in range(2):
                f, place = h_frame(h, i, half), 2 * i + half
                v = field[f] * d[XN * place : XN * place + XN]
                v = v + pltpu.roll(v, 64, 1)
                dphi[pl.ds(f, 40, stride=FR), :] = jnp.concatenate(
                    [jnp.where(lane < 64, v[:32], v[32:64]), jnp.where(lane < 64, v[64:], 0.0)], axis=0
                )

    def kernel(
        observed_h, basis_h, pick, count, coef0, incoming, mask, weight, flip,
        right_h, m2_h, ma_h, mat_h, w1_h, w1t_h,
        out, coef_out,
        observed, basis, onehot, used, coef, own, right, left, ma, mat, w1, w1t,
        spec, basis6, six, phi, dphi, field, amp, trans, sums, slots, ratio, cot, grads, objects, near, send, arrive,
        rs_send, rs_recv, ag_send, ag_recv, gr_send, gr_recv, nb_send, nb_recv, basis_sem, load_sem,
    ):
        rt, rtt = right.at[0], right.at[1]
        m2, m2t = left.at[0], left.at[1]
        t, s = lax.axis_index("tile"), lax.axis_index("spare")
        tx, tz, tc = t // 8, (t // 2) % 4, t % 2
        spare_of = [(s + d) % 4 for d in (1, 2, 3)]
        groups = [
            [(t, v) for v in spare_of] + [(t + 1 - 2 * tc, (s + d) % 4) for d in range(4)],
            [(((tx + d) % 4) * 8 + tz * 2 + tc, s) for d in (1, 2, 3)],
            [(tx * 8 + ((tz + d) % 4) * 2 + tc, s) for d in (1, 2, 3)],
        ]
        places = [tc * 4 + s, tx, tz]
        beside = [((t + 1) % 32, s), ((t + 31) % 32, s)]

        barrier = pltpu.get_barrier_semaphore()
        partners = [who for group in groups for who in group] + beside
        for who in partners:
            pl.semaphore_signal(barrier, inc=1, device_id=who, device_id_type=MESH)

        loads = [
            pltpu.make_async_copy(src, dst, load_sem.at[n])
            for n, (src, dst) in enumerate(
                [(observed_h, observed), (right_h, right), (m2_h, left), (ma_h, ma), (mat_h, mat), (w1_h, w1), (w1t_h, w1t)]
            )
        ]
        windows = [
            pltpu.make_async_copy(
                basis_h.at[m, pl.ds(X0, XN), :], basis.at[pl.ds(m * XN, XN), :], basis_sem.at[m]
            )
            for m in range(36)
        ]
        for one in windows + loads:
            one.start()

        def remote(src, dst, ssem, rsem, who):
            return pltpu.make_async_remote_copy(
                src_ref=src, dst_ref=dst, send_sem=ssem, recv_sem=rsem, device_id=who, device_id_type=MESH
            )

        def near_copy(d):
            return remote(own, near.at[d], nb_send.at[0, d], nb_recv.at[0, d], beside[d])

        def object_copy(d):
            return remote(send.at[d], arrive.at[d], nb_send.at[1, d], nb_recv.at[1, d], beside[d])

        def scatter_copy(it, pp, d):
            rows = pl.ds(pl.multiple_of(spare_of[d] * 32, 32), 32)
            return remote(
                sums.at[it, pp, :, rows, :], slots.at[it, pp, d], rs_send.at[it, pp, d], rs_recv.at[it, pp, d], groups[0][d]
            )

        my_rows = pl.ds(pl.multiple_of(s * 32, 32), 32)

        def gather_copy(it, pp, d):
            here = ratio.at[it, pp, :, my_rows, :]
            return remote(here, here, ag_send.at[it, pp, d], ag_recv.at[it, pp, d], groups[0][d])

        def grad_copy(it, stage, d):
            here = grads.at[it, stage, places[stage]]
            return remote(here, here, gr_send.at[it, stage, d], gr_recv.at[it, stage, d], groups[stage][d])

        def scatter_start(it, pp):
            for d in range(3):
                scatter_copy(it, pp, d).start()

        def scatter_finish(it, pp):
            for d in range(3):
                scatter_copy(it, pp, d).wait()
            total = [
                sums[it, pp, j, my_rows, :] + slots[it, pp, 0, j] + slots[it, pp, 1, j] + slots[it, pp, 2, j]
                for j in range(3)
            ]
            scale = 1.0 / (GAMMA + total[2])
            ratio[it, pp, 0, my_rows, :] = total[0] * scale
            ratio[it, pp, 1, my_rows, :] = total[1] * scale
            for d in range(3):
                gather_copy(it, pp, d).start()

        def gather_finish(it, pp):
            for d in range(3):
                gather_copy(it, pp, d).wait()
            qr, qi = ratio[it, pp, 0], ratio[it, pp, 1]
            cot[pp, 0] = weight[...] * qr
            cot[pp, 1] = weight[...] * qi
            cot[pp, 2] = weight[...] * (qr * qr + qi * qi)

        lane = lax.broadcasted_iota(jnp.int32, (8, 128), 1)
        wanted = jnp.full((8, 128), -1, jnp.int32)
        for j in range(4):
            wanted = jnp.where(lane == j, incoming[j], wanted)
        own[...] = wanted
        for f in range(FR):
            onehot[pl.ds(f, 1), :] = jnp.where(lane[:1] == pick[f // 8, f % 8], 1.0, 0.0)
        for row in range(16):
            pair, k = row // 8, row % 8
            bound = jnp.where(lane[:1] < 64, count[2 * pair], count[2 * pair + 1])
            used[pl.ds(row, 1), :] = jnp.where(4 * k + s < bound, 1.0, 0.0)
        coef[...] = jnp.zeros_like(coef)
        coef[0:36, :] = coef0[...]
        basis[pl.ds(36 * XN, 4 * XN), :] = jnp.zeros((4 * XN, NPIX), F32)
        for one in windows:
            one.wait()
        pl.loop(0, TILES - 1)(lambda i: prep_basis(i, basis, basis6))
        prep_basis(TILES - 1, basis, basis6, last=True)
        phi[pl.ds(2 * TILES * FR, 6 * FR), :] = jnp.zeros((6 * FR, 128), F32)
        for one in loads:
            one.wait()
        pl.loop(0, QUADS, unroll=2)(lambda g: prep_spectra(g, observed, rt, m2, spec))
        pl.semaphore_wait(barrier, len(partners))
        for d in range(2):
            near_copy(d).start()

        @pl.loop(0, ITERS + 1)
        def iteration(it):
            six[...] = coef_six(coef, onehot)
            phases(six, basis6, phi)

            @pl.loop(0, QUADS // 2)
            def forward_quads(h):
                forward(h, it, phi, mask, flip, w1, ma, rt, m2, spec, used, field, amp, trans, sums)

                @pl.when(h == 1)
                def _():
                    scatter_start(it, 0)

                @pl.when(h == 2)
                def _():
                    scatter_finish(it, 0)

                @pl.when(h == 3)
                def _():
                    scatter_start(it, 1)
                    gather_finish(it, 0)

            @pl.when(it < ITERS)
            def _():
                @pl.loop(0, QUADS // 2)
                def backward_quads(h):
                    @pl.when(h == 1)
                    def _():
                        scatter_finish(it, 1)

                    @pl.when(h == 2)
                    def _():
                        gather_finish(it, 1)

                    backward(h, cot, spec, trans, used, flip, m2t, rtt, mat, w1t, amp, field, dphi)

                acc = modes(dphi, basis6)
                slot_grad = acc[:MROWS] + acc[MROWS:]
                twice = jnp.concatenate([onehot[...], onehot[...]], axis=0).astype(BF16)
                total = None
                for part in split3(slot_grad):
                    one = mm(part.astype(BF16), twice)
                    total = one if total is None else total + one
                for stage in range(3):
                    grads[it, stage, places[stage]] = total
                    count = len(groups[stage])
                    for d in range(count):
                        grad_copy(it, stage, d).start()
                    for d in range(count):
                        grad_copy(it, stage, d).wait()
                    total = grads[it, stage, 0]
                    for d in range(count):
                        total = total + grads[it, stage, d + 1]
                mean = jnp.sum(total * total) * (1.0 / (128.0 * 36.0))
                coef[...] = coef[...] - STEP * total / jnp.sqrt(jnp.full(total.shape, mean + EPS, F32))

        scatter_finish(ITERS, 1)
        gather_finish(ITERS, 1)
        gr = jnp.concatenate([cot[0, 0], cot[1, 0]], axis=1) * (0.5 / NPIX)
        gi = jnp.concatenate([cot[0, 1], cot[1, 1]], axis=1) * (0.5 / NPIX)
        images = adjoint_images(gr, gi, m2t, rtt)
        for p in range(4):
            objects[p] = images[128 * (p // 2) : 128 * (p // 2) + 128, 128 * (p % 2) : 128 * (p % 2) + 128]

        for d in range(2):
            near_copy(d).wait()
        for d in range(2):
            wanted = near[1 - d]
            total = None
            for p in range(4):
                match = jnp.where(wanted == 4 * t + p, 1.0, 0.0)
                one = jnp.max(match[:1, :], axis=1, keepdims=True) * objects[p]
                total = one if total is None else total + one
            send[d] = total
            object_copy(d).start()
        for d in range(2):
            object_copy(d).wait()
        for j in range(4):
            source = incoming[j]
            total = jnp.where(source // 4 == (t + 31) % 32, arrive[0], arrive[1])
            for p in range(4):
                total = jnp.where(source == 4 * t + p, objects[p], total)
            out[j] = total
        coef_out[...] = coef[0:36, :]

    return kernel


def per_device(observed, frame_pick, frame_count, incoming, start_coefficients, mode_basis):
    tables, mask, weight, area = host_tables()
    flip = np.ones((8, 256), np.float32)
    flip[1, 1::2] = -1.0
    vmem = pl.BlockSpec(memory_space=pltpu.VMEM)
    smem = pl.BlockSpec(memory_space=pltpu.SMEM)
    hbm = pl.BlockSpec(memory_space=pl.ANY)
    dma = pltpu.SemaphoreType.DMA
    steps = ITERS + 1
    objects, coef = pl.pallas_call(
        make_kernel(area),
        out_shape=(
            jax.ShapeDtypeStruct((4, NPIX, NPIX), F32),
            jax.ShapeDtypeStruct((36, 128), F32),
        ),
        in_specs=[hbm, hbm, smem, smem, vmem, smem, vmem, vmem, vmem] + [hbm] * 6,
        out_specs=(vmem, vmem),
        scratch_shapes=[
            pltpu.VMEM((FR, NPIX, NPIX), BF16),
            pltpu.VMEM((MROWS * XN, NPIX), F32),
            pltpu.VMEM((FR, 128), F32),
            pltpu.VMEM((16, 128), F32),
            pltpu.VMEM((MROWS, 128), F32),
            pltpu.VMEM((8, 128), jnp.int32),
            pltpu.VMEM((2, 768, 256), BF16),
            pltpu.VMEM((2, 256, 768), BF16),
            pltpu.VMEM((256, 6 * XN), BF16),
            pltpu.VMEM((2 * XN, 768), BF16),
            pltpu.VMEM((384, 256), BF16),
            pltpu.VMEM((768, 128), BF16),
            pltpu.VMEM((QUADS, 256, 256), F32),
            pltpu.VMEM((TILES, 256, 256), BF16),
            pltpu.VMEM((FR, 256), BF16),
            pltpu.VMEM((40 * FR, 128), F32),
            pltpu.VMEM((40 * FR, 128), F32),
            pltpu.VMEM((FR, XN, 128), F32),
            pltpu.VMEM((2 * QUADS, 256, 256), F32),
            pltpu.VMEM((QUADS, 256, 256), F32),
            pltpu.VMEM((steps, 2, 3, 128, 128), F32),
            pltpu.VMEM((steps, 2, 3, 3, 32, 128), F32),
            pltpu.VMEM((steps, 2, 2, 128, 128), F32),
            pltpu.VMEM((2, 3, 128, 128), F32),
            pltpu.VMEM((ITERS, 3, 8, MROWS, 128), F32),
            pltpu.VMEM((4, 128, 128), F32),
            pltpu.VMEM((2, 8, 128), jnp.int32),
            pltpu.VMEM((2, 128, 128), F32),
            pltpu.VMEM((2, 128, 128), F32),
            dma((steps, 2, 3)),
            dma((steps, 2, 3)),
            dma((steps, 2, 3)),
            dma((steps, 2, 3)),
            dma((ITERS, 3, 7)),
            dma((ITERS, 3, 7)),
            dma((2, 2)),
            dma((2, 2)),
            dma((36,)),
            dma((7,)),
        ],
        compiler_params=pltpu.CompilerParams(
            collective_id=0, has_side_effects=True, vmem_limit_bytes=56 * 1024 * 1024
        ),
        cost_estimate=pl.CostEstimate(flops=30_000_000_000, bytes_accessed=10_000_000, transcendentals=0),
    )(
        observed.reshape(FR, NPIX, NPIX), mode_basis, frame_pick, frame_count, start_coefficients.T, incoming,
        jnp.asarray(mask), jnp.asarray(weight), jnp.asarray(flip),
        jnp.asarray(np.stack(tables[1:3])), jnp.asarray(np.stack(tables[4:6])),
        *[jnp.asarray(tables[n]) for n in (6, 7, 0, 3)],
    )
    return objects, coef.T


def solution(mesh):
    placed = (P("tile", "spare", None, None), P("tile", "spare"), P("tile"), P("tile"), P(), P())
    return jax.shard_map(
        per_device,
        mesh=mesh,
        in_specs=placed,
        out_specs=(P("tile", None, None), P()),
        check_vma=False,
    )
```

```python
import math

import jax
import jax.numpy as jnp
import ml_dtypes
import numpy as np
from jax import lax
from jax.experimental import pallas as pl
from jax.experimental.pallas import tpu as pltpu
from jax.sharding import PartitionSpec as P

MESH = pl.DeviceIdType.MESH
F32 = jnp.float32
BF16 = jnp.bfloat16
NPIX = 128
ITERS = 2
GAMMA = 0.5
STEP = 0.25
EPS = 1e-06
X0, XN = 32, 72
MROWS = 40
FR = 32
QUADS = 8
PAIRS = 4
STEPS = 16 // PAIRS
TILES = 17


def host_tables():
    index = np.arange(NPIX)
    angle = 2.0 * np.pi * (index[:, None] * index[None, :] % NPIX) / NPIX
    c, s = np.cos(angle), np.sin(angle)
    off = index - NPIX // 2
    disc = (off[:, None] ** 2 + off[None, :] ** 2 <= (NPIX // 4) ** 2).astype(np.float32)
    area = float(disc.sum())

    def two(table):
        high = table.astype(ml_dtypes.bfloat16)
        return high, (table - high.astype(np.float64)).astype(ml_dtypes.bfloat16)

    def wide(table, extra=0):
        high, low = two(table)
        return np.concatenate([high, high, low, np.zeros((len(table), extra), high.dtype)], axis=1)

    def tall(table):
        high, low = two(table)
        return np.concatenate([high, high, low], axis=0)

    def beside(table):
        return np.concatenate(two(table), axis=1)

    w1 = np.block([[c[32:96], -s[32:96]], [s[32:96], c[32:96]]]) / (NPIX * math.sqrt(area))
    w1t = np.concatenate([w1[64:].T, -w1[:64].T], axis=1)
    rows = np.concatenate([c[:64], c[64:65], s[1:64]], axis=0)
    order = np.concatenate([np.arange(65), 128 - np.arange(1, 64)])
    pupil = X0 + np.arange(XN)
    pupil[65] = NPIX // 2
    a2 = rows[:, pupil]
    a2t = np.concatenate([a2.T, np.zeros((8, NPIX))], axis=0)
    t2 = rows[:, order]
    cosine, sine = c[:, :64], -s[:, :64].copy()
    sine[:, 0] = c[:, 64]
    left, right = np.concatenate([cosine, sine], axis=1), np.concatenate([sine, cosine], axis=1)

    def twice(table):
        one = beside(table)
        return np.concatenate([one, one], axis=0)

    tables = [
        np.stack([twice(left), twice(right), twice(2.0 * left.T), twice(2.0 * right.T)]),
        np.stack([wide(t2), wide(t2.T), wide(rows), wide(rows.T)]),
        wide(a2, 8),
        wide(a2t),
        tall(w1),
        beside(w1t),
    ]
    mask = np.zeros((XN, 64), np.float32)
    mask[:65] = disc[X0 : X0 + 65, 32:96]
    mask[65, 0] = disc[64, 96]
    mask = np.concatenate([mask, mask], axis=1)
    weight = np.full((NPIX, NPIX), 4.0, np.float32)
    weight[:, 0] = 2.0
    weight[:, 64] = 2.0
    weight[64, 1] = 2.0
    weight[64, 65] = 2.0
    flip = np.ones((8, 256), np.float32)
    flip[1, 1::2] = -1.0
    return tables, mask, weight, flip


def split(x):
    high = x.astype(BF16)
    return high, (x - high.astype(F32)).astype(BF16)


def split3(x):
    high = x.astype(BF16).astype(F32)
    rest = x - high
    mid = rest.astype(BF16).astype(F32)
    return high, mid, rest - mid


def mm(a, b):
    return jnp.dot(a, b, preferred_element_type=F32)


def mm_nt(a, b):
    return lax.dot_general(a, b, (((1,), (1,)), ((), ())), preferred_element_type=F32)


def right_mul(x, table):
    high, low = split(x)
    return mm(jnp.concatenate([high, low, high], axis=1), table[...])


def left_mul(table, x):
    high, low = split(x)
    return mm(table[...], jnp.concatenate([high, low, high], axis=0))


def left_pupil(table, x):
    high = x.astype(BF16).astype(F32)
    zero = jnp.zeros((8, x.shape[1]), F32)
    return mm(table[...], jnp.concatenate([high, x - high, high, zero], axis=0).astype(BF16))


def lanes_mul(x, table):
    both = mm(jnp.concatenate(split(x), axis=1), table[...])
    return both[:, :128] + both[:, 128:]


def row0(v, first):
    here = lax.broadcasted_iota(jnp.int32, (8, v.shape[1]), 0) == 0
    return jnp.concatenate([jnp.where(here, first, v[:8]), v[8:]], axis=0)


def unfold(real, imag):
    cr, sr, ci, si = real[:64], real[64:], imag[:64], imag[64:]
    sr0, si0 = row0(sr, 0.0), row0(si, 0.0)
    return (
        jnp.concatenate([cr + si0, row0(cr - si0, sr[:8])], axis=0),
        jnp.concatenate([ci - sr0, row0(ci + sr0, si[:8])], axis=0),
    )


def fold(gr, gi):
    ga, gb, ha, hb = gr[:64], gr[64:], gi[:64], gi[64:]
    return (
        jnp.concatenate([row0(ga + gb, ga[:8]), row0(hb - ha, gb[:8])], axis=0),
        jnp.concatenate([row0(ha + hb, ha[:8]), row0(ga - gb, hb[:8])], axis=0),
    )


COS_POLY = (1.0, -4.93480214, 4.05870915, -1.33521195, 0.23493707, -0.02439593)


def horner(poly, z):
    total = poly[-1]
    for one in poly[-2::-1]:
        total = total * z + one
    return total


def unit_field(half_turns, mask):
    k = jnp.floor(half_turns + 0.5)
    r = half_turns - k
    signed = mask * (1.0 - 2.0 * k + 4.0 * jnp.floor(0.5 * k))
    return signed * horner(COS_POLY, r * r)


def lane_mask(width, first):
    lane = lax.broadcasted_iota(jnp.int32, (8, width), 1)
    return (lane % 64) == first


def rows64(arr, fix):
    return jnp.concatenate([arr[:64], fix(arr[64:72]), arr[72:]], axis=0)


def left_half():
    return lax.broadcasted_iota(jnp.int32, (8, 128), 1)[:1] < 64


def half_spectra(lefts, rights, t2):
    low, at0 = left_half(), lane_mask(128, 0)[:1]
    lone, real, imag = [], [], []
    for one, two in zip(lefts, rights):
        di = pltpu.roll(jnp.where(low, two, one), 64, 1)
        total = jnp.sum(di, axis=0, keepdims=True)
        lone.append(pltpu.roll(jnp.broadcast_to(total, (8, 128)), 1, 1))
        real.append(jnp.where(low, one, two))
        imag.append(jnp.where(at0, 0.0, di))
    tr, ti = unfold(left_mul(t2, jnp.concatenate(real, axis=1)), left_mul(t2, jnp.concatenate(imag, axis=1)))
    here = lane_mask(256, 1) & (lax.broadcasted_iota(jnp.int32, (8, 256), 0) == 0)
    lone = jnp.concatenate(lone, axis=1)
    return rows64(tr, lambda v: jnp.where(here, lone, v)), rows64(ti, lambda v: jnp.where(here, 0.0, v))


def adjoint_lanes(gr, gi, t2t):
    width = gr.shape[1]
    here = lane_mask(width, 1) & (lax.broadcasted_iota(jnp.int32, (8, width), 0) == 0)
    lone = jnp.where(here, gr[64:72], 0.0)
    xr, xi = fold(
        rows64(gr, lambda v: jnp.where(here, 0.0, v)), rows64(gi, lambda v: jnp.where(here, 0.0, v))
    )
    dr, di = left_mul(t2t, xr), left_mul(t2t, xi)
    low, at0 = left_half(), lane_mask(128, 0)[:1]
    lefts, rights = [], []
    for i in range(width // 128):
        cols = slice(128 * i, 128 * i + 128)
        back = pltpu.roll(lone[:, cols], 127, 1)[:1]
        turned = pltpu.roll(jnp.where(at0, back, di[:, cols]), 64, 1)
        lefts.append(jnp.where(low, dr[:, cols], turned))
        rights.append(jnp.where(low, turned, dr[:, cols]))
    return lefts, rights


def rows_of(x, n):
    return x[128 * n : 128 * n + 128]


def make_kernel():
    def prep_spectra(source, observed, t1, t2, spec):
        sides = []
        for half in range(2):
            both = [mm(observed[source, 2 * i + half], t1[half, 0:128, :]) for i in range(4)]
            sides.append([(one[:, :128] + one[:, 128:]) * (1.0 / NPIX) for one in both])
        for j in range(2):
            real, imag = half_spectra(sides[0][2 * j : 2 * j + 2], sides[1][2 * j : 2 * j + 2], t2)
            spec[2 * source + j, :128, :] = real
            spec[2 * source + j, 128:, :] = imag

    def prep_basis(i, basis, basis6, last=False):
        lane = lax.broadcasted_iota(jnp.int32, (MROWS, 128), 1)
        halves = []
        for j in range(2):
            if last:
                rows = pltpu.roll(basis[pl.ds(64 - 32 * j, MROWS, stride=XN), :], 96 - 64 * j, 1)
            else:
                one = pltpu.roll(basis[pl.ds(2 * i + j, MROWS, stride=XN), :], 96, 1)
                other = pltpu.roll(basis[pl.ds(2 * i + j + 32, MROWS, stride=XN), :], 32, 1)
                rows = jnp.where(lane < 64, one, other)
            high, mid, low = split3(rows)
            halves.append(
                jnp.concatenate([high, mid, high, low, mid, high, jnp.zeros((16, NPIX), F32)], axis=0)
            )
        basis6[i] = jnp.concatenate(halves, axis=1).astype(BF16)

    def coef_six(coef, onehot):
        high, mid, low = split3(coef[...] * (1.0 / math.pi))
        stack = jnp.concatenate([high, high, mid, high, mid, low, jnp.zeros((16, NPIX), F32)], axis=0)
        return mm_nt(onehot[...].astype(BF16), stack.astype(BF16)).astype(BF16)

    def phases(six, basis6, phi):
        for i in range(TILES):
            both = mm(six[...], basis6[i])
            phi[pl.ds(2 * i * FR, FR), :] = both[:, :128]
            phi[pl.ds((2 * i + 1) * FR, FR), :] = both[:, 128:]

    def frame_field(f, phi, mask):
        lane = lax.broadcasted_iota(jnp.int32, (8, 128), 1)[:1]
        packed = phi[pl.ds(f, 40, stride=FR), :]
        turned = pltpu.roll(packed, 64, 1)
        phase = jnp.concatenate(
            [jnp.where(lane < 64, packed, turned), jnp.where(lane < 64, turned[:32], packed[:32])], axis=0
        )
        phase = jnp.concatenate([phase[:32], phase[40:], phase[32:40]], axis=0)
        return unit_field(phase - jnp.where(lane < 64, 0.0, 0.5), mask[...])

    def modes(dphi, basis6):
        total = None
        for i in range(TILES):
            a = dphi[pl.ds(2 * i * FR, FR), :]
            b = dphi[pl.ds((2 * i + 1) * FR, FR), :]
            high, low = split(jnp.concatenate([a, b], axis=1))
            part = mm_nt(basis6[i, 0 : 2 * MROWS, :], jnp.concatenate([high, low], axis=0))
            total = part if total is None else total + part
        return total

    def forward(h, phi, mask, flip, w1, a2, t1, t2, field, amp, trans):
        stack = []
        for i in range(PAIRS):
            for half in range(2):
                f = 2 * (PAIRS * h + i) + half
                one = frame_field(f, phi, mask)
                field[f] = one
                stack.append(one)
        b = right_mul(jnp.concatenate(stack, axis=0), w1)
        spreads = [[], []]
        for i in range(PAIRS):
            parts = []
            for half in range(2):
                one = b[XN * (2 * i + half) : XN * (2 * i + half + 1)]
                parts.append(jnp.concatenate([one[:64], one[64:] * flip[...]], axis=0))
            ar, ai = unfold(
                left_pupil(a2, jnp.concatenate([parts[0][:, :128], parts[1][:, :128]], axis=1)),
                left_pupil(a2, jnp.concatenate([parts[0][:, 128:], parts[1][:, 128:]], axis=1)),
            )
            amp[PAIRS * h + i, :128, :] = ar
            amp[PAIRS * h + i, 128:, :] = ai
            spread = ar * ar + ai * ai
            for half in range(2):
                spreads[half].append(spread[:, 128 * half : 128 * half + 128])
        d = [lanes_mul(jnp.concatenate(spreads[half], axis=0), t1.at[half]) for half in range(2)]
        for j in range(PAIRS // 2):
            g = PAIRS // 2 * h + j
            tr, ti = half_spectra(*[[rows_of(d[half], 2 * j), rows_of(d[half], 2 * j + 1)] for half in range(2)], t2)
            trans[g, :128, :] = tr
            trans[g, 128:, :] = ti

    def products(r, trans, spec, used, weight, cot):
        nr = ni = de = None
        upper, lower = pl.ds(pl.multiple_of(16 * r, 16), 16), pl.ds(pl.multiple_of(128 + 16 * r, 16), 16)
        for g in range(QUADS):
            u = used[g : g + 1, :]
            tr, ti, sr, si = trans[g, upper, :], trans[g, lower, :], spec[g, upper, :], spec[g, lower, :]
            vr, vi = tr * u, ti * u
            one = (sr * vr + si * vi, si * vr - sr * vi, tr * vr + ti * vi)
            nr, ni, de = one if g == 0 else (nr + one[0], ni + one[1], de + one[2])
        total = []
        for v in (nr, ni, de):
            v = v[:, :128] + v[:, 128:]
            total.append(v + pltpu.roll(v, 64, 1))
        scale = 1.0 / (GAMMA + total[2])
        qr, qi = total[0] * scale, total[1] * scale
        w = weight[upper, :]
        cot[0, upper, :] = w * qr
        cot[1, upper, :] = w * qi
        cot[2, upper, :] = w * (qr * qr + qi * qi)

    def backward(h, cot, spec, trans, used, flip, t2t, t1, a2t, w1t, amp, field, dphi):
        qr, qi, qq = [jnp.concatenate([cot[n], cot[n]], axis=1) for n in range(3)]
        sides = [[], []]
        for j in range(PAIRS // 2):
            g = PAIRS // 2 * h + j
            u = used[pl.ds(g, 1), :]
            tr, ti = trans[g, :128, :], trans[g, 128:, :]
            sr, si = spec[g, :128, :], spec[g, 128:, :]
            gr = u * (qq * tr - qr * sr - qi * si)
            gi = u * (qi * sr - qr * si + qq * ti)
            for half, one in enumerate(adjoint_lanes(gr, gi, t2t)):
                sides[half] += one
        ds = [lanes_mul(jnp.concatenate(sides[half], axis=0), t1.at[2 + half]) for half in range(2)]
        stack = []
        for i in range(PAIRS):
            one = jnp.concatenate([rows_of(ds[0], i), rows_of(ds[1], i)], axis=1)
            xr, xi = fold(amp[PAIRS * h + i, :128, :] * one, amp[PAIRS * h + i, 128:, :] * one)
            dbr, dbi = left_mul(a2t, xr), left_mul(a2t, xi)
            for half in range(2):
                cols = slice(128 * half, 128 * half + 128)
                one = jnp.concatenate([dbr[:XN, cols], dbi[:XN, cols]], axis=1)
                stack += [one[:64], one[64:] * flip[...]]
        x = jnp.concatenate(stack, axis=0)
        n = x.shape[0]
        both = mm(jnp.concatenate(split(x), axis=0), w1t[...])
        d = both[:n, :128] + both[:n, 128:] + both[n:, :128] + both[n:, 128:]
        lane = lax.broadcasted_iota(jnp.int32, (8, 128), 1)[:1]
        for i in range(PAIRS):
            for half in range(2):
                f, place = 2 * (PAIRS * h + i) + half, 2 * i + half
                v = field[f] * d[XN * place : XN * place + XN]
                v = v + pltpu.roll(v, 64, 1)
                dphi[pl.ds(f, 40, stride=FR), :] = jnp.concatenate(
                    [jnp.where(lane < 64, v[:32], v[32:64]), jnp.where(lane < 64, v[64:], 0.0)], axis=0
                )

    def kernel(
        observed_h, basis_h, pick, count, coef0, incoming, mask, weight, flip,
        t1_h, t2_h, a2_h, a2t_h, w1_h, w1t_h,
        out, coef_out,
        observed, basis, picks, picked, onehot, used, coef, own, t1, t2, a2, a2t, w1, w1t,
        spec, basis6, six, phi, dphi, field, amp, trans, cot, grads, objects, near, send, arrive,
        ob_send, ob_recv, pk_send, pk_recv, gr_send, gr_recv, ag_send, ag_recv, nb_send, nb_recv, basis_sem, load_sem,
    ):
        t, s = lax.axis_index("tile"), lax.axis_index("spare")
        tx, tz, tc = t // 8, (t // 2) % 4, t % 2
        spare_of = [(s + d) % 4 for d in (1, 2, 3)]
        groups = [
            [(t, v) for v in spare_of] + [(t + 1 - 2 * tc, (s + d) % 4) for d in range(4)],
            [(((tx + d) % 4) * 8 + tz * 2 + tc, s) for d in (1, 2, 3)],
            [(tx * 8 + ((tz + d) % 4) * 2 + tc, s) for d in (1, 2, 3)],
        ]
        places = [tc * 4 + s, tx, tz]
        beside = [((t + 1) % 32, s), ((t + 31) % 32, s)]

        barrier = pltpu.get_barrier_semaphore()
        partners = [who for group in groups for who in group] + beside
        for who in partners:
            pl.semaphore_signal(barrier, inc=1, device_id=who, device_id_type=MESH)

        loads = [
            pltpu.make_async_copy(src, dst, load_sem.at[n])
            for n, (src, dst) in enumerate(
                [(observed_h.at[s], observed.at[s]), (t1_h, t1), (t2_h, t2), (a2_h, a2), (a2t_h, a2t), (w1_h, w1), (w1t_h, w1t)]
            )
        ]
        windows = [
            pltpu.make_async_copy(
                basis_h.at[m, pl.ds(X0, XN), :], basis.at[pl.ds(m * XN, XN), :], basis_sem.at[m]
            )
            for m in range(36)
        ]
        for one in windows + loads:
            one.start()

        def remote(src, dst, ssem, rsem, who):
            return pltpu.make_async_remote_copy(
                src_ref=src, dst_ref=dst, send_sem=ssem, recv_sem=rsem, device_id=who, device_id_type=MESH
            )

        def near_copy(d):
            return remote(own, near.at[d], nb_send.at[0, d], nb_recv.at[0, d], beside[d])

        def object_copy(d):
            return remote(send.at[d], arrive.at[d], nb_send.at[1, d], nb_recv.at[1, d], beside[d])

        def frames_copy(d):
            return remote(observed_h.at[spare_of[d]], observed.at[s], ob_send.at[d], ob_recv.at[d], groups[0][d])

        def picks_copy(d):
            return remote(picks.at[spare_of[d]], picked.at[s], pk_send.at[d], pk_recv.at[d], groups[0][d])

        def gather_copy(d):
            return remote(objects.at[s], objects.at[s], ag_send.at[d], ag_recv.at[d], groups[0][d])

        def grad_copy(it, stage, d):
            here = grads.at[it, stage, places[stage]]
            return remote(here, here, gr_send.at[it, stage, d], gr_recv.at[it, stage, d], groups[stage][d])

        lane = lax.broadcasted_iota(jnp.int32, (8, 128), 1)
        row = lax.broadcasted_iota(jnp.int32, (8, 128), 0)
        wanted = jnp.full((8, 128), -1, jnp.int32)
        for j in range(4):
            wanted = jnp.where(lane == j, incoming[j], wanted)
        own[...] = wanted
        for p in range(4):
            spread = jnp.full((8, 128), pick[p, 0], jnp.int32)
            for k in range(1, 8):
                spread = jnp.where(row == k, pick[p, k], spread)
            picks[p] = spread
        picked[s] = picks[s]
        pl.semaphore_wait(barrier, len(partners))
        for d in range(3):
            picks_copy(d).start()
        for d in (1, 0, 2):
            frames_copy(d).start()
        for d in range(2):
            near_copy(d).start()

        lane2 = lax.broadcasted_iota(jnp.int32, (8, 256), 1)
        row2 = lax.broadcasted_iota(jnp.int32, (8, 256), 0)
        used[...] = jnp.where(4 * (4 * (row2 % 2) + lane2 // 64) + row2 // 2 < count[s], 1.0, 0.0)
        coef[...] = jnp.zeros_like(coef)
        coef[0:36, :] = coef0[...]
        basis[pl.ds(36 * XN, 4 * XN), :] = jnp.zeros((4 * XN, NPIX), F32)
        phi[pl.ds(2 * TILES * FR, 6 * FR), :] = jnp.zeros((6 * FR, 128), F32)
        for one in windows:
            one.wait()
        pl.loop(0, TILES - 1)(lambda i: prep_basis(i, basis, basis6))
        prep_basis(TILES - 1, basis, basis6, last=True)
        for d in range(3):
            picks_copy(d).wait()
        for a in range(4):
            onehot[8 * a : 8 * a + 8, :] = jnp.where(picked[a] == lane, 1.0, 0.0)
        for one in loads:
            one.wait()

        @pl.loop(0, ITERS + 1)
        def iteration(it):
            six[...] = coef_six(coef, onehot)
            phases(six, basis6, phi)

            pl.loop(0, STEPS)(lambda h: forward(h, phi, mask, flip, w1, a2, t1, t2.at[0], field, amp, trans))

            @pl.when(it == 0)
            def _():
                prep_spectra(s, observed, t1, t2.at[2], spec)
                for d in (0, 2, 1):
                    frames_copy(d).wait()
                    prep_spectra((s + 3 - d) % 4, observed, t1, t2.at[2], spec)

            pl.loop(0, 8)(lambda r: products(r, trans, spec, used, weight, cot))

            @pl.when(it < ITERS)
            def _():
                pl.loop(0, STEPS)(
                    lambda h: backward(h, cot, spec, trans, used, flip, t2.at[1], t1, a2t, w1t, amp, field, dphi)
                )
                acc = modes(dphi, basis6)
                slot_grad = acc[:MROWS] + acc[MROWS:]
                twice = jnp.concatenate([onehot[...], onehot[...]], axis=0).astype(BF16)
                total = None
                for part in split3(slot_grad):
                    one = mm(part.astype(BF16), twice)
                    total = one if total is None else total + one
                for stage in range(3):
                    grads[it, stage, places[stage]] = total
                    count = len(groups[stage])
                    for d in range(count):
                        grad_copy(it, stage, d).start()
                    for d in range(count):
                        grad_copy(it, stage, d).wait()
                    total = grads[it, stage, 0]
                    for d in range(count):
                        total = total + grads[it, stage, d + 1]
                mean = jnp.sum(total * total) * (1.0 / (128.0 * 36.0))
                coef[...] = coef[...] - STEP * total / jnp.sqrt(jnp.full(total.shape, mean + EPS, F32))

        lefts, _ = adjoint_lanes(cot[0] * (0.25 / NPIX), cot[1] * (0.25 / NPIX), t2.at[3])
        objects[s] = lanes_mul(lefts[0], t1.at[2])
        for d in range(3):
            gather_copy(d).start()
        for d in range(3):
            gather_copy(d).wait()

        for d in range(2):
            near_copy(d).wait()
        for d in range(2):
            wanted = near[1 - d]
            total = None
            for p in range(4):
                match = jnp.where(wanted == 4 * t + p, 1.0, 0.0)
                one = jnp.max(match[:1, :], axis=1, keepdims=True) * objects[p]
                total = one if total is None else total + one
            send[d] = total
            object_copy(d).start()
        for d in range(2):
            object_copy(d).wait()
        for j in range(4):
            source = incoming[j]
            total = jnp.where(source // 4 == (t + 31) % 32, arrive[0], arrive[1])
            for p in range(4):
                total = jnp.where(source == 4 * t + p, objects[p], total)
            out[j] = total
        coef_out[...] = coef[0:36, :]

    return kernel


def per_device(observed, frame_pick, frame_count, incoming, start_coefficients, mode_basis):
    tables, mask, weight, flip = host_tables()
    vmem = pl.BlockSpec(memory_space=pltpu.VMEM)
    smem = pl.BlockSpec(memory_space=pltpu.SMEM)
    hbm = pl.BlockSpec(memory_space=pl.ANY)
    dma = pltpu.SemaphoreType.DMA
    objects, coef = pl.pallas_call(
        make_kernel(),
        out_shape=(
            jax.ShapeDtypeStruct((4, NPIX, NPIX), F32),
            jax.ShapeDtypeStruct((36, 128), F32),
        ),
        in_specs=[hbm, hbm, smem, smem, vmem, smem, vmem, vmem, vmem] + [hbm] * 6,
        out_specs=(vmem, vmem),
        scratch_shapes=[
            pltpu.VMEM((4, 8, NPIX, NPIX), BF16),
            pltpu.VMEM((MROWS * XN, NPIX), F32),
            pltpu.VMEM((4, 8, 128), jnp.int32),
            pltpu.VMEM((4, 8, 128), jnp.int32),
            pltpu.VMEM((FR, 128), F32),
            pltpu.VMEM((8, 256), F32),
            pltpu.VMEM((MROWS, 128), F32),
            pltpu.VMEM((8, 128), jnp.int32),
            pltpu.VMEM((4, 256, 256), BF16),
            pltpu.VMEM((4, 128, 384), BF16),
            pltpu.VMEM((128, 224), BF16),
            pltpu.VMEM((80, 384), BF16),
            pltpu.VMEM((384, 256), BF16),
            pltpu.VMEM((256, 256), BF16),
            pltpu.VMEM((QUADS, 256, 256), F32),
            pltpu.VMEM((TILES, 256, 256), BF16),
            pltpu.VMEM((FR, 256), BF16),
            pltpu.VMEM((40 * FR, 128), F32),
            pltpu.VMEM((40 * FR, 128), F32),
            pltpu.VMEM((FR, XN, 128), F32),
            pltpu.VMEM((2 * QUADS, 256, 256), F32),
            pltpu.VMEM((QUADS, 256, 256), F32),
            pltpu.VMEM((3, 128, 128), F32),
            pltpu.VMEM((ITERS, 3, 8, MROWS, 128), F32),
            pltpu.VMEM((4, 128, 128), F32),
            pltpu.VMEM((2, 8, 128), jnp.int32),
            pltpu.VMEM((2, 128, 128), F32),
            pltpu.VMEM((2, 128, 128), F32),
            dma((3,)),
            dma((3,)),
            dma((3,)),
            dma((3,)),
            dma((ITERS, 3, 7)),
            dma((ITERS, 3, 7)),
            dma((3,)),
            dma((3,)),
            dma((2, 2)),
            dma((2, 2)),
            dma((36,)),
            dma((7,)),
        ],
        compiler_params=pltpu.CompilerParams(
            collective_id=0, has_side_effects=True, vmem_limit_bytes=56 * 1024 * 1024
        ),
        cost_estimate=pl.CostEstimate(flops=30_000_000_000, bytes_accessed=10_000_000, transcendentals=0),
    )(
        observed, mode_basis, frame_pick, frame_count, start_coefficients.T, incoming,
        *[jnp.asarray(one) for one in [mask, weight, flip] + tables],
    )
    return objects, coef.T


def solution(mesh):
    placed = (P("tile", "spare", None, None), P("tile", "spare"), P("tile"), P("tile"), P(), P())
    return jax.shard_map(
        per_device,
        mesh=mesh,
        in_specs=placed,
        out_specs=(P("tile", None, None), P()),
        check_vma=False,
    )
```

```python
import math

import jax
import jax.numpy as jnp
import ml_dtypes
import numpy as np
from jax import lax
from jax.experimental import pallas as pl
from jax.experimental.pallas import tpu as pltpu
from jax.sharding import PartitionSpec as P

MESH = pl.DeviceIdType.MESH
F32 = jnp.float32
BF16 = jnp.bfloat16
NPIX = 128
ITERS = 2
GAMMA = 0.5
STEP = 0.25
EPS = 1e-06
X0, XN = 32, 72
MROWS = 40
FR = 32
QUADS = 8
PAIRS = 8
STEPS = 16 // PAIRS
TILES = 17


def host_tables():
    index = np.arange(NPIX)
    angle = 2.0 * np.pi * (index[:, None] * index[None, :] % NPIX) / NPIX
    c, s = np.cos(angle), np.sin(angle)
    off = index - NPIX // 2
    disc = (off[:, None] ** 2 + off[None, :] ** 2 <= (NPIX // 4) ** 2).astype(np.float32)
    area = float(disc.sum())

    def two(table):
        high = table.astype(ml_dtypes.bfloat16)
        return high, (table - high.astype(np.float64)).astype(ml_dtypes.bfloat16)

    def wide(table, extra=0):
        high, low = two(table)
        return np.concatenate([high, high, low, np.zeros((len(table), extra), high.dtype)], axis=1)

    def tall(table):
        high, low = two(table)
        return np.concatenate([high, high, low], axis=0)

    def beside(table):
        return np.concatenate(two(table), axis=1)

    w1 = np.block([[c[32:96], -s[32:96]], [s[32:96], c[32:96]]]) / (NPIX * math.sqrt(area))
    w1t = np.concatenate([w1[64:].T, -w1[:64].T], axis=1)
    rows = np.concatenate([c[:64], c[64:65], s[1:64]], axis=0)
    order = np.concatenate([np.arange(65), 128 - np.arange(1, 64)])
    pupil = X0 + np.arange(XN)
    pupil[65] = NPIX // 2
    a2 = rows[:, pupil]
    a2t = np.concatenate([a2.T, np.zeros((8, NPIX))], axis=0)
    t2 = rows[:, order]
    cosine, sine = c[:, :64], -s[:, :64].copy()
    sine[:, 0] = c[:, 64]
    left, right = np.concatenate([cosine, sine], axis=1), np.concatenate([sine, cosine], axis=1)

    def twice(table):
        one = beside(table)
        return np.concatenate([one, one], axis=0)

    tables = [
        np.stack([twice(left), twice(right), twice(2.0 * left.T), twice(2.0 * right.T)]),
        np.stack([wide(t2), wide(t2.T), wide(rows), wide(rows.T)]),
        wide(a2, 8),
        wide(a2t),
        tall(w1),
        beside(w1t),
    ]
    mask = np.zeros((XN, 64), np.float32)
    mask[:65] = disc[X0 : X0 + 65, 32:96]
    mask[65, 0] = disc[64, 96]
    mask = np.concatenate([mask, mask], axis=1)
    weight = np.full((NPIX, NPIX), 4.0, np.float32)
    weight[:, 0] = 2.0
    weight[:, 64] = 2.0
    weight[64, 1] = 2.0
    weight[64, 65] = 2.0
    flip = np.ones((8, 256), np.float32)
    flip[1, 1::2] = -1.0
    return tables, mask, weight, flip


def split(x):
    high = x.astype(BF16)
    return high, (x - high.astype(F32)).astype(BF16)


def split3(x):
    high = x.astype(BF16).astype(F32)
    rest = x - high
    mid = rest.astype(BF16).astype(F32)
    return high, mid, rest - mid


def mm(a, b):
    return jnp.dot(a, b, preferred_element_type=F32)


def mm_nt(a, b):
    return lax.dot_general(a, b, (((1,), (1,)), ((), ())), preferred_element_type=F32)


def right_mul(x, table):
    high, low = split(x)
    return mm(jnp.concatenate([high, low, high], axis=1), table[...])


def left_mul(table, x):
    high, low = split(x)
    return mm(table[...], jnp.concatenate([high, low, high], axis=0))


def left_pupil(table, x):
    high = x.astype(BF16).astype(F32)
    zero = jnp.zeros((8, x.shape[1]), F32)
    return mm(table[...], jnp.concatenate([high, x - high, high, zero], axis=0).astype(BF16))


def lanes_mul(x, table):
    both = mm(jnp.concatenate(split(x), axis=1), table[...])
    return both[:, :128] + both[:, 128:]


def row0(v, first):
    here = lax.broadcasted_iota(jnp.int32, (8, v.shape[1]), 0) == 0
    return jnp.concatenate([jnp.where(here, first, v[:8]), v[8:]], axis=0)


def unfold(real, imag):
    cr, sr, ci, si = real[:64], real[64:], imag[:64], imag[64:]
    sr0, si0 = row0(sr, 0.0), row0(si, 0.0)
    return (
        jnp.concatenate([cr + si0, row0(cr - si0, sr[:8])], axis=0),
        jnp.concatenate([ci - sr0, row0(ci + sr0, si[:8])], axis=0),
    )


def fold(gr, gi):
    ga, gb, ha, hb = gr[:64], gr[64:], gi[:64], gi[64:]
    return (
        jnp.concatenate([row0(ga + gb, ga[:8]), row0(hb - ha, gb[:8])], axis=0),
        jnp.concatenate([row0(ha + hb, ha[:8]), row0(ga - gb, hb[:8])], axis=0),
    )


COS_POLY = (1.0, -4.93480214, 4.05870915, -1.33521195, 0.23493707, -0.02439593)


def horner(poly, z):
    total = poly[-1]
    for one in poly[-2::-1]:
        total = total * z + one
    return total


def unit_field(half_turns, mask):
    k = jnp.floor(half_turns + 0.5)
    r = half_turns - k
    signed = mask * (1.0 - 2.0 * k + 4.0 * jnp.floor(0.5 * k))
    return signed * horner(COS_POLY, r * r)


def lane_mask(width, first):
    lane = lax.broadcasted_iota(jnp.int32, (8, width), 1)
    return (lane % 64) == first


def rows64(arr, fix):
    return jnp.concatenate([arr[:64], fix(arr[64:72]), arr[72:]], axis=0)


def left_half():
    return lax.broadcasted_iota(jnp.int32, (8, 128), 1)[:1] < 64


def half_spectra(lefts, rights, t2):
    low, at0 = left_half(), lane_mask(128, 0)[:1]
    lone, real, imag = [], [], []
    for one, two in zip(lefts, rights):
        di = pltpu.roll(jnp.where(low, two, one), 64, 1)
        total = jnp.sum(di, axis=0, keepdims=True)
        lone.append(pltpu.roll(jnp.broadcast_to(total, (8, 128)), 1, 1))
        real.append(jnp.where(low, one, two))
        imag.append(jnp.where(at0, 0.0, di))
    tr, ti = unfold(left_mul(t2, jnp.concatenate(real, axis=1)), left_mul(t2, jnp.concatenate(imag, axis=1)))
    here = lane_mask(256, 1) & (lax.broadcasted_iota(jnp.int32, (8, 256), 0) == 0)
    lone = jnp.concatenate(lone, axis=1)
    return rows64(tr, lambda v: jnp.where(here, lone, v)), rows64(ti, lambda v: jnp.where(here, 0.0, v))


def adjoint_lanes(gr, gi, t2t):
    width = gr.shape[1]
    here = lane_mask(width, 1) & (lax.broadcasted_iota(jnp.int32, (8, width), 0) == 0)
    lone = jnp.where(here, gr[64:72], 0.0)
    xr, xi = fold(
        rows64(gr, lambda v: jnp.where(here, 0.0, v)), rows64(gi, lambda v: jnp.where(here, 0.0, v))
    )
    dr, di = left_mul(t2t, xr), left_mul(t2t, xi)
    low, at0 = left_half(), lane_mask(128, 0)[:1]
    lefts, rights = [], []
    for i in range(width // 128):
        cols = slice(128 * i, 128 * i + 128)
        back = pltpu.roll(lone[:, cols], 127, 1)[:1]
        turned = pltpu.roll(jnp.where(at0, back, di[:, cols]), 64, 1)
        lefts.append(jnp.where(low, dr[:, cols], turned))
        rights.append(jnp.where(low, turned, dr[:, cols]))
    return lefts, rights


def rows_of(x, n):
    return x[128 * n : 128 * n + 128]


def make_kernel():
    def prep_spectra(source, observed, t1, t2, spec):
        sides = []
        for half in range(2):
            both = [mm(observed[source, 2 * i + half], t1[half, 0:128, :]) for i in range(4)]
            sides.append([(one[:, :128] + one[:, 128:]) * (1.0 / NPIX) for one in both])
        for j in range(2):
            real, imag = half_spectra(sides[0][2 * j : 2 * j + 2], sides[1][2 * j : 2 * j + 2], t2)
            spec[2 * source + j, :128, :] = real
            spec[2 * source + j, 128:, :] = imag

    def prep_basis(i, basis, basis6, last=False):
        lane = lax.broadcasted_iota(jnp.int32, (MROWS, 128), 1)
        halves = []
        for j in range(2):
            if last:
                rows = pltpu.roll(basis[pl.ds(64 - 32 * j, MROWS, stride=XN), :], 96 - 64 * j, 1)
            else:
                one = pltpu.roll(basis[pl.ds(2 * i + j, MROWS, stride=XN), :], 96, 1)
                other = pltpu.roll(basis[pl.ds(2 * i + j + 32, MROWS, stride=XN), :], 32, 1)
                rows = jnp.where(lane < 64, one, other)
            high, mid, low = split3(rows)
            halves.append(
                jnp.concatenate([high, mid, high, low, mid, high, jnp.zeros((16, NPIX), F32)], axis=0)
            )
        basis6[i] = jnp.concatenate(halves, axis=1).astype(BF16)

    def coef_six(coef, onehot):
        high, mid, low = split3(coef[...] * (1.0 / math.pi))
        stack = jnp.concatenate([high, high, mid, high, mid, low, jnp.zeros((16, NPIX), F32)], axis=0)
        return mm_nt(onehot[...].astype(BF16), stack.astype(BF16)).astype(BF16)

    def phases(six, basis6, phi):
        for i in range(TILES):
            both = mm(six[...], basis6[i])
            phi[pl.ds(2 * i * FR, FR), :] = both[:, :128]
            phi[pl.ds((2 * i + 1) * FR, FR), :] = both[:, 128:]

    def frame_field(f, phi, mask):
        lane = lax.broadcasted_iota(jnp.int32, (8, 128), 1)[:1]
        packed = phi[pl.ds(f, 40, stride=FR), :]
        turned = pltpu.roll(packed, 64, 1)
        phase = jnp.concatenate(
            [jnp.where(lane < 64, packed, turned), jnp.where(lane < 64, turned[:32], packed[:32])], axis=0
        )
        phase = jnp.concatenate([phase[:32], phase[40:], phase[32:40]], axis=0)
        return unit_field(phase - jnp.where(lane < 64, 0.0, 0.5), mask[...])

    def modes(dphi, basis6):
        total = None
        for i in range(TILES):
            a = dphi[pl.ds(2 * i * FR, FR), :]
            b = dphi[pl.ds((2 * i + 1) * FR, FR), :]
            high, low = split(jnp.concatenate([a, b], axis=1))
            part = mm_nt(basis6[i, 0 : 2 * MROWS, :], jnp.concatenate([high, low], axis=0))
            total = part if total is None else total + part
        return total

    def forward(h, phi, mask, flip, w1, a2, t1, t2, field, amp, trans):
        stack = []
        for i in range(PAIRS):
            for half in range(2):
                f = 2 * (PAIRS * h + i) + half
                one = frame_field(f, phi, mask)
                field[f] = one
                stack.append(one)
        b = right_mul(jnp.concatenate(stack, axis=0), w1)
        spreads = [[], []]
        for i in range(PAIRS):
            parts = []
            for half in range(2):
                one = b[XN * (2 * i + half) : XN * (2 * i + half + 1)]
                parts.append(jnp.concatenate([one[:64], one[64:] * flip[...]], axis=0))
            ar, ai = unfold(
                left_pupil(a2, jnp.concatenate([parts[0][:, :128], parts[1][:, :128]], axis=1)),
                left_pupil(a2, jnp.concatenate([parts[0][:, 128:], parts[1][:, 128:]], axis=1)),
            )
            amp[PAIRS * h + i, :128, :] = ar
            amp[PAIRS * h + i, 128:, :] = ai
            spread = ar * ar + ai * ai
            for half in range(2):
                spreads[half].append(spread[:, 128 * half : 128 * half + 128])
        d = [lanes_mul(jnp.concatenate(spreads[half], axis=0), t1.at[half]) for half in range(2)]
        for j in range(PAIRS // 2):
            g = PAIRS // 2 * h + j
            tr, ti = half_spectra(*[[rows_of(d[half], 2 * j), rows_of(d[half], 2 * j + 1)] for half in range(2)], t2)
            trans[g, :128, :] = tr
            trans[g, 128:, :] = ti

    def products(r, trans, spec, used, weight, cot):
        nr = ni = de = None
        upper, lower = pl.ds(pl.multiple_of(16 * r, 16), 16), pl.ds(pl.multiple_of(128 + 16 * r, 16), 16)
        for g in range(QUADS):
            u = used[g : g + 1, :]
            tr, ti, sr, si = trans[g, upper, :], trans[g, lower, :], spec[g, upper, :], spec[g, lower, :]
            vr, vi = tr * u, ti * u
            one = (sr * vr + si * vi, si * vr - sr * vi, tr * vr + ti * vi)
            nr, ni, de = one if g == 0 else (nr + one[0], ni + one[1], de + one[2])
        total = []
        for v in (nr, ni, de):
            v = v[:, :128] + v[:, 128:]
            total.append(v + pltpu.roll(v, 64, 1))
        scale = 1.0 / (GAMMA + total[2])
        qr, qi = total[0] * scale, total[1] * scale
        w = weight[upper, :]
        cot[0, upper, :] = w * qr
        cot[1, upper, :] = w * qi
        cot[2, upper, :] = w * (qr * qr + qi * qi)

    def backward(h, cot, spec, trans, used, flip, t2t, t1, a2t, w1t, amp, field, dphi):
        qr, qi, qq = [jnp.concatenate([cot[n], cot[n]], axis=1) for n in range(3)]
        sides = [[], []]
        for j in range(PAIRS // 2):
            g = PAIRS // 2 * h + j
            u = used[pl.ds(g, 1), :]
            tr, ti = trans[g, :128, :], trans[g, 128:, :]
            sr, si = spec[g, :128, :], spec[g, 128:, :]
            gr = u * (qq * tr - qr * sr - qi * si)
            gi = u * (qi * sr - qr * si + qq * ti)
            for half, one in enumerate(adjoint_lanes(gr, gi, t2t)):
                sides[half] += one
        ds = [lanes_mul(jnp.concatenate(sides[half], axis=0), t1.at[2 + half]) for half in range(2)]
        stack = []
        for i in range(PAIRS):
            one = jnp.concatenate([rows_of(ds[0], i), rows_of(ds[1], i)], axis=1)
            xr, xi = fold(amp[PAIRS * h + i, :128, :] * one, amp[PAIRS * h + i, 128:, :] * one)
            dbr, dbi = left_mul(a2t, xr), left_mul(a2t, xi)
            for half in range(2):
                cols = slice(128 * half, 128 * half + 128)
                one = jnp.concatenate([dbr[:XN, cols], dbi[:XN, cols]], axis=1)
                stack += [one[:64], one[64:] * flip[...]]
        x = jnp.concatenate(stack, axis=0)
        n = x.shape[0]
        both = mm(jnp.concatenate(split(x), axis=0), w1t[...])
        d = both[:n, :128] + both[:n, 128:] + both[n:, :128] + both[n:, 128:]
        lane = lax.broadcasted_iota(jnp.int32, (8, 128), 1)[:1]
        for i in range(PAIRS):
            for half in range(2):
                f, place = 2 * (PAIRS * h + i) + half, 2 * i + half
                v = field[f] * d[XN * place : XN * place + XN]
                v = v + pltpu.roll(v, 64, 1)
                dphi[pl.ds(f, 40, stride=FR), :] = jnp.concatenate(
                    [jnp.where(lane < 64, v[:32], v[32:64]), jnp.where(lane < 64, v[64:], 0.0)], axis=0
                )

    def kernel(
        observed_h, basis_h, pick, count, coef0, incoming, mask, weight, flip,
        t1_h, t2_h, a2_h, a2t_h, w1_h, w1t_h,
        out, coef_out,
        observed, basis, picks, picked, onehot, used, coef, own, t1, t2, a2, a2t, w1, w1t,
        spec, basis6, six, phi, dphi, field, amp, trans, cot, grads, objects, near, send, arrive,
        ob_send, ob_recv, pk_send, pk_recv, gr_send, gr_recv, ag_send, ag_recv, nb_send, nb_recv, basis_sem, load_sem,
    ):
        t, s = lax.axis_index("tile"), lax.axis_index("spare")
        tx, tz, tc = t // 8, (t // 2) % 4, t % 2
        spare_of = [(s + d) % 4 for d in (1, 2, 3)]
        groups = [
            [(t, v) for v in spare_of] + [(t + 1 - 2 * tc, (s + d) % 4) for d in range(4)],
            [(((tx + d) % 4) * 8 + tz * 2 + tc, s) for d in (1, 2, 3)],
            [(tx * 8 + ((tz + d) % 4) * 2 + tc, s) for d in (1, 2, 3)],
        ]
        places = [tc * 4 + s, tx, tz]
        beside = [((t + 1) % 32, s), ((t + 31) % 32, s)]

        barrier = pltpu.get_barrier_semaphore()
        partners = [who for group in groups for who in group] + beside
        for who in partners:
            pl.semaphore_signal(barrier, inc=1, device_id=who, device_id_type=MESH)

        loads = [
            pltpu.make_async_copy(src, dst, load_sem.at[n])
            for n, (src, dst) in enumerate(
                [(observed_h.at[s], observed.at[s]), (t1_h, t1), (t2_h, t2), (a2_h, a2), (a2t_h, a2t), (w1_h, w1), (w1t_h, w1t)]
            )
        ]
        windows = [
            pltpu.make_async_copy(
                basis_h.at[m, pl.ds(X0, XN), :], basis.at[pl.ds(m * XN, XN), :], basis_sem.at[m]
            )
            for m in range(36)
        ]
        for one in windows + loads:
            one.start()

        def remote(src, dst, ssem, rsem, who):
            return pltpu.make_async_remote_copy(
                src_ref=src, dst_ref=dst, send_sem=ssem, recv_sem=rsem, device_id=who, device_id_type=MESH
            )

        def near_copy(d):
            return remote(own, near.at[d], nb_send.at[0, d], nb_recv.at[0, d], beside[d])

        def object_copy(d):
            return remote(send.at[d], arrive.at[d], nb_send.at[1, d], nb_recv.at[1, d], beside[d])

        def frames_copy(d):
            return remote(observed_h.at[spare_of[d]], observed.at[s], ob_send.at[d], ob_recv.at[d], groups[0][d])

        def picks_copy(d):
            return remote(picks.at[spare_of[d]], picked.at[s], pk_send.at[d], pk_recv.at[d], groups[0][d])

        def gather_copy(d):
            return remote(objects.at[s], objects.at[s], ag_send.at[d], ag_recv.at[d], groups[0][d])

        def grad_copy(it, stage, d):
            here = grads.at[it, stage, places[stage]]
            return remote(here, here, gr_send.at[it, stage, d], gr_recv.at[it, stage, d], groups[stage][d])

        lane = lax.broadcasted_iota(jnp.int32, (8, 128), 1)
        row = lax.broadcasted_iota(jnp.int32, (8, 128), 0)
        wanted = jnp.full((8, 128), -1, jnp.int32)
        for j in range(4):
            wanted = jnp.where(lane == j, incoming[j], wanted)
        own[...] = wanted
        for p in range(4):
            spread = jnp.full((8, 128), pick[p, 0], jnp.int32)
            for k in range(1, 8):
                spread = jnp.where(row == k, pick[p, k], spread)
            picks[p] = spread
        picked[s] = picks[s]
        pl.semaphore_wait(barrier, len(partners))
        for d in range(3):
            picks_copy(d).start()
        for d in (1, 0, 2):
            frames_copy(d).start()
        for d in range(2):
            near_copy(d).start()

        lane2 = lax.broadcasted_iota(jnp.int32, (8, 256), 1)
        row2 = lax.broadcasted_iota(jnp.int32, (8, 256), 0)
        used[...] = jnp.where(4 * (4 * (row2 % 2) + lane2 // 64) + row2 // 2 < count[s], 1.0, 0.0)
        coef[...] = jnp.zeros_like(coef)
        coef[0:36, :] = coef0[...]
        basis[pl.ds(36 * XN, 4 * XN), :] = jnp.zeros((4 * XN, NPIX), F32)
        phi[pl.ds(2 * TILES * FR, 6 * FR), :] = jnp.zeros((6 * FR, 128), F32)
        for one in windows:
            one.wait()
        pl.loop(0, TILES - 1)(lambda i: prep_basis(i, basis, basis6))
        prep_basis(TILES - 1, basis, basis6, last=True)
        for d in range(3):
            picks_copy(d).wait()
        for a in range(4):
            onehot[8 * a : 8 * a + 8, :] = jnp.where(picked[a] == lane, 1.0, 0.0)
        for one in loads:
            one.wait()

        @pl.loop(0, ITERS + 1)
        def iteration(it):
            six[...] = coef_six(coef, onehot)
            phases(six, basis6, phi)

            pl.loop(0, STEPS)(lambda h: forward(h, phi, mask, flip, w1, a2, t1, t2.at[0], field, amp, trans))

            @pl.when(it == 0)
            def _():
                prep_spectra(s, observed, t1, t2.at[2], spec)
                for d in (0, 2, 1):
                    frames_copy(d).wait()
                    prep_spectra((s + 3 - d) % 4, observed, t1, t2.at[2], spec)

            pl.loop(0, 8)(lambda r: products(r, trans, spec, used, weight, cot))

            @pl.when(it < ITERS)
            def _():
                pl.loop(0, STEPS)(
                    lambda h: backward(h, cot, spec, trans, used, flip, t2.at[1], t1, a2t, w1t, amp, field, dphi)
                )
                acc = modes(dphi, basis6)
                slot_grad = acc[:MROWS] + acc[MROWS:]
                twice = jnp.concatenate([onehot[...], onehot[...]], axis=0).astype(BF16)
                total = None
                for part in split3(slot_grad):
                    one = mm(part.astype(BF16), twice)
                    total = one if total is None else total + one
                for stage in range(3):
                    grads[it, stage, places[stage]] = total
                    count = len(groups[stage])
                    for d in range(count):
                        grad_copy(it, stage, d).start()
                    for d in range(count):
                        grad_copy(it, stage, d).wait()
                    total = grads[it, stage, 0]
                    for d in range(count):
                        total = total + grads[it, stage, d + 1]
                mean = jnp.sum(total * total) * (1.0 / (128.0 * 36.0))
                coef[...] = coef[...] - STEP * total / jnp.sqrt(jnp.full(total.shape, mean + EPS, F32))

        lefts, _ = adjoint_lanes(cot[0] * (0.25 / NPIX), cot[1] * (0.25 / NPIX), t2.at[3])
        objects[s] = lanes_mul(lefts[0], t1.at[2])
        for d in range(3):
            gather_copy(d).start()
        for d in range(3):
            gather_copy(d).wait()

        for d in range(2):
            near_copy(d).wait()
        for d in range(2):
            wanted = near[1 - d]
            total = None
            for p in range(4):
                match = jnp.where(wanted == 4 * t + p, 1.0, 0.0)
                one = jnp.max(match[:1, :], axis=1, keepdims=True) * objects[p]
                total = one if total is None else total + one
            send[d] = total
            object_copy(d).start()
        for d in range(2):
            object_copy(d).wait()
        for j in range(4):
            source = incoming[j]
            total = jnp.where(source // 4 == (t + 31) % 32, arrive[0], arrive[1])
            for p in range(4):
                total = jnp.where(source == 4 * t + p, objects[p], total)
            out[j] = total
        coef_out[...] = coef[0:36, :]

    return kernel


def per_device(observed, frame_pick, frame_count, incoming, start_coefficients, mode_basis):
    tables, mask, weight, flip = host_tables()
    vmem = pl.BlockSpec(memory_space=pltpu.VMEM)
    smem = pl.BlockSpec(memory_space=pltpu.SMEM)
    hbm = pl.BlockSpec(memory_space=pl.ANY)
    dma = pltpu.SemaphoreType.DMA
    objects, coef = pl.pallas_call(
        make_kernel(),
        out_shape=(
            jax.ShapeDtypeStruct((4, NPIX, NPIX), F32),
            jax.ShapeDtypeStruct((36, 128), F32),
        ),
        in_specs=[hbm, hbm, smem, smem, vmem, smem, vmem, vmem, vmem] + [hbm] * 6,
        out_specs=(vmem, vmem),
        scratch_shapes=[
            pltpu.VMEM((4, 8, NPIX, NPIX), BF16),
            pltpu.VMEM((MROWS * XN, NPIX), F32),
            pltpu.VMEM((4, 8, 128), jnp.int32),
            pltpu.VMEM((4, 8, 128), jnp.int32),
            pltpu.VMEM((FR, 128), F32),
            pltpu.VMEM((8, 256), F32),
            pltpu.VMEM((MROWS, 128), F32),
            pltpu.VMEM((8, 128), jnp.int32),
            pltpu.VMEM((4, 256, 256), BF16),
            pltpu.VMEM((4, 128, 384), BF16),
            pltpu.VMEM((128, 224), BF16),
            pltpu.VMEM((80, 384), BF16),
            pltpu.VMEM((384, 256), BF16),
            pltpu.VMEM((256, 256), BF16),
            pltpu.VMEM((QUADS, 256, 256), F32),
            pltpu.VMEM((TILES, 256, 256), BF16),
            pltpu.VMEM((FR, 256), BF16),
            pltpu.VMEM((40 * FR, 128), F32),
            pltpu.VMEM((40 * FR, 128), F32),
            pltpu.VMEM((FR, XN, 128), F32),
            pltpu.VMEM((2 * QUADS, 256, 256), F32),
            pltpu.VMEM((QUADS, 256, 256), F32),
            pltpu.VMEM((3, 128, 128), F32),
            pltpu.VMEM((ITERS, 3, 8, MROWS, 128), F32),
            pltpu.VMEM((4, 128, 128), F32),
            pltpu.VMEM((2, 8, 128), jnp.int32),
            pltpu.VMEM((2, 128, 128), F32),
            pltpu.VMEM((2, 128, 128), F32),
            dma((3,)),
            dma((3,)),
            dma((3,)),
            dma((3,)),
            dma((ITERS, 3, 7)),
            dma((ITERS, 3, 7)),
            dma((3,)),
            dma((3,)),
            dma((2, 2)),
            dma((2, 2)),
            dma((36,)),
            dma((7,)),
        ],
        compiler_params=pltpu.CompilerParams(
            collective_id=0, has_side_effects=True, vmem_limit_bytes=56 * 1024 * 1024
        ),
        cost_estimate=pl.CostEstimate(flops=30_000_000_000, bytes_accessed=10_000_000, transcendentals=0),
    )(
        observed, mode_basis, frame_pick, frame_count, start_coefficients.T, incoming,
        *[jnp.asarray(one) for one in [mask, weight, flip] + tables],
    )
    return objects, coef.T


def solution(mesh):
    placed = (P("tile", "spare", None, None), P("tile", "spare"), P("tile"), P("tile"), P(), P())
    return jax.shard_map(
        per_device,
        mesh=mesh,
        in_specs=placed,
        out_specs=(P("tile", None, None), P()),
        check_vma=False,
    )
```

```python
import math

import jax
import jax.numpy as jnp
import ml_dtypes
import numpy as np
from jax import lax
from jax.experimental import pallas as pl
from jax.experimental.pallas import tpu as pltpu
from jax.sharding import PartitionSpec as P

MESH = pl.DeviceIdType.MESH
F32 = jnp.float32
BF16 = jnp.bfloat16
NPIX = 128
ITERS = 2
GAMMA = 0.5
STEP = 0.25
EPS = 1e-06
X0, XN = 32, 72
MROWS = 40
FR = 32
QUADS = 8
PAIRS = 16
STEPS = 16 // PAIRS
TILES = 17


def host_tables():
    index = np.arange(NPIX)
    angle = 2.0 * np.pi * (index[:, None] * index[None, :] % NPIX) / NPIX
    c, s = np.cos(angle), np.sin(angle)
    off = index - NPIX // 2
    disc = (off[:, None] ** 2 + off[None, :] ** 2 <= (NPIX // 4) ** 2).astype(np.float32)
    area = float(disc.sum())

    def two(table):
        high = table.astype(ml_dtypes.bfloat16)
        return high, (table - high.astype(np.float64)).astype(ml_dtypes.bfloat16)

    def wide(table, extra=0):
        high, low = two(table)
        return np.concatenate([high, high, low, np.zeros((len(table), extra), high.dtype)], axis=1)

    def tall(table):
        high, low = two(table)
        return np.concatenate([high, high, low], axis=0)

    def beside(table):
        return np.concatenate(two(table), axis=1)

    w1 = np.block([[c[32:96], -s[32:96]], [s[32:96], c[32:96]]]) / (NPIX * math.sqrt(area))
    w1t = np.concatenate([w1[64:].T, -w1[:64].T], axis=1)
    rows = np.concatenate([c[:64], c[64:65], s[1:64]], axis=0)
    order = np.concatenate([np.arange(65), 128 - np.arange(1, 64)])
    pupil = X0 + np.arange(XN)
    pupil[65] = NPIX // 2
    a2 = rows[:, pupil]
    a2t = np.concatenate([a2.T, np.zeros((8, NPIX))], axis=0)
    t2 = rows[:, order]
    cosine, sine = c[:, :64], -s[:, :64].copy()
    sine[:, 0] = c[:, 64]
    left, right = np.concatenate([cosine, sine], axis=1), np.concatenate([sine, cosine], axis=1)

    def twice(table):
        one = beside(table)
        return np.concatenate([one, one], axis=0)

    tables = [
        np.stack([twice(left), twice(right), twice(2.0 * left.T), twice(2.0 * right.T)]),
        np.stack([wide(t2), wide(t2.T), wide(rows), wide(rows.T)]),
        wide(a2, 8),
        wide(a2t),
        tall(w1),
        beside(w1t),
    ]
    mask = np.zeros((XN, 64), np.float32)
    mask[:65] = disc[X0 : X0 + 65, 32:96]
    mask[65, 0] = disc[64, 96]
    mask = np.concatenate([mask, mask], axis=1)
    weight = np.full((NPIX, NPIX), 4.0, np.float32)
    weight[:, 0] = 2.0
    weight[:, 64] = 2.0
    weight[64, 1] = 2.0
    weight[64, 65] = 2.0
    flip = np.ones((8, 256), np.float32)
    flip[1, 1::2] = -1.0
    return tables, mask, weight, flip


def split(x):
    high = x.astype(BF16)
    return high, (x - high.astype(F32)).astype(BF16)


def split3(x):
    high = x.astype(BF16).astype(F32)
    rest = x - high
    mid = rest.astype(BF16).astype(F32)
    return high, mid, rest - mid


def mm(a, b):
    return jnp.dot(a, b, preferred_element_type=F32)


def mm_nt(a, b):
    return lax.dot_general(a, b, (((1,), (1,)), ((), ())), preferred_element_type=F32)


def right_mul(x, table):
    high, low = split(x)
    return mm(jnp.concatenate([high, low, high], axis=1), table[...])


def left_mul(table, x):
    high, low = split(x)
    return mm(table[...], jnp.concatenate([high, low, high], axis=0))


def left_pupil(table, x):
    high = x.astype(BF16).astype(F32)
    zero = jnp.zeros((8, x.shape[1]), F32)
    return mm(table[...], jnp.concatenate([high, x - high, high, zero], axis=0).astype(BF16))


def lanes_mul(x, table):
    both = mm(jnp.concatenate(split(x), axis=1), table[...])
    return both[:, :128] + both[:, 128:]


def row0(v, first):
    here = lax.broadcasted_iota(jnp.int32, (8, v.shape[1]), 0) == 0
    return jnp.concatenate([jnp.where(here, first, v[:8]), v[8:]], axis=0)


def unfold(real, imag):
    cr, sr, ci, si = real[:64], real[64:], imag[:64], imag[64:]
    sr0, si0 = row0(sr, 0.0), row0(si, 0.0)
    return (
        jnp.concatenate([cr + si0, row0(cr - si0, sr[:8])], axis=0),
        jnp.concatenate([ci - sr0, row0(ci + sr0, si[:8])], axis=0),
    )


def fold(gr, gi):
    ga, gb, ha, hb = gr[:64], gr[64:], gi[:64], gi[64:]
    return (
        jnp.concatenate([row0(ga + gb, ga[:8]), row0(hb - ha, gb[:8])], axis=0),
        jnp.concatenate([row0(ha + hb, ha[:8]), row0(ga - gb, hb[:8])], axis=0),
    )


COS_POLY = (1.0, -4.93480214, 4.05870915, -1.33521195, 0.23493707, -0.02439593)


def horner(poly, z):
    total = poly[-1]
    for one in poly[-2::-1]:
        total = total * z + one
    return total


def unit_field(half_turns, mask):
    k = jnp.floor(half_turns + 0.5)
    r = half_turns - k
    signed = mask * (1.0 - 2.0 * k + 4.0 * jnp.floor(0.5 * k))
    return signed * horner(COS_POLY, r * r)


def lane_mask(width, first):
    lane = lax.broadcasted_iota(jnp.int32, (8, width), 1)
    return (lane % 64) == first


def rows64(arr, fix):
    return jnp.concatenate([arr[:64], fix(arr[64:72]), arr[72:]], axis=0)


def left_half():
    return lax.broadcasted_iota(jnp.int32, (8, 128), 1)[:1] < 64


def half_spectra(lefts, rights, t2):
    low, at0 = left_half(), lane_mask(128, 0)[:1]
    lone, real, imag = [], [], []
    for one, two in zip(lefts, rights):
        di = pltpu.roll(jnp.where(low, two, one), 64, 1)
        total = jnp.sum(di, axis=0, keepdims=True)
        lone.append(pltpu.roll(jnp.broadcast_to(total, (8, 128)), 1, 1))
        real.append(jnp.where(low, one, two))
        imag.append(jnp.where(at0, 0.0, di))
    tr, ti = unfold(left_mul(t2, jnp.concatenate(real, axis=1)), left_mul(t2, jnp.concatenate(imag, axis=1)))
    here = lane_mask(256, 1) & (lax.broadcasted_iota(jnp.int32, (8, 256), 0) == 0)
    lone = jnp.concatenate(lone, axis=1)
    return rows64(tr, lambda v: jnp.where(here, lone, v)), rows64(ti, lambda v: jnp.where(here, 0.0, v))


def adjoint_lanes(gr, gi, t2t):
    width = gr.shape[1]
    here = lane_mask(width, 1) & (lax.broadcasted_iota(jnp.int32, (8, width), 0) == 0)
    lone = jnp.where(here, gr[64:72], 0.0)
    xr, xi = fold(
        rows64(gr, lambda v: jnp.where(here, 0.0, v)), rows64(gi, lambda v: jnp.where(here, 0.0, v))
    )
    dr, di = left_mul(t2t, xr), left_mul(t2t, xi)
    low, at0 = left_half(), lane_mask(128, 0)[:1]
    lefts, rights = [], []
    for i in range(width // 128):
        cols = slice(128 * i, 128 * i + 128)
        back = pltpu.roll(lone[:, cols], 127, 1)[:1]
        turned = pltpu.roll(jnp.where(at0, back, di[:, cols]), 64, 1)
        lefts.append(jnp.where(low, dr[:, cols], turned))
        rights.append(jnp.where(low, turned, dr[:, cols]))
    return lefts, rights


def rows_of(x, n):
    return x[128 * n : 128 * n + 128]


def make_kernel():
    def prep_spectra(source, observed, t1, t2, spec):
        sides = []
        for half in range(2):
            both = [mm(observed[source, 2 * i + half], t1[half, 0:128, :]) for i in range(4)]
            sides.append([(one[:, :128] + one[:, 128:]) * (1.0 / NPIX) for one in both])
        for j in range(2):
            real, imag = half_spectra(sides[0][2 * j : 2 * j + 2], sides[1][2 * j : 2 * j + 2], t2)
            spec[2 * source + j, :128, :] = real
            spec[2 * source + j, 128:, :] = imag

    def prep_basis(i, basis, basis6, last=False):
        lane = lax.broadcasted_iota(jnp.int32, (MROWS, 128), 1)
        halves = []
        for j in range(2):
            if last:
                rows = pltpu.roll(basis[pl.ds(64 - 32 * j, MROWS, stride=XN), :], 96 - 64 * j, 1)
            else:
                one = pltpu.roll(basis[pl.ds(2 * i + j, MROWS, stride=XN), :], 96, 1)
                other = pltpu.roll(basis[pl.ds(2 * i + j + 32, MROWS, stride=XN), :], 32, 1)
                rows = jnp.where(lane < 64, one, other)
            high, mid, low = split3(rows)
            halves.append(
                jnp.concatenate([high, mid, high, low, mid, high, jnp.zeros((16, NPIX), F32)], axis=0)
            )
        basis6[i] = jnp.concatenate(halves, axis=1).astype(BF16)

    def coef_six(coef, onehot):
        high, mid, low = split3(coef[...] * (1.0 / math.pi))
        stack = jnp.concatenate([high, high, mid, high, mid, low, jnp.zeros((16, NPIX), F32)], axis=0)
        return mm_nt(onehot[...].astype(BF16), stack.astype(BF16)).astype(BF16)

    def phases(six, basis6, phi):
        for i in range(TILES):
            both = mm(six[...], basis6[i])
            phi[pl.ds(2 * i * FR, FR), :] = both[:, :128]
            phi[pl.ds((2 * i + 1) * FR, FR), :] = both[:, 128:]

    def frame_field(f, phi, mask):
        lane = lax.broadcasted_iota(jnp.int32, (8, 128), 1)[:1]
        packed = phi[pl.ds(f, 40, stride=FR), :]
        turned = pltpu.roll(packed, 64, 1)
        phase = jnp.concatenate(
            [jnp.where(lane < 64, packed, turned), jnp.where(lane < 64, turned[:32], packed[:32])], axis=0
        )
        phase = jnp.concatenate([phase[:32], phase[40:], phase[32:40]], axis=0)
        return unit_field(phase - jnp.where(lane < 64, 0.0, 0.5), mask[...])

    def modes(dphi, basis6):
        total = None
        for i in range(TILES):
            a = dphi[pl.ds(2 * i * FR, FR), :]
            b = dphi[pl.ds((2 * i + 1) * FR, FR), :]
            high, low = split(jnp.concatenate([a, b], axis=1))
            part = mm_nt(basis6[i, 0 : 2 * MROWS, :], jnp.concatenate([high, low], axis=0))
            total = part if total is None else total + part
        return total

    def forward(h, phi, mask, flip, w1, a2, t1, t2, field, amp, trans):
        stack = []
        for i in range(PAIRS):
            for half in range(2):
                f = 2 * (PAIRS * h + i) + half
                one = frame_field(f, phi, mask)
                field[f] = one
                stack.append(one)
        b = right_mul(jnp.concatenate(stack, axis=0), w1)
        spreads = [[], []]
        for i in range(PAIRS):
            parts = []
            for half in range(2):
                one = b[XN * (2 * i + half) : XN * (2 * i + half + 1)]
                parts.append(jnp.concatenate([one[:64], one[64:] * flip[...]], axis=0))
            ar, ai = unfold(
                left_pupil(a2, jnp.concatenate([parts[0][:, :128], parts[1][:, :128]], axis=1)),
                left_pupil(a2, jnp.concatenate([parts[0][:, 128:], parts[1][:, 128:]], axis=1)),
            )
            amp[PAIRS * h + i, :128, :] = ar
            amp[PAIRS * h + i, 128:, :] = ai
            spread = ar * ar + ai * ai
            for half in range(2):
                spreads[half].append(spread[:, 128 * half : 128 * half + 128])
        d = [lanes_mul(jnp.concatenate(spreads[half], axis=0), t1.at[half]) for half in range(2)]
        for j in range(PAIRS // 2):
            g = PAIRS // 2 * h + j
            tr, ti = half_spectra(*[[rows_of(d[half], 2 * j), rows_of(d[half], 2 * j + 1)] for half in range(2)], t2)
            trans[g, :128, :] = tr
            trans[g, 128:, :] = ti

    def products(r, trans, spec, used, weight, cot):
        nr = ni = de = None
        upper, lower = pl.ds(pl.multiple_of(16 * r, 16), 16), pl.ds(pl.multiple_of(128 + 16 * r, 16), 16)
        for g in range(QUADS):
            u = used[g : g + 1, :]
            tr, ti, sr, si = trans[g, upper, :], trans[g, lower, :], spec[g, upper, :], spec[g, lower, :]
            vr, vi = tr * u, ti * u
            one = (sr * vr + si * vi, si * vr - sr * vi, tr * vr + ti * vi)
            nr, ni, de = one if g == 0 else (nr + one[0], ni + one[1], de + one[2])
        total = []
        for v in (nr, ni, de):
            v = v[:, :128] + v[:, 128:]
            total.append(v + pltpu.roll(v, 64, 1))
        scale = 1.0 / (GAMMA + total[2])
        qr, qi = total[0] * scale, total[1] * scale
        w = weight[upper, :]
        cot[0, upper, :] = w * qr
        cot[1, upper, :] = w * qi
        cot[2, upper, :] = w * (qr * qr + qi * qi)

    def backward(h, cot, spec, trans, used, flip, t2t, t1, a2t, w1t, amp, field, dphi):
        qr, qi, qq = [jnp.concatenate([cot[n], cot[n]], axis=1) for n in range(3)]
        sides = [[], []]
        for j in range(PAIRS // 2):
            g = PAIRS // 2 * h + j
            u = used[pl.ds(g, 1), :]
            tr, ti = trans[g, :128, :], trans[g, 128:, :]
            sr, si = spec[g, :128, :], spec[g, 128:, :]
            gr = u * (qq * tr - qr * sr - qi * si)
            gi = u * (qi * sr - qr * si + qq * ti)
            for half, one in enumerate(adjoint_lanes(gr, gi, t2t)):
                sides[half] += one
        ds = [lanes_mul(jnp.concatenate(sides[half], axis=0), t1.at[2 + half]) for half in range(2)]
        stack = []
        for i in range(PAIRS):
            one = jnp.concatenate([rows_of(ds[0], i), rows_of(ds[1], i)], axis=1)
            xr, xi = fold(amp[PAIRS * h + i, :128, :] * one, amp[PAIRS * h + i, 128:, :] * one)
            dbr, dbi = left_mul(a2t, xr), left_mul(a2t, xi)
            for half in range(2):
                cols = slice(128 * half, 128 * half + 128)
                one = jnp.concatenate([dbr[:XN, cols], dbi[:XN, cols]], axis=1)
                stack += [one[:64], one[64:] * flip[...]]
        x = jnp.concatenate(stack, axis=0)
        n = x.shape[0]
        both = mm(jnp.concatenate(split(x), axis=0), w1t[...])
        d = both[:n, :128] + both[:n, 128:] + both[n:, :128] + both[n:, 128:]
        lane = lax.broadcasted_iota(jnp.int32, (8, 128), 1)[:1]
        for i in range(PAIRS):
            for half in range(2):
                f, place = 2 * (PAIRS * h + i) + half, 2 * i + half
                v = field[f] * d[XN * place : XN * place + XN]
                v = v + pltpu.roll(v, 64, 1)
                dphi[pl.ds(f, 40, stride=FR), :] = jnp.concatenate(
                    [jnp.where(lane < 64, v[:32], v[32:64]), jnp.where(lane < 64, v[64:], 0.0)], axis=0
                )

    def kernel(
        observed_h, basis_h, pick, count, coef0, incoming, mask, weight, flip,
        t1_h, t2_h, a2_h, a2t_h, w1_h, w1t_h,
        out, coef_out,
        observed, basis, picks, picked, onehot, used, coef, own, t1, t2, a2, a2t, w1, w1t,
        spec, basis6, six, phi, dphi, field, amp, trans, cot, grads, objects, near, send, arrive,
        ob_send, ob_recv, pk_send, pk_recv, gr_send, gr_recv, ag_send, ag_recv, nb_send, nb_recv, basis_sem, load_sem,
    ):
        t, s = lax.axis_index("tile"), lax.axis_index("spare")
        tx, tz, tc = t // 8, (t // 2) % 4, t % 2
        spare_of = [(s + d) % 4 for d in (1, 2, 3)]
        groups = [
            [(t, v) for v in spare_of] + [(t + 1 - 2 * tc, (s + d) % 4) for d in range(4)],
            [(((tx + d) % 4) * 8 + tz * 2 + tc, s) for d in (1, 2, 3)],
            [(tx * 8 + ((tz + d) % 4) * 2 + tc, s) for d in (1, 2, 3)],
        ]
        places = [tc * 4 + s, tx, tz]
        beside = [((t + 1) % 32, s), ((t + 31) % 32, s)]

        barrier = pltpu.get_barrier_semaphore()
        partners = [who for group in groups for who in group] + beside
        for who in partners:
            pl.semaphore_signal(barrier, inc=1, device_id=who, device_id_type=MESH)

        loads = [
            pltpu.make_async_copy(src, dst, load_sem.at[n])
            for n, (src, dst) in enumerate(
                [(observed_h.at[s], observed.at[s]), (t1_h, t1), (t2_h, t2), (a2_h, a2), (a2t_h, a2t), (w1_h, w1), (w1t_h, w1t)]
            )
        ]
        windows = [
            pltpu.make_async_copy(
                basis_h.at[m, pl.ds(X0, XN), :], basis.at[pl.ds(m * XN, XN), :], basis_sem.at[m]
            )
            for m in range(36)
        ]
        for one in windows + loads:
            one.start()

        def remote(src, dst, ssem, rsem, who):
            return pltpu.make_async_remote_copy(
                src_ref=src, dst_ref=dst, send_sem=ssem, recv_sem=rsem, device_id=who, device_id_type=MESH
            )

        def near_copy(d):
            return remote(own, near.at[d], nb_send.at[0, d], nb_recv.at[0, d], beside[d])

        def object_copy(d):
            return remote(send.at[d], arrive.at[d], nb_send.at[1, d], nb_recv.at[1, d], beside[d])

        def frames_copy(d):
            return remote(observed_h.at[spare_of[d]], observed.at[s], ob_send.at[d], ob_recv.at[d], groups[0][d])

        def picks_copy(d):
            return remote(picks.at[spare_of[d]], picked.at[s], pk_send.at[d], pk_recv.at[d], groups[0][d])

        def gather_copy(d):
            return remote(objects.at[s], objects.at[s], ag_send.at[d], ag_recv.at[d], groups[0][d])

        def grad_copy(it, stage, d):
            here = grads.at[it, stage, places[stage]]
            return remote(here, here, gr_send.at[it, stage, d], gr_recv.at[it, stage, d], groups[stage][d])

        lane = lax.broadcasted_iota(jnp.int32, (8, 128), 1)
        row = lax.broadcasted_iota(jnp.int32, (8, 128), 0)
        wanted = jnp.full((8, 128), -1, jnp.int32)
        for j in range(4):
            wanted = jnp.where(lane == j, incoming[j], wanted)
        own[...] = wanted
        for p in range(4):
            spread = jnp.full((8, 128), pick[p, 0], jnp.int32)
            for k in range(1, 8):
                spread = jnp.where(row == k, pick[p, k], spread)
            picks[p] = spread
        picked[s] = picks[s]
        pl.semaphore_wait(barrier, len(partners))
        for d in range(3):
            picks_copy(d).start()
        for d in (1, 0, 2):
            frames_copy(d).start()
        for d in range(2):
            near_copy(d).start()

        lane2 = lax.broadcasted_iota(jnp.int32, (8, 256), 1)
        row2 = lax.broadcasted_iota(jnp.int32, (8, 256), 0)
        used[...] = jnp.where(4 * (4 * (row2 % 2) + lane2 // 64) + row2 // 2 < count[s], 1.0, 0.0)
        coef[...] = jnp.zeros_like(coef)
        coef[0:36, :] = coef0[...]
        basis[pl.ds(36 * XN, 4 * XN), :] = jnp.zeros((4 * XN, NPIX), F32)
        phi[pl.ds(2 * TILES * FR, 6 * FR), :] = jnp.zeros((6 * FR, 128), F32)
        for one in windows:
            one.wait()
        pl.loop(0, TILES - 1)(lambda i: prep_basis(i, basis, basis6))
        prep_basis(TILES - 1, basis, basis6, last=True)
        for d in range(3):
            picks_copy(d).wait()
        for a in range(4):
            onehot[8 * a : 8 * a + 8, :] = jnp.where(picked[a] == lane, 1.0, 0.0)
        for one in loads:
            one.wait()

        @pl.loop(0, ITERS + 1)
        def iteration(it):
            six[...] = coef_six(coef, onehot)
            phases(six, basis6, phi)

            forward(0, phi, mask, flip, w1, a2, t1, t2.at[0], field, amp, trans)

            @pl.when(it == 0)
            def _():
                prep_spectra(s, observed, t1, t2.at[2], spec)
                for d in (0, 2, 1):
                    frames_copy(d).wait()
                    prep_spectra((s + 3 - d) % 4, observed, t1, t2.at[2], spec)

            pl.loop(0, 8, unroll=2)(lambda r: products(r, trans, spec, used, weight, cot))

            @pl.when(it < ITERS)
            def _():
                backward(0, cot, spec, trans, used, flip, t2.at[1], t1, a2t, w1t, amp, field, dphi)
                acc = modes(dphi, basis6)
                slot_grad = acc[:MROWS] + acc[MROWS:]
                twice = jnp.concatenate([onehot[...], onehot[...]], axis=0).astype(BF16)
                total = None
                for part in split3(slot_grad):
                    one = mm(part.astype(BF16), twice)
                    total = one if total is None else total + one
                for stage in range(3):
                    grads[it, stage, places[stage]] = total
                    count = len(groups[stage])
                    for d in range(count):
                        grad_copy(it, stage, d).start()
                    for d in range(count):
                        grad_copy(it, stage, d).wait()
                    total = grads[it, stage, 0]
                    for d in range(count):
                        total = total + grads[it, stage, d + 1]
                mean = jnp.sum(total * total) * (1.0 / (128.0 * 36.0))
                coef[...] = coef[...] - STEP * total / jnp.sqrt(jnp.full(total.shape, mean + EPS, F32))

        lefts, _ = adjoint_lanes(cot[0] * (0.25 / NPIX), cot[1] * (0.25 / NPIX), t2.at[3])
        objects[s] = lanes_mul(lefts[0], t1.at[2])
        for d in range(3):
            gather_copy(d).start()
        for d in range(3):
            gather_copy(d).wait()

        for d in range(2):
            near_copy(d).wait()
        for d in range(2):
            wanted = near[1 - d]
            total = None
            for p in range(4):
                match = jnp.where(wanted == 4 * t + p, 1.0, 0.0)
                one = jnp.max(match[:1, :], axis=1, keepdims=True) * objects[p]
                total = one if total is None else total + one
            send[d] = total
            object_copy(d).start()
        for d in range(2):
            object_copy(d).wait()
        for j in range(4):
            source = incoming[j]
            total = jnp.where(source // 4 == (t + 31) % 32, arrive[0], arrive[1])
            for p in range(4):
                total = jnp.where(source == 4 * t + p, objects[p], total)
            out[j] = total
        coef_out[...] = coef[0:36, :]

    return kernel


def per_device(observed, frame_pick, frame_count, incoming, start_coefficients, mode_basis):
    tables, mask, weight, flip = host_tables()
    vmem = pl.BlockSpec(memory_space=pltpu.VMEM)
    smem = pl.BlockSpec(memory_space=pltpu.SMEM)
    hbm = pl.BlockSpec(memory_space=pl.ANY)
    dma = pltpu.SemaphoreType.DMA
    objects, coef = pl.pallas_call(
        make_kernel(),
        out_shape=(
            jax.ShapeDtypeStruct((4, NPIX, NPIX), F32),
            jax.ShapeDtypeStruct((36, 128), F32),
        ),
        in_specs=[hbm, hbm, smem, smem, vmem, smem, vmem, vmem, vmem] + [hbm] * 6,
        out_specs=(vmem, vmem),
        scratch_shapes=[
            pltpu.VMEM((4, 8, NPIX, NPIX), BF16),
            pltpu.VMEM((MROWS * XN, NPIX), F32),
            pltpu.VMEM((4, 8, 128), jnp.int32),
            pltpu.VMEM((4, 8, 128), jnp.int32),
            pltpu.VMEM((FR, 128), F32),
            pltpu.VMEM((8, 256), F32),
            pltpu.VMEM((MROWS, 128), F32),
            pltpu.VMEM((8, 128), jnp.int32),
            pltpu.VMEM((4, 256, 256), BF16),
            pltpu.VMEM((4, 128, 384), BF16),
            pltpu.VMEM((128, 224), BF16),
            pltpu.VMEM((80, 384), BF16),
            pltpu.VMEM((384, 256), BF16),
            pltpu.VMEM((256, 256), BF16),
            pltpu.VMEM((QUADS, 256, 256), F32),
            pltpu.VMEM((TILES, 256, 256), BF16),
            pltpu.VMEM((FR, 256), BF16),
            pltpu.VMEM((40 * FR, 128), F32),
            pltpu.VMEM((40 * FR, 128), F32),
            pltpu.VMEM((FR, XN, 128), F32),
            pltpu.VMEM((2 * QUADS, 256, 256), F32),
            pltpu.VMEM((QUADS, 256, 256), F32),
            pltpu.VMEM((3, 128, 128), F32),
            pltpu.VMEM((ITERS, 3, 8, MROWS, 128), F32),
            pltpu.VMEM((4, 128, 128), F32),
            pltpu.VMEM((2, 8, 128), jnp.int32),
            pltpu.VMEM((2, 128, 128), F32),
            pltpu.VMEM((2, 128, 128), F32),
            dma((3,)),
            dma((3,)),
            dma((3,)),
            dma((3,)),
            dma((ITERS, 3, 7)),
            dma((ITERS, 3, 7)),
            dma((3,)),
            dma((3,)),
            dma((2, 2)),
            dma((2, 2)),
            dma((36,)),
            dma((7,)),
        ],
        compiler_params=pltpu.CompilerParams(
            collective_id=0, has_side_effects=True, vmem_limit_bytes=56 * 1024 * 1024
        ),
        cost_estimate=pl.CostEstimate(flops=30_000_000_000, bytes_accessed=10_000_000, transcendentals=0),
    )(
        observed, mode_basis, frame_pick, frame_count, start_coefficients.T, incoming,
        *[jnp.asarray(one) for one in [mask, weight, flip] + tables],
    )
    return objects, coef.T


def solution(mesh):
    placed = (P("tile", "spare", None, None), P("tile", "spare"), P("tile"), P("tile"), P(), P())
    return jax.shard_map(
        per_device,
        mesh=mesh,
        in_specs=placed,
        out_specs=(P("tile", None, None), P()),
        check_vma=False,
    )
```

```python
import math

import jax
import jax.numpy as jnp
import ml_dtypes
import numpy as np
from jax import lax
from jax.experimental import pallas as pl
from jax.experimental.pallas import tpu as pltpu
from jax.sharding import PartitionSpec as P

MESH = pl.DeviceIdType.MESH
F32 = jnp.float32
BF16 = jnp.bfloat16
NPIX = 128
ITERS = 2
GAMMA = 0.5
STEP = 0.25
EPS = 1e-06
X0, XN = 32, 72
MROWS = 40
FR = 32
ODD = 33
BODD = 73
QUADS = 8
PAIRS = 16
STEPS = 16 // PAIRS
TILES = 17


def host_tables():
    index = np.arange(NPIX)
    angle = 2.0 * np.pi * (index[:, None] * index[None, :] % NPIX) / NPIX
    c, s = np.cos(angle), np.sin(angle)
    off = index - NPIX // 2
    disc = (off[:, None] ** 2 + off[None, :] ** 2 <= (NPIX // 4) ** 2).astype(np.float32)
    area = float(disc.sum())

    def two(table):
        high = table.astype(ml_dtypes.bfloat16)
        return high, (table - high.astype(np.float64)).astype(ml_dtypes.bfloat16)

    def wide(table, extra=0):
        high, low = two(table)
        return np.concatenate([high, high, low, np.zeros((len(table), extra), high.dtype)], axis=1)

    def tall(table):
        high, low = two(table)
        return np.concatenate([high, high, low], axis=0)

    def beside(table):
        return np.concatenate(two(table), axis=1)

    w1 = np.block([[c[32:96], -s[32:96]], [s[32:96], c[32:96]]]) / (NPIX * math.sqrt(area))
    w1t = np.concatenate([w1[64:].T, -w1[:64].T], axis=1)
    rows = np.concatenate([c[:64], c[64:65], s[1:64]], axis=0)
    order = np.concatenate([np.arange(65), 128 - np.arange(1, 64)])
    pupil = X0 + np.arange(XN)
    pupil[65] = NPIX // 2
    a2 = rows[:, pupil]
    a2t = np.concatenate([a2.T, np.zeros((8, NPIX))], axis=0)
    t2 = rows[:, order]
    cosine, sine = c[:, :64], -s[:, :64].copy()
    sine[:, 0] = c[:, 64]
    left, right = np.concatenate([cosine, sine], axis=1), np.concatenate([sine, cosine], axis=1)

    def twice(table):
        one = beside(table)
        return np.concatenate([one, one], axis=0)

    tables = [
        np.stack([twice(left), twice(right), twice(2.0 * left.T), twice(2.0 * right.T)]),
        np.stack([wide(t2), wide(t2.T), wide(rows), wide(rows.T)]),
        wide(a2, 8),
        wide(a2t),
        tall(w1),
        beside(w1t),
    ]
    mask = np.zeros((XN, 64), np.float32)
    mask[:65] = disc[X0 : X0 + 65, 32:96]
    mask[65, 0] = disc[64, 96]
    mask = np.concatenate([mask, mask], axis=1)
    weight = np.full((NPIX, NPIX), 4.0, np.float32)
    weight[:, 0] = 2.0
    weight[:, 64] = 2.0
    weight[64, 1] = 2.0
    weight[64, 65] = 2.0
    flip = np.ones((8, 256), np.float32)
    flip[1, 1::2] = -1.0
    return tables, mask, weight, flip


def split(x):
    high = x.astype(BF16)
    return high, (x - high.astype(F32)).astype(BF16)


def split3(x):
    high = x.astype(BF16).astype(F32)
    rest = x - high
    mid = rest.astype(BF16).astype(F32)
    return high, mid, rest - mid


def mm(a, b):
    return jnp.dot(a, b, preferred_element_type=F32)


def mm_nt(a, b):
    return lax.dot_general(a, b, (((1,), (1,)), ((), ())), preferred_element_type=F32)


def right_mul(x, table):
    high, low = split(x)
    return mm(jnp.concatenate([high, low, high], axis=1), table[...])


def left_mul(table, x):
    high, low = split(x)
    return mm(table[...], jnp.concatenate([high, low, high], axis=0))


def left_pupil(table, x):
    high = x.astype(BF16).astype(F32)
    zero = jnp.zeros((8, x.shape[1]), F32)
    return mm(table[...], jnp.concatenate([high, x - high, high, zero], axis=0).astype(BF16))


def lanes_mul(x, table):
    both = mm(jnp.concatenate(split(x), axis=1), table[...])
    return both[:, :128] + both[:, 128:]


def row0(v, first):
    here = lax.broadcasted_iota(jnp.int32, (8, v.shape[1]), 0) == 0
    return jnp.concatenate([jnp.where(here, first, v[:8]), v[8:]], axis=0)


def unfold(real, imag):
    cr, sr, ci, si = real[:64], real[64:], imag[:64], imag[64:]
    sr0, si0 = row0(sr, 0.0), row0(si, 0.0)
    return (
        jnp.concatenate([cr + si0, row0(cr - si0, sr[:8])], axis=0),
        jnp.concatenate([ci - sr0, row0(ci + sr0, si[:8])], axis=0),
    )


def fold(gr, gi):
    ga, gb, ha, hb = gr[:64], gr[64:], gi[:64], gi[64:]
    return (
        jnp.concatenate([row0(ga + gb, ga[:8]), row0(hb - ha, gb[:8])], axis=0),
        jnp.concatenate([row0(ha + hb, ha[:8]), row0(ga - gb, hb[:8])], axis=0),
    )


COS_POLY = (1.0, -4.93480214, 4.05870915, -1.33521195, 0.23493707, -0.02439593)


def horner(poly, z):
    total = poly[-1]
    for one in poly[-2::-1]:
        total = total * z + one
    return total


def unit_field(half_turns, mask):
    k = jnp.floor(half_turns + 0.5)
    r = half_turns - k
    signed = mask * (1.0 - 2.0 * k + 4.0 * jnp.floor(0.5 * k))
    return signed * horner(COS_POLY, r * r)


def lane_mask(width, first):
    lane = lax.broadcasted_iota(jnp.int32, (8, width), 1)
    return (lane % 64) == first


def rows64(arr, fix):
    return jnp.concatenate([arr[:64], fix(arr[64:72]), arr[72:]], axis=0)


def left_half():
    return lax.broadcasted_iota(jnp.int32, (8, 128), 1)[:1] < 64


def half_spectra(lefts, rights, t2):
    low, at0 = left_half(), lane_mask(128, 0)[:1]
    lone, real, imag = [], [], []
    for one, two in zip(lefts, rights):
        di = pltpu.roll(jnp.where(low, two, one), 64, 1)
        total = jnp.sum(di, axis=0, keepdims=True)
        lone.append(pltpu.roll(jnp.broadcast_to(total, (8, 128)), 1, 1))
        real.append(jnp.where(low, one, two))
        imag.append(jnp.where(at0, 0.0, di))
    tr, ti = unfold(left_mul(t2, jnp.concatenate(real, axis=1)), left_mul(t2, jnp.concatenate(imag, axis=1)))
    here = lane_mask(256, 1) & (lax.broadcasted_iota(jnp.int32, (8, 256), 0) == 0)
    lone = jnp.concatenate(lone, axis=1)
    return rows64(tr, lambda v: jnp.where(here, lone, v)), rows64(ti, lambda v: jnp.where(here, 0.0, v))


def adjoint_lanes(gr, gi, t2t):
    width = gr.shape[1]
    here = lane_mask(width, 1) & (lax.broadcasted_iota(jnp.int32, (8, width), 0) == 0)
    lone = jnp.where(here, gr[64:72], 0.0)
    xr, xi = fold(
        rows64(gr, lambda v: jnp.where(here, 0.0, v)), rows64(gi, lambda v: jnp.where(here, 0.0, v))
    )
    dr, di = left_mul(t2t, xr), left_mul(t2t, xi)
    low, at0 = left_half(), lane_mask(128, 0)[:1]
    lefts, rights = [], []
    for i in range(width // 128):
        cols = slice(128 * i, 128 * i + 128)
        back = pltpu.roll(lone[:, cols], 127, 1)[:1]
        turned = pltpu.roll(jnp.where(at0, back, di[:, cols]), 64, 1)
        lefts.append(jnp.where(low, dr[:, cols], turned))
        rights.append(jnp.where(low, turned, dr[:, cols]))
    return lefts, rights


def rows_of(x, n):
    return x[128 * n : 128 * n + 128]


def make_kernel():
    def prep_spectra(source, observed, t1, t2, spec):
        sides = []
        for half in range(2):
            both = [mm(observed[source, 2 * i + half], t1[half, 0:128, :]) for i in range(4)]
            sides.append([(one[:, :128] + one[:, 128:]) * (1.0 / NPIX) for one in both])
        for j in range(2):
            real, imag = half_spectra(sides[0][2 * j : 2 * j + 2], sides[1][2 * j : 2 * j + 2], t2)
            spec[2 * source + j, :128, :] = real
            spec[2 * source + j, 128:, :] = imag

    def prep_basis(i, basis, basis6, last=False):
        lane = lax.broadcasted_iota(jnp.int32, (MROWS, 128), 1)
        halves = []
        for j in range(2):
            if last:
                rows = pltpu.roll(basis[pl.ds(64 - 32 * j, MROWS, stride=BODD), :], 96 - 64 * j, 1)
            else:
                one = pltpu.roll(basis[pl.ds(2 * i + j, MROWS, stride=BODD), :], 96, 1)
                other = pltpu.roll(basis[pl.ds(2 * i + j + 32, MROWS, stride=BODD), :], 32, 1)
                rows = jnp.where(lane < 64, one, other)
            high, mid, low = split3(rows)
            halves.append(
                jnp.concatenate([high, mid, high, low, mid, high, jnp.zeros((16, NPIX), F32)], axis=0)
            )
        basis6[i] = jnp.concatenate(halves, axis=1).astype(BF16)

    def coef_six(coef, onehot):
        high, mid, low = split3(coef[...] * (1.0 / math.pi))
        stack = jnp.concatenate([high, high, mid, high, mid, low, jnp.zeros((16, NPIX), F32)], axis=0)
        return mm_nt(onehot[...].astype(BF16), stack.astype(BF16)).astype(BF16)

    def phases(six, basis6, phi):
        for i in range(TILES):
            both = mm(six[...], basis6[i])
            phi[pl.ds(2 * i * ODD, FR), :] = both[:, :128]
            phi[pl.ds((2 * i + 1) * ODD, FR), :] = both[:, 128:]

    def frame_field(f, phi, mask):
        lane = lax.broadcasted_iota(jnp.int32, (8, 128), 1)[:1]
        packed = phi[pl.ds(f, 40, stride=ODD), :]
        turned = pltpu.roll(packed, 64, 1)
        phase = jnp.concatenate(
            [jnp.where(lane < 64, packed, turned), jnp.where(lane < 64, turned[:32], packed[:32])], axis=0
        )
        phase = jnp.concatenate([phase[:32], phase[40:], phase[32:40]], axis=0)
        return unit_field(phase - jnp.where(lane < 64, 0.0, 0.5), mask[...])

    def modes(dphi, basis6):
        total = None
        for i in range(TILES):
            a = dphi[pl.ds(2 * i * ODD, FR), :]
            b = dphi[pl.ds((2 * i + 1) * ODD, FR), :]
            high, low = split(jnp.concatenate([a, b], axis=1))
            part = mm_nt(basis6[i, 0 : 2 * MROWS, :], jnp.concatenate([high, low], axis=0))
            total = part if total is None else total + part
        return total

    def forward(h, phi, mask, flip, w1, a2, t1, t2, field, amp, trans):
        stack = []
        for i in range(PAIRS):
            for half in range(2):
                f = 2 * (PAIRS * h + i) + half
                one = frame_field(f, phi, mask)
                field[f] = one
                stack.append(one)
        b = right_mul(jnp.concatenate(stack, axis=0), w1)
        spreads = [[], []]
        for i in range(PAIRS):
            parts = []
            for half in range(2):
                one = b[XN * (2 * i + half) : XN * (2 * i + half + 1)]
                parts.append(jnp.concatenate([one[:64], one[64:] * flip[...]], axis=0))
            ar, ai = unfold(
                left_pupil(a2, jnp.concatenate([parts[0][:, :128], parts[1][:, :128]], axis=1)),
                left_pupil(a2, jnp.concatenate([parts[0][:, 128:], parts[1][:, 128:]], axis=1)),
            )
            amp[PAIRS * h + i, :128, :] = ar
            amp[PAIRS * h + i, 128:, :] = ai
            spread = ar * ar + ai * ai
            for half in range(2):
                spreads[half].append(spread[:, 128 * half : 128 * half + 128])
        d = [lanes_mul(jnp.concatenate(spreads[half], axis=0), t1.at[half]) for half in range(2)]
        for j in range(PAIRS // 2):
            g = PAIRS // 2 * h + j
            tr, ti = half_spectra(*[[rows_of(d[half], 2 * j), rows_of(d[half], 2 * j + 1)] for half in range(2)], t2)
            trans[g, :128, :] = tr
            trans[g, 128:, :] = ti

    def products(r, trans, spec, used, weight, cot):
        nr = ni = de = None
        upper, lower = pl.ds(pl.multiple_of(16 * r, 16), 16), pl.ds(pl.multiple_of(128 + 16 * r, 16), 16)
        for g in range(QUADS):
            u = used[g : g + 1, :]
            tr, ti, sr, si = trans[g, upper, :], trans[g, lower, :], spec[g, upper, :], spec[g, lower, :]
            vr, vi = tr * u, ti * u
            one = (sr * vr + si * vi, si * vr - sr * vi, tr * vr + ti * vi)
            nr, ni, de = one if g == 0 else (nr + one[0], ni + one[1], de + one[2])
        total = []
        for v in (nr, ni, de):
            v = v[:, :128] + v[:, 128:]
            total.append(v + pltpu.roll(v, 64, 1))
        scale = 1.0 / (GAMMA + total[2])
        qr, qi = total[0] * scale, total[1] * scale
        w = weight[upper, :]
        cot[0, upper, :] = w * qr
        cot[1, upper, :] = w * qi
        cot[2, upper, :] = w * (qr * qr + qi * qi)

    def backward(h, cot, spec, trans, used, flip, t2t, t1, a2t, w1t, amp, field, dphi):
        qr, qi, qq = [jnp.concatenate([cot[n], cot[n]], axis=1) for n in range(3)]
        sides = [[], []]
        for j in range(PAIRS // 2):
            g = PAIRS // 2 * h + j
            u = used[pl.ds(g, 1), :]
            tr, ti = trans[g, :128, :], trans[g, 128:, :]
            sr, si = spec[g, :128, :], spec[g, 128:, :]
            gr = u * (qq * tr - qr * sr - qi * si)
            gi = u * (qi * sr - qr * si + qq * ti)
            for half, one in enumerate(adjoint_lanes(gr, gi, t2t)):
                sides[half] += one
        ds = [lanes_mul(jnp.concatenate(sides[half], axis=0), t1.at[2 + half]) for half in range(2)]
        stack = []
        for i in range(PAIRS):
            one = jnp.concatenate([rows_of(ds[0], i), rows_of(ds[1], i)], axis=1)
            xr, xi = fold(amp[PAIRS * h + i, :128, :] * one, amp[PAIRS * h + i, 128:, :] * one)
            dbr, dbi = left_mul(a2t, xr), left_mul(a2t, xi)
            for half in range(2):
                cols = slice(128 * half, 128 * half + 128)
                one = jnp.concatenate([dbr[:XN, cols], dbi[:XN, cols]], axis=1)
                stack += [one[:64], one[64:] * flip[...]]
        x = jnp.concatenate(stack, axis=0)
        n = x.shape[0]
        both = mm(jnp.concatenate(split(x), axis=0), w1t[...])
        d = both[:n, :128] + both[:n, 128:] + both[n:, :128] + both[n:, 128:]
        lane = lax.broadcasted_iota(jnp.int32, (8, 128), 1)[:1]
        for i in range(PAIRS):
            for half in range(2):
                f, place = 2 * (PAIRS * h + i) + half, 2 * i + half
                v = field[f] * d[XN * place : XN * place + XN]
                v = v + pltpu.roll(v, 64, 1)
                dphi[pl.ds(f, 40, stride=ODD), :] = jnp.concatenate(
                    [jnp.where(lane < 64, v[:32], v[32:64]), jnp.where(lane < 64, v[64:], 0.0)], axis=0
                )

    def kernel(
        observed_h, basis_h, pick, count, coef0, incoming, mask, weight, flip,
        t1_h, t2_h, a2_h, a2t_h, w1_h, w1t_h,
        out, coef_out,
        observed, window, basis, picks, picked, onehot, used, coef, own, t1, t2, a2, a2t, w1, w1t,
        spec, basis6, six, phi, dphi, field, amp, trans, cot, grads, objects, near, send, arrive,
        ob_send, ob_recv, pk_send, pk_recv, gr_send, gr_recv, ag_send, ag_recv, nb_send, nb_recv, basis_sem, load_sem,
    ):
        t, s = lax.axis_index("tile"), lax.axis_index("spare")
        tx, tz, tc = t // 8, (t // 2) % 4, t % 2
        spare_of = [(s + d) % 4 for d in (1, 2, 3)]
        groups = [
            [(t, v) for v in spare_of] + [(t + 1 - 2 * tc, (s + d) % 4) for d in range(4)],
            [(((tx + d) % 4) * 8 + tz * 2 + tc, s) for d in (1, 2, 3)],
            [(tx * 8 + ((tz + d) % 4) * 2 + tc, s) for d in (1, 2, 3)],
        ]
        places = [tc * 4 + s, tx, tz]
        beside = [((t + 1) % 32, s), ((t + 31) % 32, s)]

        barrier = pltpu.get_barrier_semaphore()
        partners = [who for group in groups for who in group] + beside
        for who in partners:
            pl.semaphore_signal(barrier, inc=1, device_id=who, device_id_type=MESH)

        loads = [
            pltpu.make_async_copy(src, dst, load_sem.at[n])
            for n, (src, dst) in enumerate(
                [(observed_h.at[s], observed.at[s]), (t1_h, t1), (t2_h, t2), (a2_h, a2), (a2t_h, a2t), (w1_h, w1), (w1t_h, w1t)]
            )
        ]
        windows = [
            pltpu.make_async_copy(
                basis_h.at[m, pl.ds(X0, XN), :], window.at[m], basis_sem.at[m]
            )
            for m in range(36)
        ]
        for one in windows + loads:
            one.start()

        def remote(src, dst, ssem, rsem, who):
            return pltpu.make_async_remote_copy(
                src_ref=src, dst_ref=dst, send_sem=ssem, recv_sem=rsem, device_id=who, device_id_type=MESH
            )

        def near_copy(d):
            return remote(own, near.at[d], nb_send.at[0, d], nb_recv.at[0, d], beside[d])

        def object_copy(d):
            return remote(send.at[d], arrive.at[d], nb_send.at[1, d], nb_recv.at[1, d], beside[d])

        def frames_copy(d):
            return remote(observed_h.at[spare_of[d]], observed.at[s], ob_send.at[d], ob_recv.at[d], groups[0][d])

        def picks_copy(d):
            return remote(picks.at[spare_of[d]], picked.at[s], pk_send.at[d], pk_recv.at[d], groups[0][d])

        def gather_copy(d):
            return remote(objects.at[s], objects.at[s], ag_send.at[d], ag_recv.at[d], groups[0][d])

        def grad_copy(it, stage, d):
            here = grads.at[it, stage, places[stage]]
            return remote(here, here, gr_send.at[it, stage, d], gr_recv.at[it, stage, d], groups[stage][d])

        lane = lax.broadcasted_iota(jnp.int32, (8, 128), 1)
        row = lax.broadcasted_iota(jnp.int32, (8, 128), 0)
        wanted = jnp.full((8, 128), -1, jnp.int32)
        for j in range(4):
            wanted = jnp.where(lane == j, incoming[j], wanted)
        own[...] = wanted
        for p in range(4):
            spread = jnp.full((8, 128), pick[p, 0], jnp.int32)
            for k in range(1, 8):
                spread = jnp.where(row == k, pick[p, k], spread)
            picks[p] = spread
        picked[s] = picks[s]
        pl.semaphore_wait(barrier, len(partners))
        for d in range(3):
            picks_copy(d).start()
        for d in (1, 0, 2):
            frames_copy(d).start()
        for d in range(2):
            near_copy(d).start()

        lane2 = lax.broadcasted_iota(jnp.int32, (8, 256), 1)
        row2 = lax.broadcasted_iota(jnp.int32, (8, 256), 0)
        used[...] = jnp.where(4 * (4 * (row2 % 2) + lane2 // 64) + row2 // 2 < count[s], 1.0, 0.0)
        coef[...] = jnp.zeros_like(coef)
        coef[0:36, :] = coef0[...]
        basis[pl.ds(36 * BODD, 4 * BODD), :] = jnp.zeros((4 * BODD, NPIX), F32)
        phi[...] = jnp.zeros_like(phi)
        for m in range(36):
            windows[m].wait()
            basis[pl.ds(m * BODD, XN), :] = window[m]
        pl.loop(0, TILES - 1)(lambda i: prep_basis(i, basis, basis6))
        prep_basis(TILES - 1, basis, basis6, last=True)
        for d in range(3):
            picks_copy(d).wait()
        for a in range(4):
            onehot[8 * a : 8 * a + 8, :] = jnp.where(picked[a] == lane, 1.0, 0.0)
        for one in loads:
            one.wait()

        @pl.loop(0, ITERS + 1)
        def iteration(it):
            six[...] = coef_six(coef, onehot)
            phases(six, basis6, phi)

            forward(0, phi, mask, flip, w1, a2, t1, t2.at[0], field, amp, trans)

            @pl.when(it == 0)
            def _():
                prep_spectra(s, observed, t1, t2.at[2], spec)
                for d in (0, 2, 1):
                    frames_copy(d).wait()
                    prep_spectra((s + 3 - d) % 4, observed, t1, t2.at[2], spec)

            pl.loop(0, 8, unroll=2)(lambda r: products(r, trans, spec, used, weight, cot))

            @pl.when(it < ITERS)
            def _():
                backward(0, cot, spec, trans, used, flip, t2.at[1], t1, a2t, w1t, amp, field, dphi)
                acc = modes(dphi, basis6)
                slot_grad = acc[:MROWS] + acc[MROWS:]
                twice = jnp.concatenate([onehot[...], onehot[...]], axis=0).astype(BF16)
                total = None
                for part in split3(slot_grad):
                    one = mm(part.astype(BF16), twice)
                    total = one if total is None else total + one
                for stage in range(3):
                    grads[it, stage, places[stage]] = total
                    count = len(groups[stage])
                    for d in range(count):
                        grad_copy(it, stage, d).start()
                    for d in range(count):
                        grad_copy(it, stage, d).wait()
                    total = grads[it, stage, 0]
                    for d in range(count):
                        total = total + grads[it, stage, d + 1]
                mean = jnp.sum(total * total) * (1.0 / (128.0 * 36.0))
                coef[...] = coef[...] - STEP * total / jnp.sqrt(jnp.full(total.shape, mean + EPS, F32))

        lefts, _ = adjoint_lanes(cot[0] * (0.25 / NPIX), cot[1] * (0.25 / NPIX), t2.at[3])
        objects[s] = lanes_mul(lefts[0], t1.at[2])
        for d in range(3):
            gather_copy(d).start()
        for d in range(3):
            gather_copy(d).wait()

        for d in range(2):
            near_copy(d).wait()
        for d in range(2):
            wanted = near[1 - d]
            total = None
            for p in range(4):
                match = jnp.where(wanted == 4 * t + p, 1.0, 0.0)
                one = jnp.max(match[:1, :], axis=1, keepdims=True) * objects[p]
                total = one if total is None else total + one
            send[d] = total
            object_copy(d).start()
        for d in range(2):
            object_copy(d).wait()
        for j in range(4):
            source = incoming[j]
            total = jnp.where(source // 4 == (t + 31) % 32, arrive[0], arrive[1])
            for p in range(4):
                total = jnp.where(source == 4 * t + p, objects[p], total)
            out[j] = total
        coef_out[...] = coef[0:36, :]

    return kernel


def per_device(observed, frame_pick, frame_count, incoming, start_coefficients, mode_basis):
    tables, mask, weight, flip = host_tables()
    vmem = pl.BlockSpec(memory_space=pltpu.VMEM)
    smem = pl.BlockSpec(memory_space=pltpu.SMEM)
    hbm = pl.BlockSpec(memory_space=pl.ANY)
    dma = pltpu.SemaphoreType.DMA
    objects, coef = pl.pallas_call(
        make_kernel(),
        out_shape=(
            jax.ShapeDtypeStruct((4, NPIX, NPIX), F32),
            jax.ShapeDtypeStruct((36, 128), F32),
        ),
        in_specs=[hbm, hbm, smem, smem, vmem, smem, vmem, vmem, vmem] + [hbm] * 6,
        out_specs=(vmem, vmem),
        scratch_shapes=[
            pltpu.VMEM((4, 8, NPIX, NPIX), BF16),
            pltpu.VMEM((36, XN, NPIX), F32),
            pltpu.VMEM((MROWS * BODD, NPIX), F32),
            pltpu.VMEM((4, 8, 128), jnp.int32),
            pltpu.VMEM((4, 8, 128), jnp.int32),
            pltpu.VMEM((FR, 128), F32),
            pltpu.VMEM((8, 256), F32),
            pltpu.VMEM((MROWS, 128), F32),
            pltpu.VMEM((8, 128), jnp.int32),
            pltpu.VMEM((4, 256, 256), BF16),
            pltpu.VMEM((4, 128, 384), BF16),
            pltpu.VMEM((128, 224), BF16),
            pltpu.VMEM((80, 384), BF16),
            pltpu.VMEM((384, 256), BF16),
            pltpu.VMEM((256, 256), BF16),
            pltpu.VMEM((QUADS, 256, 256), F32),
            pltpu.VMEM((TILES, 256, 256), BF16),
            pltpu.VMEM((FR, 256), BF16),
            pltpu.VMEM((40 * ODD, 128), F32),
            pltpu.VMEM((40 * ODD, 128), F32),
            pltpu.VMEM((FR, XN, 128), F32),
            pltpu.VMEM((2 * QUADS, 256, 256), F32),
            pltpu.VMEM((QUADS, 256, 256), F32),
            pltpu.VMEM((3, 128, 128), F32),
            pltpu.VMEM((ITERS, 3, 8, MROWS, 128), F32),
            pltpu.VMEM((4, 128, 128), F32),
            pltpu.VMEM((2, 8, 128), jnp.int32),
            pltpu.VMEM((2, 128, 128), F32),
            pltpu.VMEM((2, 128, 128), F32),
            dma((3,)),
            dma((3,)),
            dma((3,)),
            dma((3,)),
            dma((ITERS, 3, 7)),
            dma((ITERS, 3, 7)),
            dma((3,)),
            dma((3,)),
            dma((2, 2)),
            dma((2, 2)),
            dma((36,)),
            dma((7,)),
        ],
        compiler_params=pltpu.CompilerParams(
            collective_id=0, has_side_effects=True, vmem_limit_bytes=56 * 1024 * 1024
        ),
        cost_estimate=pl.CostEstimate(flops=30_000_000_000, bytes_accessed=10_000_000, transcendentals=0),
    )(
        observed, mode_basis, frame_pick, frame_count, start_coefficients.T, incoming,
        *[jnp.asarray(one) for one in [mask, weight, flip] + tables],
    )
    return objects, coef.T


def solution(mesh):
    placed = (P("tile", "spare", None, None), P("tile", "spare"), P("tile"), P("tile"), P(), P())
    return jax.shard_map(
        per_device,
        mesh=mesh,
        in_specs=placed,
        out_specs=(P("tile", None, None), P()),
        check_vma=False,
    )
```

```python
import math

import jax
import jax.numpy as jnp
import ml_dtypes
import numpy as np
from jax import lax
from jax.experimental import pallas as pl
from jax.experimental.pallas import tpu as pltpu
from jax.sharding import PartitionSpec as P

MESH = pl.DeviceIdType.MESH
F32 = jnp.float32
BF16 = jnp.bfloat16
NPIX = 128
ITERS = 2
GAMMA = 0.5
STEP = 0.25
EPS = 1e-06
X0, XN = 32, 72
MROWS = 40
FR = 32
ODD = 33
BODD = 73
QUADS = 8
PAIRS = 16
TILES = 17


def host_tables():
    index = np.arange(NPIX)
    angle = 2.0 * np.pi * (index[:, None] * index[None, :] % NPIX) / NPIX
    c, s = np.cos(angle), np.sin(angle)
    off = index - NPIX // 2
    disc = (off[:, None] ** 2 + off[None, :] ** 2 <= (NPIX // 4) ** 2).astype(np.float32)
    area = float(disc.sum())

    def two(table):
        high = table.astype(ml_dtypes.bfloat16)
        return high, (table - high.astype(np.float64)).astype(ml_dtypes.bfloat16)

    def wide(table, extra=0):
        high, low = two(table)
        return np.concatenate([high, high, low, np.zeros((len(table), extra), high.dtype)], axis=1)

    def tall(table):
        high, low = two(table)
        return np.concatenate([high, high, low], axis=0)

    def beside(table):
        return np.concatenate(two(table), axis=1)

    w1 = np.block([[c[32:96], -s[32:96]], [s[32:96], c[32:96]]]) / (NPIX * math.sqrt(area))
    w1t = np.concatenate([w1[64:].T, -w1[:64].T], axis=1)
    rows = np.concatenate([c[:64], c[64:65], s[1:64]], axis=0)
    order = np.concatenate([np.arange(65), 128 - np.arange(1, 64)])
    pupil = X0 + np.arange(XN)
    pupil[65] = NPIX // 2
    a2 = rows[:, pupil]
    a2t = np.concatenate([a2.T, np.zeros((8, NPIX))], axis=0)
    t2 = rows[:, order]
    cosine, sine = c[:, :64], -s[:, :64].copy()
    sine[:, 0] = c[:, 64]
    left, right = np.concatenate([cosine, sine], axis=1), np.concatenate([sine, cosine], axis=1)

    def twice(table):
        one = beside(table)
        return np.concatenate([one, one], axis=0)

    tables = [
        np.stack([twice(left), twice(right), twice(2.0 * left.T), twice(2.0 * right.T)]),
        np.stack([wide(t2), wide(t2.T), wide(rows), wide(rows.T)]),
        wide(a2, 8),
        wide(a2t),
        tall(w1),
        beside(w1t),
    ]
    mask = np.zeros((XN, 64), np.float32)
    mask[:65] = disc[X0 : X0 + 65, 32:96]
    mask[65, 0] = disc[64, 96]
    mask = np.concatenate([mask, mask], axis=1)
    weight = np.full((NPIX, NPIX), 4.0, np.float32)
    weight[:, 0] = 2.0
    weight[:, 64] = 2.0
    weight[64, 1] = 2.0
    weight[64, 65] = 2.0
    flip = np.ones((8, 256), np.float32)
    flip[1, 1::2] = -1.0
    return tables, mask, weight, flip


def split(x):
    high = x.astype(BF16)
    return high, (x - high.astype(F32)).astype(BF16)


def split3(x):
    high = x.astype(BF16).astype(F32)
    rest = x - high
    mid = rest.astype(BF16).astype(F32)
    return high, mid, rest - mid


def mm(a, b):
    return jnp.dot(a, b, preferred_element_type=F32)


def mm_nt(a, b):
    return lax.dot_general(a, b, (((1,), (1,)), ((), ())), preferred_element_type=F32)


def right_mul(x, table):
    high, low = split(x)
    return mm(jnp.concatenate([high, low, high], axis=1), table[...])


def left_mul(table, x):
    high, low = split(x)
    return mm(table[...], jnp.concatenate([high, low, high], axis=0))


def left_pupil(table, x):
    high = x.astype(BF16).astype(F32)
    zero = jnp.zeros((8, x.shape[1]), F32)
    return mm(table[...], jnp.concatenate([high, x - high, high, zero], axis=0).astype(BF16))


def lanes_mul(x, table):
    both = mm(jnp.concatenate(split(x), axis=1), table[...])
    return both[:, :128] + both[:, 128:]


def row0(v, first):
    here = lax.broadcasted_iota(jnp.int32, (8, v.shape[1]), 0) == 0
    return jnp.concatenate([jnp.where(here, first, v[:8]), v[8:]], axis=0)


def unfold(real, imag):
    cr, sr, ci, si = real[:64], real[64:], imag[:64], imag[64:]
    sr0, si0 = row0(sr, 0.0), row0(si, 0.0)
    return (
        jnp.concatenate([cr + si0, row0(cr - si0, sr[:8])], axis=0),
        jnp.concatenate([ci - sr0, row0(ci + sr0, si[:8])], axis=0),
    )


def fold(gr, gi):
    ga, gb, ha, hb = gr[:64], gr[64:], gi[:64], gi[64:]
    return (
        jnp.concatenate([row0(ga + gb, ga[:8]), row0(hb - ha, gb[:8])], axis=0),
        jnp.concatenate([row0(ha + hb, ha[:8]), row0(ga - gb, hb[:8])], axis=0),
    )


COS_POLY = (0.9999999889, -19.7392044666, 64.9391159283, -85.4501134275, 60.1674297919, -25.9668846126, 6.5277059630)


def horner(poly, z):
    total = poly[-1]
    for one in poly[-2::-1]:
        total = total * z + one
    return total


def unit_field(turns, mask):
    r = turns - jnp.floor(turns + 0.5)
    return mask * horner(COS_POLY, r * r)


def lane_mask(width, first):
    lane = lax.broadcasted_iota(jnp.int32, (8, width), 1)
    return (lane % 64) == first


def rows64(arr, fix):
    return jnp.concatenate([arr[:64], fix(arr[64:72]), arr[72:]], axis=0)


def left_half():
    return lax.broadcasted_iota(jnp.int32, (8, 128), 1)[:1] < 64


def half_spectra(lefts, rights, t2):
    low, at0 = left_half(), lane_mask(128, 0)[:1]
    lone, real, imag = [], [], []
    for one, two in zip(lefts, rights):
        di = pltpu.roll(jnp.where(low, two, one), 64, 1)
        total = jnp.sum(di, axis=0, keepdims=True)
        lone.append(pltpu.roll(jnp.broadcast_to(total, (8, 128)), 1, 1))
        real.append(jnp.where(low, one, two))
        imag.append(jnp.where(at0, 0.0, di))
    tr, ti = unfold(left_mul(t2, jnp.concatenate(real, axis=1)), left_mul(t2, jnp.concatenate(imag, axis=1)))
    here = lane_mask(256, 1) & (lax.broadcasted_iota(jnp.int32, (8, 256), 0) == 0)
    lone = jnp.concatenate(lone, axis=1)
    return rows64(tr, lambda v: jnp.where(here, lone, v)), rows64(ti, lambda v: jnp.where(here, 0.0, v))


def adjoint_lanes(gr, gi, t2t):
    width = gr.shape[1]
    here = lane_mask(width, 1) & (lax.broadcasted_iota(jnp.int32, (8, width), 0) == 0)
    lone = jnp.where(here, gr[64:72], 0.0)
    xr, xi = fold(
        rows64(gr, lambda v: jnp.where(here, 0.0, v)), rows64(gi, lambda v: jnp.where(here, 0.0, v))
    )
    dr, di = left_mul(t2t, xr), left_mul(t2t, xi)
    low, at0 = left_half(), lane_mask(128, 0)[:1]
    lefts, rights = [], []
    for i in range(width // 128):
        cols = slice(128 * i, 128 * i + 128)
        back = pltpu.roll(lone[:, cols], 127, 1)[:1]
        turned = pltpu.roll(jnp.where(at0, back, di[:, cols]), 64, 1)
        lefts.append(jnp.where(low, dr[:, cols], turned))
        rights.append(jnp.where(low, turned, dr[:, cols]))
    return lefts, rights


def rows_of(x, n):
    return x[128 * n : 128 * n + 128]


def make_kernel():
    def prep_spectra(sources, observed, t1, t2, spec):
        lanes = []
        for source in sources:
            sides = []
            for half in range(2):
                both = [mm(observed[source, 2 * i + half], t1[half, 0:128, :]) for i in range(4)]
                sides.append([(one[:, :128] + one[:, 128:]) * (1.0 / NPIX) for one in both])
            lanes.append(sides)
        for source, sides in zip(sources, lanes):
            for j in range(2):
                real, imag = half_spectra(sides[0][2 * j : 2 * j + 2], sides[1][2 * j : 2 * j + 2], t2)
                spec[2 * source + j, :128, :] = real
                spec[2 * source + j, 128:, :] = imag

    def prep_basis(i, basis, basis6, last=False):
        lane = lax.broadcasted_iota(jnp.int32, (MROWS, 128), 1)
        halves = []
        for j in range(2):
            if last:
                rows = pltpu.roll(basis[pl.ds(64 - 32 * j, MROWS, stride=BODD), :], 96 - 64 * j, 1)
            else:
                one = pltpu.roll(basis[pl.ds(2 * i + j, MROWS, stride=BODD), :], 96, 1)
                other = pltpu.roll(basis[pl.ds(2 * i + j + 32, MROWS, stride=BODD), :], 32, 1)
                rows = jnp.where(lane < 64, one, other)
            high, mid, low = split3(rows)
            halves.append(
                jnp.concatenate([high, mid, high, low, mid, high, jnp.zeros((16, NPIX), F32)], axis=0)
            )
        basis6[i] = jnp.concatenate(halves, axis=1).astype(BF16)

    def coef_six(coef, onehot):
        high, mid, low = split3(coef[...] * (0.5 / math.pi))
        stack = jnp.concatenate([high, high, mid, high, mid, low, jnp.zeros((16, NPIX), F32)], axis=0)
        return mm_nt(onehot[...].astype(BF16), stack.astype(BF16)).astype(BF16)

    def phases(six, basis6, phi):
        for i in range(TILES):
            both = mm(six[...], basis6[i])
            phi[pl.ds(2 * i * ODD, FR), :] = both[:, :128]
            phi[pl.ds((2 * i + 1) * ODD, FR), :] = both[:, 128:]

    def frame_field(f, phi, mask):
        lane = lax.broadcasted_iota(jnp.int32, (8, 128), 1)[:1]
        packed = phi[pl.ds(f, 40, stride=ODD), :]
        turned = pltpu.roll(packed, 64, 1)
        phase = jnp.concatenate(
            [jnp.where(lane < 64, packed, turned), jnp.where(lane < 64, turned[:32], packed[:32])], axis=0
        )
        phase = jnp.concatenate([phase[:32], phase[40:], phase[32:40]], axis=0)
        return unit_field(phase - jnp.where(lane < 64, 0.0, 0.25), mask[...])

    def modes(dphi, basis6):
        total = None
        for i in range(TILES):
            a = dphi[pl.ds(2 * i * ODD, FR), :]
            b = dphi[pl.ds((2 * i + 1) * ODD, FR), :]
            high, low = split(jnp.concatenate([a, b], axis=1))
            part = mm_nt(basis6[i, 0 : 2 * MROWS, :], jnp.concatenate([high, low], axis=0))
            total = part if total is None else total + part
        return total

    def forward(phi, mask, flip, w1, a2, t1, t2, field, amp, trans, keep):
        stack = []
        for i in range(PAIRS):
            for half in range(2):
                f = 2 * i + half
                one = frame_field(f, phi, mask)
                if keep:
                    field[f] = one
                stack.append(one)
        b = right_mul(jnp.concatenate(stack, axis=0), w1)
        spreads = [[], []]
        for i in range(PAIRS):
            parts = []
            for half in range(2):
                one = b[XN * (2 * i + half) : XN * (2 * i + half + 1)]
                parts.append(jnp.concatenate([one[:64], one[64:] * flip[...]], axis=0))
            ar, ai = unfold(
                left_pupil(a2, jnp.concatenate([parts[0][:, :128], parts[1][:, :128]], axis=1)),
                left_pupil(a2, jnp.concatenate([parts[0][:, 128:], parts[1][:, 128:]], axis=1)),
            )
            if keep:
                amp[i, :128, :] = ar
                amp[i, 128:, :] = ai
            spread = ar * ar + ai * ai
            for half in range(2):
                spreads[half].append(spread[:, 128 * half : 128 * half + 128])
        d = [lanes_mul(jnp.concatenate(spreads[half], axis=0), t1.at[half]) for half in range(2)]
        for g in range(QUADS):
            tr, ti = half_spectra(*[[rows_of(d[half], 2 * g), rows_of(d[half], 2 * g + 1)] for half in range(2)], t2)
            trans[g, :128, :] = tr
            trans[g, 128:, :] = ti

    def products(r, trans, spec, used, weight, cot):
        nr = ni = de = None
        upper, lower = pl.ds(pl.multiple_of(16 * r, 16), 16), pl.ds(pl.multiple_of(128 + 16 * r, 16), 16)
        for g in range(QUADS):
            u = used[g : g + 1, :]
            tr, ti, sr, si = trans[g, upper, :], trans[g, lower, :], spec[g, upper, :], spec[g, lower, :]
            vr, vi = tr * u, ti * u
            one = (sr * vr + si * vi, si * vr - sr * vi, tr * vr + ti * vi)
            nr, ni, de = one if g == 0 else (nr + one[0], ni + one[1], de + one[2])
        total = []
        for v in (nr, ni, de):
            v = v[:, :128] + v[:, 128:]
            total.append(v + pltpu.roll(v, 64, 1))
        scale = 1.0 / (GAMMA + total[2])
        qr, qi = total[0] * scale, total[1] * scale
        w = weight[upper, :]
        cot[0, upper, :] = w * qr
        cot[1, upper, :] = w * qi
        cot[2, upper, :] = w * (qr * qr + qi * qi)

    def backward(cot, spec, trans, used, flip, t2t, t1, a2t, w1t, amp, field, dphi):
        qr, qi, qq = [jnp.concatenate([cot[n], cot[n]], axis=1) for n in range(3)]
        sides = [[], []]
        for g in range(QUADS):
            u = used[g : g + 1, :]
            tr, ti = trans[g, :128, :], trans[g, 128:, :]
            sr, si = spec[g, :128, :], spec[g, 128:, :]
            gr = u * (qq * tr - qr * sr - qi * si)
            gi = u * (qi * sr - qr * si + qq * ti)
            for half, one in enumerate(adjoint_lanes(gr, gi, t2t)):
                sides[half] += one
        ds = [lanes_mul(jnp.concatenate(sides[half], axis=0), t1.at[2 + half]) for half in range(2)]
        stack = []
        for i in range(PAIRS):
            one = jnp.concatenate([rows_of(ds[0], i), rows_of(ds[1], i)], axis=1)
            xr, xi = fold(amp[i, :128, :] * one, amp[i, 128:, :] * one)
            dbr, dbi = left_mul(a2t, xr), left_mul(a2t, xi)
            for half in range(2):
                cols = slice(128 * half, 128 * half + 128)
                one = jnp.concatenate([dbr[:XN, cols], dbi[:XN, cols]], axis=1)
                stack += [one[:64], one[64:] * flip[...]]
        x = jnp.concatenate(stack, axis=0)
        n = x.shape[0]
        both = mm(jnp.concatenate(split(x), axis=0), w1t[...])
        d = both[:n, :128] + both[:n, 128:] + both[n:, :128] + both[n:, 128:]
        lane = lax.broadcasted_iota(jnp.int32, (8, 128), 1)[:1]
        for i in range(PAIRS):
            for half in range(2):
                f = place = 2 * i + half
                v = field[f] * d[XN * place : XN * place + XN]
                v = v + pltpu.roll(v, 64, 1)
                dphi[pl.ds(f, 40, stride=ODD), :] = jnp.concatenate(
                    [jnp.where(lane < 64, v[:32], v[32:64]), jnp.where(lane < 64, v[64:], 0.0)], axis=0
                )

    def kernel(
        observed_h, basis_h, pick, count, coef0, incoming, mask, weight, flip,
        t1_h, t2_h, a2_h, a2t_h, w1_h, w1t_h,
        out, coef_out,
        observed, window, basis, picks, picked, onehot, used, coef, own, t1, t2, a2, a2t, w1, w1t,
        spec, basis6, six, phi, dphi, field, amp, trans, cot, grads, objects, near, send, arrive,
        ob_send, ob_recv, pk_send, pk_recv, gr_send, gr_recv, ag_send, ag_recv, nb_send, nb_recv, basis_sem, load_sem,
    ):
        t, s = lax.axis_index("tile"), lax.axis_index("spare")
        tx, tz, tc = t // 8, (t // 2) % 4, t % 2
        spare_of = [(s + d) % 4 for d in (1, 2, 3)]
        groups = [
            [(t, v) for v in spare_of] + [(t + 1 - 2 * tc, (s + d) % 4) for d in range(4)],
            [(((tx + d) % 4) * 8 + tz * 2 + tc, s) for d in (1, 2, 3)],
            [(tx * 8 + ((tz + d) % 4) * 2 + tc, s) for d in (1, 2, 3)],
        ]
        places = [tc * 4 + s, tx, tz]
        beside = [((t + 1) % 32, s), ((t + 31) % 32, s)]

        barrier = pltpu.get_barrier_semaphore()
        partners = [who for group in groups for who in group] + beside
        for who in partners:
            pl.semaphore_signal(barrier, inc=1, device_id=who, device_id_type=MESH)

        loads = [
            pltpu.make_async_copy(src, dst, load_sem.at[n])
            for n, (src, dst) in enumerate(
                [(observed_h.at[s], observed.at[s]), (t1_h, t1), (t2_h, t2), (a2_h, a2), (a2t_h, a2t), (w1_h, w1), (w1t_h, w1t)]
            )
        ]
        windows = [
            pltpu.make_async_copy(
                basis_h.at[m, pl.ds(X0, XN), :], window.at[m], basis_sem.at[m]
            )
            for m in range(36)
        ]
        for one in windows + loads:
            one.start()

        def remote(src, dst, ssem, rsem, who):
            return pltpu.make_async_remote_copy(
                src_ref=src, dst_ref=dst, send_sem=ssem, recv_sem=rsem, device_id=who, device_id_type=MESH
            )

        def near_copy(d):
            return remote(own, near.at[d], nb_send.at[0, d], nb_recv.at[0, d], beside[d])

        def object_copy(d):
            return remote(send.at[d], arrive.at[d], nb_send.at[1, d], nb_recv.at[1, d], beside[d])

        def frames_copy(d):
            return remote(observed_h.at[spare_of[d]], observed.at[s], ob_send.at[d], ob_recv.at[d], groups[0][d])

        def picks_copy(d):
            return remote(picks.at[spare_of[d]], picked.at[s], pk_send.at[d], pk_recv.at[d], groups[0][d])

        def gather_copy(d):
            return remote(objects.at[s], objects.at[s], ag_send.at[d], ag_recv.at[d], groups[0][d])

        def grad_copy(it, stage, d):
            here = grads.at[it, stage, places[stage]]
            return remote(here, here, gr_send.at[it, stage, d], gr_recv.at[it, stage, d], groups[stage][d])

        lane = lax.broadcasted_iota(jnp.int32, (8, 128), 1)
        row = lax.broadcasted_iota(jnp.int32, (8, 128), 0)
        wanted = jnp.full((8, 128), -1, jnp.int32)
        for j in range(4):
            wanted = jnp.where(lane == j, incoming[j], wanted)
        own[...] = wanted
        for p in range(4):
            spread = jnp.full((8, 128), pick[p, 0], jnp.int32)
            for k in range(1, 8):
                spread = jnp.where(row == k, pick[p, k], spread)
            picks[p] = spread
        picked[s] = picks[s]
        pl.semaphore_wait(barrier, len(partners))
        for d in range(3):
            picks_copy(d).start()
        for d in (1, 0, 2):
            frames_copy(d).start()
        for d in range(2):
            near_copy(d).start()

        lane2 = lax.broadcasted_iota(jnp.int32, (8, 256), 1)
        row2 = lax.broadcasted_iota(jnp.int32, (8, 256), 0)
        used[...] = jnp.where(4 * (4 * (row2 % 2) + lane2 // 64) + row2 // 2 < count[s], 1.0, 0.0)
        coef[...] = jnp.zeros_like(coef)
        coef[0:36, :] = coef0[...]
        basis[pl.ds(36 * BODD, 4 * BODD), :] = jnp.zeros((4 * BODD, NPIX), F32)
        phi[...] = jnp.zeros_like(phi)
        for m in range(36):
            windows[m].wait()
            basis[pl.ds(m * BODD, XN), :] = window[m]
        for i in range(TILES):
            prep_basis(i, basis, basis6, last=i == TILES - 1)
        for d in range(3):
            picks_copy(d).wait()
        for a in range(4):
            onehot[8 * a : 8 * a + 8, :] = jnp.where(picked[a] == lane, 1.0, 0.0)
        for one in loads:
            one.wait()

        def transfer(keep):
            six[...] = coef_six(coef, onehot)
            phases(six, basis6, phi)
            forward(phi, mask, flip, w1, a2, t1, t2.at[0], field, amp, trans, keep)

        def ratios():
            pl.loop(0, 8, unroll=2)(lambda r: products(r, trans, spec, used, weight, cot))

        @pl.loop(0, ITERS)
        def iteration(it):
            transfer(keep=True)

            @pl.when(it == 0)
            def _():
                frames_copy(0).wait()
                frames_copy(2).wait()
                prep_spectra([s, (s + 3) % 4, (s + 1) % 4], observed, t1, t2.at[2], spec)
                frames_copy(1).wait()
                prep_spectra([(s + 2) % 4], observed, t1, t2.at[2], spec)

            ratios()
            backward(cot, spec, trans, used, flip, t2.at[1], t1, a2t, w1t, amp, field, dphi)
            acc = modes(dphi, basis6)
            slot_grad = acc[:MROWS] + acc[MROWS:]
            twice = jnp.concatenate([onehot[...], onehot[...]], axis=0).astype(BF16)
            total = None
            for part in split3(slot_grad):
                one = mm(part.astype(BF16), twice)
                total = one if total is None else total + one
            for stage in range(3):
                grads[it, stage, places[stage]] = total
                count = len(groups[stage])
                for d in range(count):
                    grad_copy(it, stage, d).start()
                for d in range(count):
                    grad_copy(it, stage, d).wait()
                total = grads[it, stage, 0]
                for d in range(count):
                    total = total + grads[it, stage, d + 1]
            mean = jnp.sum(total * total) * (1.0 / (128.0 * 36.0))
            coef[...] = coef[...] - STEP * total / jnp.sqrt(jnp.full(total.shape, mean + EPS, F32))

        transfer(keep=False)
        ratios()
        lefts, _ = adjoint_lanes(cot[0] * (0.25 / NPIX), cot[1] * (0.25 / NPIX), t2.at[3])
        objects[s] = lanes_mul(lefts[0], t1.at[2])
        for d in range(3):
            gather_copy(d).start()
        for d in range(3):
            gather_copy(d).wait()

        for d in range(2):
            near_copy(d).wait()
        for d in range(2):
            wanted = near[1 - d]
            total = None
            for p in range(4):
                match = jnp.where(wanted == 4 * t + p, 1.0, 0.0)
                one = jnp.max(match[:1, :], axis=1, keepdims=True) * objects[p]
                total = one if total is None else total + one
            send[d] = total
            object_copy(d).start()
        for d in range(2):
            object_copy(d).wait()
        for j in range(4):
            source = incoming[j]
            total = jnp.where(source // 4 == (t + 31) % 32, arrive[0], arrive[1])
            for p in range(4):
                total = jnp.where(source == 4 * t + p, objects[p], total)
            out[j] = total
        coef_out[...] = coef[0:36, :]

    return kernel


def hand_on(objects, coef, out, coef_out):
    out[...] = objects[...]
    coef_out[...] = coef[...]


def per_device(observed, frame_pick, frame_count, incoming, start_coefficients, mode_basis):
    tables, mask, weight, flip = host_tables()
    vmem = pl.BlockSpec(memory_space=pltpu.VMEM)
    smem = pl.BlockSpec(memory_space=pltpu.SMEM)
    hbm = pl.BlockSpec(memory_space=pl.ANY)
    dma = pltpu.SemaphoreType.DMA
    objects, coef = pl.pallas_call(
        make_kernel(),
        out_shape=(
            jax.ShapeDtypeStruct((4, NPIX, NPIX), F32),
            jax.ShapeDtypeStruct((36, 128), F32),
        ),
        in_specs=[hbm, hbm, smem, smem, vmem, smem, vmem, vmem, vmem] + [hbm] * 6,
        out_specs=(vmem, vmem),
        scratch_shapes=[
            pltpu.VMEM((4, 8, NPIX, NPIX), BF16),
            pltpu.VMEM((36, XN, NPIX), F32),
            pltpu.VMEM((MROWS * BODD, NPIX), F32),
            pltpu.VMEM((4, 8, 128), jnp.int32),
            pltpu.VMEM((4, 8, 128), jnp.int32),
            pltpu.VMEM((FR, 128), F32),
            pltpu.VMEM((8, 256), F32),
            pltpu.VMEM((MROWS, 128), F32),
            pltpu.VMEM((8, 128), jnp.int32),
            pltpu.VMEM((4, 256, 256), BF16),
            pltpu.VMEM((4, 128, 384), BF16),
            pltpu.VMEM((128, 224), BF16),
            pltpu.VMEM((80, 384), BF16),
            pltpu.VMEM((384, 256), BF16),
            pltpu.VMEM((256, 256), BF16),
            pltpu.VMEM((QUADS, 256, 256), F32),
            pltpu.VMEM((TILES, 256, 256), BF16),
            pltpu.VMEM((FR, 256), BF16),
            pltpu.VMEM((40 * ODD, 128), F32),
            pltpu.VMEM((40 * ODD, 128), F32),
            pltpu.VMEM((FR, XN, 128), F32),
            pltpu.VMEM((2 * QUADS, 256, 256), F32),
            pltpu.VMEM((QUADS, 256, 256), F32),
            pltpu.VMEM((3, 128, 128), F32),
            pltpu.VMEM((ITERS, 3, 8, MROWS, 128), F32),
            pltpu.VMEM((4, 128, 128), F32),
            pltpu.VMEM((2, 8, 128), jnp.int32),
            pltpu.VMEM((2, 128, 128), F32),
            pltpu.VMEM((2, 128, 128), F32),
            dma((3,)),
            dma((3,)),
            dma((3,)),
            dma((3,)),
            dma((ITERS, 3, 7)),
            dma((ITERS, 3, 7)),
            dma((3,)),
            dma((3,)),
            dma((2, 2)),
            dma((2, 2)),
            dma((36,)),
            dma((7,)),
        ],
        compiler_params=pltpu.CompilerParams(
            collective_id=0, has_side_effects=True, vmem_limit_bytes=56 * 1024 * 1024
        ),
        cost_estimate=pl.CostEstimate(flops=30_000_000_000, bytes_accessed=10_000_000, transcendentals=0),
    )(
        observed, mode_basis, frame_pick, frame_count, start_coefficients.T, incoming,
        *[jnp.asarray(one) for one in [mask, weight, flip] + tables],
    )
    restored, coef = pl.pallas_call(
        hand_on,
        out_shape=(jax.ShapeDtypeStruct((4, NPIX, NPIX), F32), jax.ShapeDtypeStruct((36, 128), F32)),
        in_specs=[vmem, vmem],
        out_specs=(vmem, vmem),
        cost_estimate=pl.CostEstimate(flops=500_000, bytes_accessed=700_000, transcendentals=0),
    )(objects, coef)
    return restored, coef.T


def solution(mesh):
    placed = (P("tile", "spare", None, None), P("tile", "spare"), P("tile"), P("tile"), P(), P())
    return jax.shard_map(
        per_device,
        mesh=mesh,
        in_specs=placed,
        out_specs=(P("tile", None, None), P()),
        check_vma=False,
    )
```

```python
import math

import jax
import jax.numpy as jnp
import ml_dtypes
import numpy as np
from jax import lax
from jax.experimental import pallas as pl
from jax.experimental.pallas import tpu as pltpu
from jax.sharding import PartitionSpec as P

MESH = pl.DeviceIdType.MESH
F32 = jnp.float32
BF16 = jnp.bfloat16
NPIX = 128
ITERS = 2
GAMMA = 0.5
STEP = 0.25
EPS = 1e-06
X0, XN = 32, 72
MROWS = 40
FR = 32
ODD = 33
BODD = 73
QUADS = 8
PAIRS = 16
TILES = 17


def host_tables():
    index = np.arange(NPIX)
    angle = 2.0 * np.pi * (index[:, None] * index[None, :] % NPIX) / NPIX
    c, s = np.cos(angle), np.sin(angle)
    off = index - NPIX // 2
    disc = (off[:, None] ** 2 + off[None, :] ** 2 <= (NPIX // 4) ** 2).astype(np.float32)
    area = float(disc.sum())

    def two(table):
        high = table.astype(ml_dtypes.bfloat16)
        return high, (table - high.astype(np.float64)).astype(ml_dtypes.bfloat16)

    def wide(table, extra=0):
        high, low = two(table)
        return np.concatenate([high, high, low, np.zeros((len(table), extra), high.dtype)], axis=1)

    def tall(table):
        high, low = two(table)
        return np.concatenate([high, high, low], axis=0)

    def beside(table):
        return np.concatenate(two(table), axis=1)

    w1 = np.block([[c[32:96], -s[32:96]], [s[32:96], c[32:96]]]) / (NPIX * math.sqrt(area))
    w1t = np.concatenate([w1[64:].T, -w1[:64].T], axis=1)
    rows = np.concatenate([c[:64], c[64:65], s[1:64]], axis=0)
    order = np.concatenate([np.arange(65), 128 - np.arange(1, 64)])
    pupil = X0 + np.arange(XN)
    pupil[65] = NPIX // 2
    a2 = rows[:, pupil]
    a2t = np.concatenate([a2.T, np.zeros((8, NPIX))], axis=0)
    t2 = rows[:, order]
    cosine, sine = c[:, :64], -s[:, :64].copy()
    sine[:, 0] = c[:, 64]
    left, right = np.concatenate([cosine, sine], axis=1), np.concatenate([sine, cosine], axis=1)

    def twice(table):
        one = beside(table)
        return np.concatenate([one, one], axis=0)

    tables = [
        np.stack([twice(left), twice(right), twice(2.0 * left.T), twice(2.0 * right.T)]),
        np.stack([wide(t2), wide(t2.T), wide(rows), wide(rows.T)]),
        wide(a2, 8),
        wide(a2t),
        tall(w1),
        beside(w1t),
    ]
    mask = np.zeros((XN, 64), np.float32)
    mask[:65] = disc[X0 : X0 + 65, 32:96]
    mask[65, 0] = disc[64, 96]
    mask = np.concatenate([mask, mask], axis=1)
    weight = np.full((NPIX, NPIX), 4.0, np.float32)
    weight[:, 0] = 2.0
    weight[:, 64] = 2.0
    weight[64, 1] = 2.0
    weight[64, 65] = 2.0
    flip = np.ones((8, 256), np.float32)
    flip[1, 1::2] = -1.0
    return tables, mask, weight, flip


def split(x):
    high = x.astype(BF16)
    return high, (x - high.astype(F32)).astype(BF16)


def split3(x):
    high = x.astype(BF16).astype(F32)
    rest = x - high
    mid = rest.astype(BF16).astype(F32)
    return high, mid, rest - mid


def mm(a, b):
    return jnp.dot(a, b, preferred_element_type=F32)


def mm_nt(a, b):
    return lax.dot_general(a, b, (((1,), (1,)), ((), ())), preferred_element_type=F32)


def right_mul(x, table):
    high, low = split(x)
    return mm(jnp.concatenate([high, low, high], axis=1), table[...])


def left_mul(table, x):
    high, low = split(x)
    return mm(table[...], jnp.concatenate([high, low, high], axis=0))


def left_pupil(table, x):
    high = x.astype(BF16).astype(F32)
    zero = jnp.zeros((8, x.shape[1]), F32)
    return mm(table[...], jnp.concatenate([high, x - high, high, zero], axis=0).astype(BF16))


def lanes_mul(x, table):
    both = mm(jnp.concatenate(split(x), axis=1), table[...])
    return both[:, :128] + both[:, 128:]


def row0(v, first):
    here = lax.broadcasted_iota(jnp.int32, (8, v.shape[1]), 0) == 0
    return jnp.concatenate([jnp.where(here, first, v[:8]), v[8:]], axis=0)


def unfold(real, imag):
    cr, sr, ci, si = real[:64], real[64:], imag[:64], imag[64:]
    sr0, si0 = row0(sr, 0.0), row0(si, 0.0)
    return (
        jnp.concatenate([cr + si0, row0(cr - si0, sr[:8])], axis=0),
        jnp.concatenate([ci - sr0, row0(ci + sr0, si[:8])], axis=0),
    )


def fold(gr, gi):
    ga, gb, ha, hb = gr[:64], gr[64:], gi[:64], gi[64:]
    return (
        jnp.concatenate([row0(ga + gb, ga[:8]), row0(hb - ha, gb[:8])], axis=0),
        jnp.concatenate([row0(ha + hb, ha[:8]), row0(ga - gb, hb[:8])], axis=0),
    )


COS_POLY = (0.9999999889, -19.7392044666, 64.9391159283, -85.4501134275, 60.1674297919, -25.9668846126, 6.5277059630)


def horner(poly, z):
    total = poly[-1]
    for one in poly[-2::-1]:
        total = total * z + one
    return total


def unit_field(turns, mask):
    r = turns - jnp.floor(turns + 0.5)
    return mask * horner(COS_POLY, r * r)


def lane_mask(width, first):
    lane = lax.broadcasted_iota(jnp.int32, (8, width), 1)
    return (lane % 64) == first


def rows64(arr, fix):
    return jnp.concatenate([arr[:64], fix(arr[64:72]), arr[72:]], axis=0)


def left_half():
    return lax.broadcasted_iota(jnp.int32, (8, 128), 1)[:1] < 64


def half_spectra(lefts, rights, t2):
    low, at0 = left_half(), lane_mask(128, 0)[:1]
    lone, real, imag = [], [], []
    for one, two in zip(lefts, rights):
        di = pltpu.roll(jnp.where(low, two, one), 64, 1)
        total = jnp.sum(di, axis=0, keepdims=True)
        lone.append(pltpu.roll(jnp.broadcast_to(total, (8, 128)), 1, 1))
        real.append(jnp.where(low, one, two))
        imag.append(jnp.where(at0, 0.0, di))
    tr, ti = unfold(left_mul(t2, jnp.concatenate(real, axis=1)), left_mul(t2, jnp.concatenate(imag, axis=1)))
    here = lane_mask(256, 1) & (lax.broadcasted_iota(jnp.int32, (8, 256), 0) == 0)
    lone = jnp.concatenate(lone, axis=1)
    return rows64(tr, lambda v: jnp.where(here, lone, v)), rows64(ti, lambda v: jnp.where(here, 0.0, v))


def adjoint_lanes(gr, gi, t2t):
    width = gr.shape[1]
    here = lane_mask(width, 1) & (lax.broadcasted_iota(jnp.int32, (8, width), 0) == 0)
    lone = jnp.where(here, gr[64:72], 0.0)
    xr, xi = fold(
        rows64(gr, lambda v: jnp.where(here, 0.0, v)), rows64(gi, lambda v: jnp.where(here, 0.0, v))
    )
    dr, di = left_mul(t2t, xr), left_mul(t2t, xi)
    low, at0 = left_half(), lane_mask(128, 0)[:1]
    lefts, rights = [], []
    for i in range(width // 128):
        cols = slice(128 * i, 128 * i + 128)
        back = pltpu.roll(lone[:, cols], 127, 1)[:1]
        turned = pltpu.roll(jnp.where(at0, back, di[:, cols]), 64, 1)
        lefts.append(jnp.where(low, dr[:, cols], turned))
        rights.append(jnp.where(low, turned, dr[:, cols]))
    return lefts, rights


def rows_of(x, n):
    return x[128 * n : 128 * n + 128]


def make_kernel():
    def prep_spectra(sources, observed, t1, t2, spec):
        lanes = []
        for source in sources:
            sides = []
            for half in range(2):
                both = [mm(observed[source, 2 * i + half], t1[half, 0:128, :]) for i in range(4)]
                sides.append([(one[:, :128] + one[:, 128:]) * (1.0 / NPIX) for one in both])
            lanes.append(sides)
        for source, sides in zip(sources, lanes):
            for j in range(2):
                real, imag = half_spectra(sides[0][2 * j : 2 * j + 2], sides[1][2 * j : 2 * j + 2], t2)
                spec[2 * source + j, :128, :] = real
                spec[2 * source + j, 128:, :] = imag

    def prep_basis(i, basis, basis6, last=False):
        lane = lax.broadcasted_iota(jnp.int32, (MROWS, 128), 1)
        halves = []
        for j in range(2):
            if last:
                rows = pltpu.roll(basis[pl.ds(64 - 32 * j, MROWS, stride=BODD), :], 96 - 64 * j, 1)
            else:
                one = pltpu.roll(basis[pl.ds(2 * i + j, MROWS, stride=BODD), :], 96, 1)
                other = pltpu.roll(basis[pl.ds(2 * i + j + 32, MROWS, stride=BODD), :], 32, 1)
                rows = jnp.where(lane < 64, one, other)
            high, mid, low = split3(rows)
            halves.append(
                jnp.concatenate([high, mid, high, low, mid, high, jnp.zeros((16, NPIX), F32)], axis=0)
            )
        basis6[i] = jnp.concatenate(halves, axis=1).astype(BF16)

    def coef_six(coef, onehot):
        high, mid, low = split3(coef[...] * (0.5 / math.pi))
        stack = jnp.concatenate([high, high, mid, high, mid, low, jnp.zeros((16, NPIX), F32)], axis=0)
        return mm_nt(onehot[...].astype(BF16), stack.astype(BF16)).astype(BF16)

    def phases(six, basis6, phi):
        for i in range(TILES):
            both = mm(six[...], basis6[i])
            phi[pl.ds(2 * i * ODD, FR), :] = both[:, :128]
            phi[pl.ds((2 * i + 1) * ODD, FR), :] = both[:, 128:]

    def frame_field(f, phi, mask):
        lane = lax.broadcasted_iota(jnp.int32, (8, 128), 1)[:1]
        packed = phi[pl.ds(f, 40, stride=ODD), :]
        turned = pltpu.roll(packed, 64, 1)
        phase = jnp.concatenate(
            [jnp.where(lane < 64, packed, turned), jnp.where(lane < 64, turned[:32], packed[:32])], axis=0
        )
        phase = jnp.concatenate([phase[:32], phase[40:], phase[32:40]], axis=0)
        return unit_field(phase - jnp.where(lane < 64, 0.0, 0.25), mask[...])

    def modes(dphi, basis6):
        total = None
        for i in range(TILES):
            a = dphi[pl.ds(2 * i * ODD, FR), :]
            b = dphi[pl.ds((2 * i + 1) * ODD, FR), :]
            high, low = split(jnp.concatenate([a, b], axis=1))
            part = mm_nt(basis6[i, 0 : 2 * MROWS, :], jnp.concatenate([high, low], axis=0))
            total = part if total is None else total + part
        return total

    def forward(phi, mask, flip, w1, a2, t1, t2, field, amp, trans, keep):
        stack = []
        for i in range(PAIRS):
            for half in range(2):
                f = 2 * i + half
                one = frame_field(f, phi, mask)
                if keep:
                    field[f] = one
                stack.append(one)
        b = right_mul(jnp.concatenate(stack, axis=0), w1)
        spreads = [[], []]
        for i in range(PAIRS):
            parts = []
            for half in range(2):
                one = b[XN * (2 * i + half) : XN * (2 * i + half + 1)]
                parts.append(jnp.concatenate([one[:64], one[64:] * flip[...]], axis=0))
            ar, ai = unfold(
                left_pupil(a2, jnp.concatenate([parts[0][:, :128], parts[1][:, :128]], axis=1)),
                left_pupil(a2, jnp.concatenate([parts[0][:, 128:], parts[1][:, 128:]], axis=1)),
            )
            if keep:
                amp[i, :128, :] = ar
                amp[i, 128:, :] = ai
            spread = ar * ar + ai * ai
            for half in range(2):
                spreads[half].append(spread[:, 128 * half : 128 * half + 128])
        d = [lanes_mul(jnp.concatenate(spreads[half], axis=0), t1.at[half]) for half in range(2)]
        for g in range(QUADS):
            tr, ti = half_spectra(*[[rows_of(d[half], 2 * g), rows_of(d[half], 2 * g + 1)] for half in range(2)], t2)
            trans[g, :128, :] = tr
            trans[g, 128:, :] = ti

    def products(r, trans, spec, used, weight, cot):
        nr = ni = de = None
        upper, lower = pl.ds(pl.multiple_of(16 * r, 16), 16), pl.ds(pl.multiple_of(128 + 16 * r, 16), 16)
        for g in range(QUADS):
            u = used[g : g + 1, :]
            tr, ti, sr, si = trans[g, upper, :], trans[g, lower, :], spec[g, upper, :], spec[g, lower, :]
            vr, vi = tr * u, ti * u
            one = (sr * vr + si * vi, si * vr - sr * vi, tr * vr + ti * vi)
            nr, ni, de = one if g == 0 else (nr + one[0], ni + one[1], de + one[2])
        total = []
        for v in (nr, ni, de):
            v = v[:, :128] + v[:, 128:]
            total.append(v + pltpu.roll(v, 64, 1))
        scale = 1.0 / (GAMMA + total[2])
        qr, qi = total[0] * scale, total[1] * scale
        w = weight[upper, :]
        cot[0, upper, :] = w * qr
        cot[1, upper, :] = w * qi
        cot[2, upper, :] = w * (qr * qr + qi * qi)

    def backward(cot, spec, trans, used, flip, t2t, t1, a2t, w1t, amp, field, dphi):
        qr, qi, qq = [jnp.concatenate([cot[n], cot[n]], axis=1) for n in range(3)]
        sides = [[], []]
        for g in range(QUADS):
            u = used[g : g + 1, :]
            tr, ti = trans[g, :128, :], trans[g, 128:, :]
            sr, si = spec[g, :128, :], spec[g, 128:, :]
            gr = u * (qq * tr - qr * sr - qi * si)
            gi = u * (qi * sr - qr * si + qq * ti)
            for half, one in enumerate(adjoint_lanes(gr, gi, t2t)):
                sides[half] += one
        ds = [lanes_mul(jnp.concatenate(sides[half], axis=0), t1.at[2 + half]) for half in range(2)]
        stack = []
        for i in range(PAIRS):
            one = jnp.concatenate([rows_of(ds[0], i), rows_of(ds[1], i)], axis=1)
            xr, xi = fold(amp[i, :128, :] * one, amp[i, 128:, :] * one)
            dbr, dbi = left_mul(a2t, xr), left_mul(a2t, xi)
            for half in range(2):
                cols = slice(128 * half, 128 * half + 128)
                one = jnp.concatenate([dbr[:XN, cols], dbi[:XN, cols]], axis=1)
                stack += [one[:64], one[64:] * flip[...]]
        x = jnp.concatenate(stack, axis=0)
        n = x.shape[0]
        both = mm(jnp.concatenate(split(x), axis=0), w1t[...])
        d = both[:n, :128] + both[:n, 128:] + both[n:, :128] + both[n:, 128:]
        lane = lax.broadcasted_iota(jnp.int32, (8, 128), 1)[:1]
        for i in range(PAIRS):
            for half in range(2):
                f = place = 2 * i + half
                v = field[f] * d[XN * place : XN * place + XN]
                v = v + pltpu.roll(v, 64, 1)
                dphi[pl.ds(f, 40, stride=ODD), :] = jnp.concatenate(
                    [jnp.where(lane < 64, v[:32], v[32:64]), jnp.where(lane < 64, v[64:], 0.0)], axis=0
                )

    def kernel(
        observed_h, basis_h, pick, count, coef0, incoming, mask, weight, flip,
        t1_h, t2_h, a2_h, a2t_h, w1_h, w1t_h,
        out, coef_out,
        observed, relay, window, basis, picks, picked, onehot, used, coef, own, t1, t2, a2, a2t, w1, w1t,
        spec, basis6, six, phi, dphi, field, amp, trans, cot, grads, objects, near, send, arrive,
        ob_send, ob_recv, pk_send, pk_recv, gr_send, gr_recv, ag_send, ag_recv, nb_send, nb_recv, basis_sem, load_sem,
    ):
        t, s = lax.axis_index("tile"), lax.axis_index("spare")
        tx, tz, tc = t // 8, (t // 2) % 4, t % 2
        spare_of = [(s + d) % 4 for d in (1, 2, 3)]
        groups = [
            [(t, v) for v in spare_of] + [(t + 1 - 2 * tc, (s + d) % 4) for d in range(4)],
            [(((tx + d) % 4) * 8 + tz * 2 + tc, s) for d in (1, 2, 3)],
            [(tx * 8 + ((tz + d) % 4) * 2 + tc, s) for d in (1, 2, 3)],
        ]
        places = [tc * 4 + s, tx, tz]
        beside = [((t + 1) % 32, s), ((t + 31) % 32, s)]

        barrier = pltpu.get_barrier_semaphore()
        partners = [who for group in groups for who in group] + beside
        for who in partners:
            pl.semaphore_signal(barrier, inc=1, device_id=who, device_id_type=MESH)

        loads = [
            pltpu.make_async_copy(src, dst, load_sem.at[n])
            for n, (src, dst) in enumerate(
                [(observed_h.at[s], observed.at[s]), (t1_h, t1), (t2_h, t2), (a2_h, a2), (a2t_h, a2t), (w1_h, w1), (w1t_h, w1t)]
            )
        ]
        windows = [
            pltpu.make_async_copy(
                basis_h.at[m, pl.ds(X0, XN), :], window.at[m], basis_sem.at[m]
            )
            for m in range(36)
        ]
        for one in windows + loads:
            one.start()

        def remote(src, dst, ssem, rsem, who):
            return pltpu.make_async_remote_copy(
                src_ref=src, dst_ref=dst, send_sem=ssem, recv_sem=rsem, device_id=who, device_id_type=MESH
            )

        def near_copy(d):
            return remote(own, near.at[d], nb_send.at[0, d], nb_recv.at[0, d], beside[d])

        def object_copy(d):
            return remote(send.at[d], arrive.at[d], nb_send.at[1, d], nb_recv.at[1, d], beside[d])

        ways = [(s + 1) % 4, (s + 3) % 4]
        across = (s + 2) % 4

        def frames_copy(way):
            return remote(
                observed_h.at[ways[way]], observed.at[s], ob_send.at[0, way], ob_recv.at[0, way], (t, ways[way])
            )

        def relay_copy(way):
            return remote(
                observed_h.at[across, pl.ds(4 * way, 4)], relay.at[way], ob_send.at[1, way], ob_recv.at[1, way], (t, ways[way])
            )

        def onward_copy(way):
            return remote(
                relay.at[way], observed.at[ways[1 - way], pl.ds(4 * way, 4)], ob_send.at[2, way], ob_recv.at[2, way],
                (t, ways[way]),
            )

        def picks_copy(d):
            return remote(picks.at[spare_of[d]], picked.at[s], pk_send.at[d], pk_recv.at[d], groups[0][d])

        def gather_copy(d):
            return remote(objects.at[s], objects.at[s], ag_send.at[d], ag_recv.at[d], groups[0][d])

        def grad_copy(it, stage, d):
            here = grads.at[it, stage, places[stage]]
            return remote(here, here, gr_send.at[it, stage, d], gr_recv.at[it, stage, d], groups[stage][d])

        lane = lax.broadcasted_iota(jnp.int32, (8, 128), 1)
        row = lax.broadcasted_iota(jnp.int32, (8, 128), 0)
        wanted = jnp.full((8, 128), -1, jnp.int32)
        for j in range(4):
            wanted = jnp.where(lane == j, incoming[j], wanted)
        own[...] = wanted
        for p in range(4):
            spread = jnp.full((8, 128), pick[p, 0], jnp.int32)
            for k in range(1, 8):
                spread = jnp.where(row == k, pick[p, k], spread)
            picks[p] = spread
        picked[s] = picks[s]
        pl.semaphore_wait(barrier, len(partners))
        for d in range(3):
            picks_copy(d).start()
        for way in range(2):
            relay_copy(way).start()
        for way in range(2):
            frames_copy(way).start()
        for d in range(2):
            near_copy(d).start()

        lane2 = lax.broadcasted_iota(jnp.int32, (8, 256), 1)
        row2 = lax.broadcasted_iota(jnp.int32, (8, 256), 0)
        used[...] = jnp.where(4 * (4 * (row2 % 2) + lane2 // 64) + row2 // 2 < count[s], 1.0, 0.0)
        coef[...] = jnp.zeros_like(coef)
        coef[0:36, :] = coef0[...]
        basis[pl.ds(36 * BODD, 4 * BODD), :] = jnp.zeros((4 * BODD, NPIX), F32)
        phi[...] = jnp.zeros_like(phi)
        for m in range(36):
            windows[m].wait()
            basis[pl.ds(m * BODD, XN), :] = window[m]
        for i in range(TILES):
            prep_basis(i, basis, basis6, last=i == TILES - 1)
        for d in range(3):
            picks_copy(d).wait()
        for a in range(4):
            onehot[8 * a : 8 * a + 8, :] = jnp.where(picked[a] == lane, 1.0, 0.0)
        for one in loads:
            one.wait()

        def transfer(keep, between=None):
            six[...] = coef_six(coef, onehot)
            phases(six, basis6, phi)
            if between is not None:
                between()
            forward(phi, mask, flip, w1, a2, t1, t2.at[0], field, amp, trans, keep)

        def ratios():
            pl.loop(0, 8, unroll=2)(lambda r: products(r, trans, spec, used, weight, cot))

        @pl.loop(0, ITERS)
        def iteration(it):
            def pass_on():
                @pl.when(it == 0)
                def _():
                    for way in range(2):
                        relay_copy(way).wait()
                        onward_copy(way).start()

            transfer(keep=True, between=pass_on)

            @pl.when(it == 0)
            def _():
                for way in range(2):
                    frames_copy(way).wait()
                prep_spectra([s] + ways, observed, t1, t2.at[2], spec)
                for way in range(2):
                    onward_copy(way).wait()
                prep_spectra([across], observed, t1, t2.at[2], spec)

            ratios()
            backward(cot, spec, trans, used, flip, t2.at[1], t1, a2t, w1t, amp, field, dphi)
            acc = modes(dphi, basis6)
            slot_grad = acc[:MROWS] + acc[MROWS:]
            twice = jnp.concatenate([onehot[...], onehot[...]], axis=0).astype(BF16)
            total = None
            for part in split3(slot_grad):
                one = mm(part.astype(BF16), twice)
                total = one if total is None else total + one
            for stage in range(3):
                grads[it, stage, places[stage]] = total
                count = len(groups[stage])
                for d in range(count):
                    grad_copy(it, stage, d).start()
                for d in range(count):
                    grad_copy(it, stage, d).wait()
                total = grads[it, stage, 0]
                for d in range(count):
                    total = total + grads[it, stage, d + 1]
            mean = jnp.sum(total * total) * (1.0 / (128.0 * 36.0))
            coef[...] = coef[...] - STEP * total / jnp.sqrt(jnp.full(total.shape, mean + EPS, F32))

        transfer(keep=False)
        ratios()
        lefts, _ = adjoint_lanes(cot[0] * (0.25 / NPIX), cot[1] * (0.25 / NPIX), t2.at[3])
        objects[s] = lanes_mul(lefts[0], t1.at[2])
        for d in range(3):
            gather_copy(d).start()
        for d in range(3):
            gather_copy(d).wait()

        for d in range(2):
            near_copy(d).wait()
        for d in range(2):
            wanted = near[1 - d]
            total = None
            for p in range(4):
                match = jnp.where(wanted == 4 * t + p, 1.0, 0.0)
                one = jnp.max(match[:1, :], axis=1, keepdims=True) * objects[p]
                total = one if total is None else total + one
            send[d] = total
            object_copy(d).start()
        for d in range(2):
            object_copy(d).wait()
        for j in range(4):
            source = incoming[j]
            total = jnp.where(source // 4 == (t + 31) % 32, arrive[0], arrive[1])
            for p in range(4):
                total = jnp.where(source == 4 * t + p, objects[p], total)
            out[j] = total
        coef_out[...] = coef[0:36, :]

    return kernel


def hand_on(objects, coef, out, coef_out):
    out[...] = objects[...]
    coef_out[...] = coef[...]


def per_device(observed, frame_pick, frame_count, incoming, start_coefficients, mode_basis):
    tables, mask, weight, flip = host_tables()
    vmem = pl.BlockSpec(memory_space=pltpu.VMEM)
    smem = pl.BlockSpec(memory_space=pltpu.SMEM)
    hbm = pl.BlockSpec(memory_space=pl.ANY)
    dma = pltpu.SemaphoreType.DMA
    objects, coef = pl.pallas_call(
        make_kernel(),
        out_shape=(
            jax.ShapeDtypeStruct((4, NPIX, NPIX), F32),
            jax.ShapeDtypeStruct((36, 128), F32),
        ),
        in_specs=[hbm, hbm, smem, smem, vmem, smem, vmem, vmem, vmem] + [hbm] * 6,
        out_specs=(vmem, vmem),
        scratch_shapes=[
            pltpu.VMEM((4, 8, NPIX, NPIX), BF16),
            pltpu.VMEM((2, 4, NPIX, NPIX), BF16),
            pltpu.VMEM((36, XN, NPIX), F32),
            pltpu.VMEM((MROWS * BODD, NPIX), F32),
            pltpu.VMEM((4, 8, 128), jnp.int32),
            pltpu.VMEM((4, 8, 128), jnp.int32),
            pltpu.VMEM((FR, 128), F32),
            pltpu.VMEM((8, 256), F32),
            pltpu.VMEM((MROWS, 128), F32),
            pltpu.VMEM((8, 128), jnp.int32),
            pltpu.VMEM((4, 256, 256), BF16),
            pltpu.VMEM((4, 128, 384), BF16),
            pltpu.VMEM((128, 224), BF16),
            pltpu.VMEM((80, 384), BF16),
            pltpu.VMEM((384, 256), BF16),
            pltpu.VMEM((256, 256), BF16),
            pltpu.VMEM((QUADS, 256, 256), F32),
            pltpu.VMEM((TILES, 256, 256), BF16),
            pltpu.VMEM((FR, 256), BF16),
            pltpu.VMEM((40 * ODD, 128), F32),
            pltpu.VMEM((40 * ODD, 128), F32),
            pltpu.VMEM((FR, XN, 128), F32),
            pltpu.VMEM((2 * QUADS, 256, 256), F32),
            pltpu.VMEM((QUADS, 256, 256), F32),
            pltpu.VMEM((3, 128, 128), F32),
            pltpu.VMEM((ITERS, 3, 8, MROWS, 128), F32),
            pltpu.VMEM((4, 128, 128), F32),
            pltpu.VMEM((2, 8, 128), jnp.int32),
            pltpu.VMEM((2, 128, 128), F32),
            pltpu.VMEM((2, 128, 128), F32),
            dma((3, 2)),
            dma((3, 2)),
            dma((3,)),
            dma((3,)),
            dma((ITERS, 3, 7)),
            dma((ITERS, 3, 7)),
            dma((3,)),
            dma((3,)),
            dma((2, 2)),
            dma((2, 2)),
            dma((36,)),
            dma((7,)),
        ],
        compiler_params=pltpu.CompilerParams(
            collective_id=0, has_side_effects=True, vmem_limit_bytes=56 * 1024 * 1024
        ),
        cost_estimate=pl.CostEstimate(flops=30_000_000_000, bytes_accessed=10_000_000, transcendentals=0),
    )(
        observed, mode_basis, frame_pick, frame_count, start_coefficients.T, incoming,
        *[jnp.asarray(one) for one in [mask, weight, flip] + tables],
    )
    restored, coef = pl.pallas_call(
        hand_on,
        out_shape=(jax.ShapeDtypeStruct((4, NPIX, NPIX), F32), jax.ShapeDtypeStruct((36, 128), F32)),
        in_specs=[vmem, vmem],
        out_specs=(vmem, vmem),
        cost_estimate=pl.CostEstimate(flops=500_000, bytes_accessed=700_000, transcendentals=0),
    )(objects, coef)
    return restored, coef.T


def solution(mesh):
    placed = (P("tile", "spare", None, None), P("tile", "spare"), P("tile"), P("tile"), P(), P())
    return jax.shard_map(
        per_device,
        mesh=mesh,
        in_specs=placed,
        out_specs=(P("tile", None, None), P()),
        check_vma=False,
    )
```

```python
import math

import jax
import jax.numpy as jnp
import ml_dtypes
import numpy as np
from jax import lax
from jax.experimental import pallas as pl
from jax.experimental.pallas import tpu as pltpu
from jax.sharding import PartitionSpec as P

MESH = pl.DeviceIdType.MESH
F32 = jnp.float32
BF16 = jnp.bfloat16
NPIX = 128
ITERS = 2
GAMMA = 0.5
STEP = 0.25
EPS = 1e-06
X0, XN = 32, 72
MROWS = 40
FR = 32
ODD = 33
BODD = 73
QUADS = 8
PAIRS = 16
TILES = 17


def host_tables():
    index = np.arange(NPIX)
    angle = 2.0 * np.pi * (index[:, None] * index[None, :] % NPIX) / NPIX
    c, s = np.cos(angle), np.sin(angle)
    off = index - NPIX // 2
    disc = (off[:, None] ** 2 + off[None, :] ** 2 <= (NPIX // 4) ** 2).astype(np.float32)
    area = float(disc.sum())

    def two(table):
        high = table.astype(ml_dtypes.bfloat16)
        return high, (table - high.astype(np.float64)).astype(ml_dtypes.bfloat16)

    def wide(table, extra=0):
        high, low = two(table)
        return np.concatenate([high, high, low, np.zeros((len(table), extra), high.dtype)], axis=1)

    def tall(table):
        high, low = two(table)
        return np.concatenate([high, high, low], axis=0)

    def beside(table):
        return np.concatenate(two(table), axis=1)

    w1 = np.block([[c[32:96], -s[32:96]], [s[32:96], c[32:96]]]) / (NPIX * math.sqrt(area))
    w1t = np.concatenate([w1[64:].T, -w1[:64].T], axis=1)
    rows = np.concatenate([c[:64], c[64:65], s[1:64]], axis=0)
    order = np.concatenate([np.arange(65), 128 - np.arange(1, 64)])
    pupil = X0 + np.arange(XN)
    pupil[65] = NPIX // 2
    a2 = rows[:, pupil]
    a2t = np.concatenate([a2.T, np.zeros((8, NPIX))], axis=0)
    t2 = rows[:, order]
    cosine, sine = c[:, :64], -s[:, :64].copy()
    sine[:, 0] = c[:, 64]
    left, right = np.concatenate([cosine, sine], axis=1), np.concatenate([sine, cosine], axis=1)

    def twice(table):
        one = beside(table)
        return np.concatenate([one, one], axis=0)

    tables = [
        np.stack([twice(left), twice(right), twice(2.0 * left.T), twice(2.0 * right.T)]),
        np.stack([wide(t2), wide(t2.T), wide(rows), wide(rows.T)]),
        wide(a2, 8),
        wide(a2t),
        tall(w1),
        beside(w1t),
    ]
    mask = np.zeros((XN, 64), np.float32)
    mask[:65] = disc[X0 : X0 + 65, 32:96]
    mask[65, 0] = disc[64, 96]
    mask = np.concatenate([mask, mask], axis=1)
    weight = np.full((NPIX, NPIX), 4.0, np.float32)
    weight[:, 0] = 2.0
    weight[:, 64] = 2.0
    weight[64, 1] = 2.0
    weight[64, 65] = 2.0
    flip = np.ones((8, 256), np.float32)
    flip[1, 1::2] = -1.0
    return tables, mask, weight, flip


def split(x):
    high = x.astype(BF16)
    return high, (x - high.astype(F32)).astype(BF16)


def split3(x):
    high = x.astype(BF16).astype(F32)
    rest = x - high
    mid = rest.astype(BF16).astype(F32)
    return high, mid, rest - mid


def mm(a, b):
    return jnp.dot(a, b, preferred_element_type=F32)


def mm_nt(a, b):
    return lax.dot_general(a, b, (((1,), (1,)), ((), ())), preferred_element_type=F32)


def right_mul(x, table):
    high, low = split(x)
    return mm(jnp.concatenate([high, low, high], axis=1), table[...])


def left_mul(table, x):
    high, low = split(x)
    return mm(table[...], jnp.concatenate([high, low, high], axis=0))


def left_pupil(table, x):
    high = x.astype(BF16).astype(F32)
    zero = jnp.zeros((8, x.shape[1]), F32)
    return mm(table[...], jnp.concatenate([high, x - high, high, zero], axis=0).astype(BF16))


def lanes_mul(x, table):
    both = mm(jnp.concatenate(split(x), axis=1), table[...])
    return both[:, :128] + both[:, 128:]


def row0(v, first):
    here = lax.broadcasted_iota(jnp.int32, (8, v.shape[1]), 0) == 0
    return jnp.concatenate([jnp.where(here, first, v[:8]), v[8:]], axis=0)


def unfold(real, imag):
    cr, sr, ci, si = real[:64], real[64:], imag[:64], imag[64:]
    sr0, si0 = row0(sr, 0.0), row0(si, 0.0)
    return (
        jnp.concatenate([cr + si0, row0(cr - si0, sr[:8])], axis=0),
        jnp.concatenate([ci - sr0, row0(ci + sr0, si[:8])], axis=0),
    )


def fold(gr, gi):
    ga, gb, ha, hb = gr[:64], gr[64:], gi[:64], gi[64:]
    return (
        jnp.concatenate([row0(ga + gb, ga[:8]), row0(hb - ha, gb[:8])], axis=0),
        jnp.concatenate([row0(ha + hb, ha[:8]), row0(ga - gb, hb[:8])], axis=0),
    )


COS_POLY = (0.9999999889, -19.7392044666, 64.9391159283, -85.4501134275, 60.1674297919, -25.9668846126, 6.5277059630)


def horner(poly, z):
    total = poly[-1]
    for one in poly[-2::-1]:
        total = total * z + one
    return total


def unit_field(turns, mask):
    r = turns - jnp.floor(turns + 0.5)
    return mask * horner(COS_POLY, r * r)


def lane_mask(width, first):
    lane = lax.broadcasted_iota(jnp.int32, (8, width), 1)
    return (lane % 64) == first


def rows64(arr, fix):
    return jnp.concatenate([arr[:64], fix(arr[64:72]), arr[72:]], axis=0)


def left_half():
    return lax.broadcasted_iota(jnp.int32, (8, 128), 1)[:1] < 64


def half_spectra(lefts, rights, t2):
    low, at0 = left_half(), lane_mask(128, 0)[:1]
    lone, real, imag = [], [], []
    for one, two in zip(lefts, rights):
        di = pltpu.roll(jnp.where(low, two, one), 64, 1)
        total = jnp.sum(di, axis=0, keepdims=True)
        lone.append(pltpu.roll(jnp.broadcast_to(total, (8, 128)), 1, 1))
        real.append(jnp.where(low, one, two))
        imag.append(jnp.where(at0, 0.0, di))
    tr, ti = unfold(left_mul(t2, jnp.concatenate(real, axis=1)), left_mul(t2, jnp.concatenate(imag, axis=1)))
    here = lane_mask(256, 1) & (lax.broadcasted_iota(jnp.int32, (8, 256), 0) == 0)
    lone = jnp.concatenate(lone, axis=1)
    return rows64(tr, lambda v: jnp.where(here, lone, v)), rows64(ti, lambda v: jnp.where(here, 0.0, v))


def adjoint_lanes(gr, gi, t2t):
    width = gr.shape[1]
    here = lane_mask(width, 1) & (lax.broadcasted_iota(jnp.int32, (8, width), 0) == 0)
    lone = jnp.where(here, gr[64:72], 0.0)
    xr, xi = fold(
        rows64(gr, lambda v: jnp.where(here, 0.0, v)), rows64(gi, lambda v: jnp.where(here, 0.0, v))
    )
    dr, di = left_mul(t2t, xr), left_mul(t2t, xi)
    low, at0 = left_half(), lane_mask(128, 0)[:1]
    lefts, rights = [], []
    for i in range(width // 128):
        cols = slice(128 * i, 128 * i + 128)
        back = pltpu.roll(lone[:, cols], 127, 1)[:1]
        turned = pltpu.roll(jnp.where(at0, back, di[:, cols]), 64, 1)
        lefts.append(jnp.where(low, dr[:, cols], turned))
        rights.append(jnp.where(low, turned, dr[:, cols]))
    return lefts, rights


def rows_of(x, n):
    return x[128 * n : 128 * n + 128]


def make_kernel():
    def prep_spectra(sources, observed, t1, t2, spec):
        lanes = []
        for source in sources:
            sides = []
            for half in range(2):
                both = [mm(observed[source, 2 * i + half], t1[half, 0:128, :]) for i in range(4)]
                sides.append([(one[:, :128] + one[:, 128:]) * (1.0 / NPIX) for one in both])
            lanes.append(sides)
        for source, sides in zip(sources, lanes):
            for j in range(2):
                real, imag = half_spectra(sides[0][2 * j : 2 * j + 2], sides[1][2 * j : 2 * j + 2], t2)
                spec[2 * source + j, :128, :] = real
                spec[2 * source + j, 128:, :] = imag

    def prep_basis(i, basis, basis6, last=False):
        lane = lax.broadcasted_iota(jnp.int32, (MROWS, 128), 1)
        halves = []
        for j in range(2):
            if last:
                rows = pltpu.roll(basis[pl.ds(64 - 32 * j, MROWS, stride=BODD), :], 96 - 64 * j, 1)
            else:
                one = pltpu.roll(basis[pl.ds(2 * i + j, MROWS, stride=BODD), :], 96, 1)
                other = pltpu.roll(basis[pl.ds(2 * i + j + 32, MROWS, stride=BODD), :], 32, 1)
                rows = jnp.where(lane < 64, one, other)
            high, mid, low = split3(rows)
            halves.append(
                jnp.concatenate([high, mid, high, low, mid, high, jnp.zeros((16, NPIX), F32)], axis=0)
            )
        basis6[i] = jnp.concatenate(halves, axis=1).astype(BF16)

    def coef_six(coef, onehot):
        high, mid, low = split3(coef[...] * (0.5 / math.pi))
        stack = jnp.concatenate([high, high, mid, high, mid, low, jnp.zeros((16, NPIX), F32)], axis=0)
        return mm_nt(onehot[...].astype(BF16), stack.astype(BF16)).astype(BF16)

    def phases(six, basis6, phi):
        for i in range(TILES):
            both = mm(six[...], basis6[i])
            phi[pl.ds(2 * i * ODD, FR), :] = both[:, :128]
            phi[pl.ds((2 * i + 1) * ODD, FR), :] = both[:, 128:]

    def frame_field(f, phi, mask):
        lane = lax.broadcasted_iota(jnp.int32, (8, 128), 1)[:1]
        packed = phi[pl.ds(f, 40, stride=ODD), :]
        turned = pltpu.roll(packed, 64, 1)
        phase = jnp.concatenate(
            [jnp.where(lane < 64, packed, turned), jnp.where(lane < 64, turned[:32], packed[:32])], axis=0
        )
        phase = jnp.concatenate([phase[:32], phase[40:], phase[32:40]], axis=0)
        return unit_field(phase - jnp.where(lane < 64, 0.0, 0.25), mask[...])

    def modes(dphi, basis6):
        total = None
        for i in range(TILES):
            a = dphi[pl.ds(2 * i * ODD, FR), :]
            b = dphi[pl.ds((2 * i + 1) * ODD, FR), :]
            high, low = split(jnp.concatenate([a, b], axis=1))
            part = mm_nt(basis6[i, 0 : 2 * MROWS, :], jnp.concatenate([high, low], axis=0))
            total = part if total is None else total + part
        return total

    def forward(phi, mask, flip, w1, a2, t1, t2, field, amp, trans, keep):
        stack = []
        for i in range(PAIRS):
            for half in range(2):
                f = 2 * i + half
                one = frame_field(f, phi, mask)
                if keep:
                    field[f] = one
                stack.append(one)
        b = right_mul(jnp.concatenate(stack, axis=0), w1)
        spreads = [[], []]
        for i in range(PAIRS):
            parts = []
            for half in range(2):
                one = b[XN * (2 * i + half) : XN * (2 * i + half + 1)]
                parts.append(jnp.concatenate([one[:64], one[64:] * flip[...]], axis=0))
            ar, ai = unfold(
                left_pupil(a2, jnp.concatenate([parts[0][:, :128], parts[1][:, :128]], axis=1)),
                left_pupil(a2, jnp.concatenate([parts[0][:, 128:], parts[1][:, 128:]], axis=1)),
            )
            if keep:
                amp[i, :128, :] = ar
                amp[i, 128:, :] = ai
            spread = ar * ar + ai * ai
            for half in range(2):
                spreads[half].append(spread[:, 128 * half : 128 * half + 128])
        d = [lanes_mul(jnp.concatenate(spreads[half], axis=0), t1.at[half]) for half in range(2)]
        for g in range(QUADS):
            tr, ti = half_spectra(*[[rows_of(d[half], 2 * g), rows_of(d[half], 2 * g + 1)] for half in range(2)], t2)
            trans[g, :128, :] = tr
            trans[g, 128:, :] = ti

    def products(r, trans, spec, used, weight, cot):
        nr = ni = de = None
        upper, lower = pl.ds(pl.multiple_of(16 * r, 16), 16), pl.ds(pl.multiple_of(128 + 16 * r, 16), 16)
        for g in range(QUADS):
            u = used[g : g + 1, :]
            tr, ti, sr, si = trans[g, upper, :], trans[g, lower, :], spec[g, upper, :], spec[g, lower, :]
            vr, vi = tr * u, ti * u
            one = (sr * vr + si * vi, si * vr - sr * vi, tr * vr + ti * vi)
            nr, ni, de = one if g == 0 else (nr + one[0], ni + one[1], de + one[2])
        total = []
        for v in (nr, ni, de):
            v = v[:, :128] + v[:, 128:]
            total.append(v + pltpu.roll(v, 64, 1))
        scale = 1.0 / (GAMMA + total[2])
        qr, qi = total[0] * scale, total[1] * scale
        w = weight[upper, :]
        cot[0, upper, :] = w * qr
        cot[1, upper, :] = w * qi
        cot[2, upper, :] = w * (qr * qr + qi * qi)

    def backward(cot, spec, trans, used, flip, t2t, t1, a2t, w1t, amp, field, dphi):
        qr, qi, qq = [jnp.concatenate([cot[n], cot[n]], axis=1) for n in range(3)]
        sides = [[], []]
        for g in range(QUADS):
            u = used[g : g + 1, :]
            tr, ti = trans[g, :128, :], trans[g, 128:, :]
            sr, si = spec[g, :128, :], spec[g, 128:, :]
            gr = u * (qq * tr - qr * sr - qi * si)
            gi = u * (qi * sr - qr * si + qq * ti)
            for half, one in enumerate(adjoint_lanes(gr, gi, t2t)):
                sides[half] += one
        ds = [lanes_mul(jnp.concatenate(sides[half], axis=0), t1.at[2 + half]) for half in range(2)]
        stack = []
        for i in range(PAIRS):
            one = jnp.concatenate([rows_of(ds[0], i), rows_of(ds[1], i)], axis=1)
            xr, xi = fold(amp[i, :128, :] * one, amp[i, 128:, :] * one)
            dbr, dbi = left_mul(a2t, xr), left_mul(a2t, xi)
            for half in range(2):
                cols = slice(128 * half, 128 * half + 128)
                one = jnp.concatenate([dbr[:XN, cols], dbi[:XN, cols]], axis=1)
                stack += [one[:64], one[64:] * flip[...]]
        x = jnp.concatenate(stack, axis=0)
        n = x.shape[0]
        both = mm(jnp.concatenate(split(x), axis=0), w1t[...])
        d = both[:n, :128] + both[:n, 128:] + both[n:, :128] + both[n:, 128:]
        lane = lax.broadcasted_iota(jnp.int32, (8, 128), 1)[:1]
        for i in range(PAIRS):
            for half in range(2):
                f = place = 2 * i + half
                v = field[f] * d[XN * place : XN * place + XN]
                v = v + pltpu.roll(v, 64, 1)
                dphi[pl.ds(f, 40, stride=ODD), :] = jnp.concatenate(
                    [jnp.where(lane < 64, v[:32], v[32:64]), jnp.where(lane < 64, v[64:], 0.0)], axis=0
                )

    def kernel(
        observed_h, basis_h, pick, count, coef0, incoming, mask, weight, flip,
        t1_h, t2_h, a2_h, a2t_h, w1_h, w1t_h,
        out, coef_out,
        observed, relay, window, basis, picks, picked, onehot, used, coef, own, t1, t2, a2, a2t, w1, w1t,
        spec, basis6, six, phi, dphi, field, amp, trans, cot, pieces, grads, objects, near, send, arrive,
        ob_send, ob_recv, pk_send, pk_recv, gr_send, gr_recv, ag_send, ag_recv, nb_send, nb_recv, basis_sem, load_sem,
    ):
        t, s = lax.axis_index("tile"), lax.axis_index("spare")
        tx, tz, tc = t // 8, (t // 2) % 4, t % 2
        spare_of = [(s + d) % 4 for d in (1, 2, 3)]
        groups = [
            [(t, v) for v in spare_of] + [(t + 1 - 2 * tc, (s + d) % 4) for d in range(4)],
            [(((tx + d) % 4) * 8 + tz * 2 + tc, s) for d in (1, 2, 3)],
            [(tx * 8 + ((tz + d) % 4) * 2 + tc, s) for d in (1, 2, 3)],
        ]
        place = tc * 4 + s
        piece_of = [tc * 4 + v for v in spare_of] + [(1 - tc) * 4 + (s + d) % 4 for d in range(4)]
        beside = [((t + 1) % 32, s), ((t + 31) % 32, s)]

        barrier = pltpu.get_barrier_semaphore()
        partners = [who for group in groups for who in group] + beside
        for who in partners:
            pl.semaphore_signal(barrier, inc=1, device_id=who, device_id_type=MESH)

        loads = [
            pltpu.make_async_copy(src, dst, load_sem.at[n])
            for n, (src, dst) in enumerate(
                [(observed_h.at[s], observed.at[s]), (t1_h, t1), (t2_h, t2), (a2_h, a2), (a2t_h, a2t), (w1_h, w1), (w1t_h, w1t)]
            )
        ]
        windows = [
            pltpu.make_async_copy(
                basis_h.at[m, pl.ds(X0, XN), :], window.at[m], basis_sem.at[m]
            )
            for m in range(36)
        ]
        for one in windows + loads:
            one.start()

        def remote(src, dst, ssem, rsem, who):
            return pltpu.make_async_remote_copy(
                src_ref=src, dst_ref=dst, send_sem=ssem, recv_sem=rsem, device_id=who, device_id_type=MESH
            )

        def near_copy(d):
            return remote(own, near.at[d], nb_send.at[0, d], nb_recv.at[0, d], beside[d])

        def object_copy(d):
            return remote(send.at[d], arrive.at[d], nb_send.at[1, d], nb_recv.at[1, d], beside[d])

        ways = [(s + 1) % 4, (s + 3) % 4]
        across = (s + 2) % 4

        def frames_copy(way):
            return remote(
                observed_h.at[ways[way]], observed.at[s], ob_send.at[0, way], ob_recv.at[0, way], (t, ways[way])
            )

        def relay_copy(way):
            return remote(
                observed_h.at[across, pl.ds(4 * way, 4)], relay.at[way], ob_send.at[1, way], ob_recv.at[1, way], (t, ways[way])
            )

        def onward_copy(way):
            return remote(
                relay.at[way], observed.at[ways[1 - way], pl.ds(4 * way, 4)], ob_send.at[2, way], ob_recv.at[2, way],
                (t, ways[way]),
            )

        def picks_copy(d):
            return remote(picks.at[spare_of[d]], picked.at[s], pk_send.at[d], pk_recv.at[d], groups[0][d])

        def gather_copy(part, way):
            here = objects.at[s, pl.ds(64 * (way ^ part), 64), :]
            return remote(here, here, ag_send.at[part, way], ag_recv.at[part, way], (t, ways[way]))

        def gather_onward(way):
            here = objects.at[ways[1 - way], pl.ds(64 * way, 64), :]
            return remote(here, here, ag_send.at[2, way], ag_recv.at[2, way], (t, ways[way]))

        stages = [groups[0], groups[1], groups[2], groups[0]]
        places = [place, tx, tz, place]

        def grad_copy(it, stage, d):
            here = grads.at[it, stage, places[stage]]
            src = pieces.at[it, piece_of[d]] if stage == 0 else here
            return remote(src, here, gr_send.at[it, stage, d], gr_recv.at[it, stage, d], stages[stage][d])

        lane = lax.broadcasted_iota(jnp.int32, (8, 128), 1)
        row = lax.broadcasted_iota(jnp.int32, (8, 128), 0)
        wanted = jnp.full((8, 128), -1, jnp.int32)
        for j in range(4):
            wanted = jnp.where(lane == j, incoming[j], wanted)
        own[...] = wanted
        for p in range(4):
            spread = jnp.full((8, 128), pick[p, 0], jnp.int32)
            for k in range(1, 8):
                spread = jnp.where(row == k, pick[p, k], spread)
            picks[p] = spread
        picked[s] = picks[s]
        pl.semaphore_wait(barrier, len(partners))
        for d in range(3):
            picks_copy(d).start()
        for way in range(2):
            relay_copy(way).start()
        for way in range(2):
            frames_copy(way).start()
        for d in range(2):
            near_copy(d).start()

        lane2 = lax.broadcasted_iota(jnp.int32, (8, 256), 1)
        row2 = lax.broadcasted_iota(jnp.int32, (8, 256), 0)
        used[...] = jnp.where(4 * (4 * (row2 % 2) + lane2 // 64) + row2 // 2 < count[s], 1.0, 0.0)
        coef[...] = jnp.zeros_like(coef)
        coef[0:36, :] = coef0[...]
        basis[pl.ds(36 * BODD, 4 * BODD), :] = jnp.zeros((4 * BODD, NPIX), F32)
        phi[...] = jnp.zeros_like(phi)
        for m in range(36):
            windows[m].wait()
            basis[pl.ds(m * BODD, XN), :] = window[m]
        for i in range(TILES):
            prep_basis(i, basis, basis6, last=i == TILES - 1)
        for d in range(3):
            picks_copy(d).wait()
        for a in range(4):
            onehot[8 * a : 8 * a + 8, :] = jnp.where(picked[a] == lane, 1.0, 0.0)
        for one in loads:
            one.wait()

        def transfer(keep, between=None):
            six[...] = coef_six(coef, onehot)
            phases(six, basis6, phi)
            if between is not None:
                between()
            forward(phi, mask, flip, w1, a2, t1, t2.at[0], field, amp, trans, keep)

        def ratios():
            pl.loop(0, 8, unroll=2)(lambda r: products(r, trans, spec, used, weight, cot))

        @pl.loop(0, ITERS)
        def iteration(it):
            def pass_on():
                @pl.when(it == 0)
                def _():
                    for way in range(2):
                        relay_copy(way).wait()
                        onward_copy(way).start()

            transfer(keep=True, between=pass_on)

            @pl.when(it == 0)
            def _():
                for way in range(2):
                    frames_copy(way).wait()
                prep_spectra([s] + ways, observed, t1, t2.at[2], spec)
                for way in range(2):
                    onward_copy(way).wait()
                prep_spectra([across], observed, t1, t2.at[2], spec)

            ratios()
            backward(cot, spec, trans, used, flip, t2.at[1], t1, a2t, w1t, amp, field, dphi)
            acc = modes(dphi, basis6)
            slot_grad = acc[:MROWS] + acc[MROWS:]
            twice = jnp.concatenate([onehot[...], onehot[...]], axis=0).astype(BF16)
            total = None
            for part in split3(slot_grad):
                one = mm(part.astype(BF16), twice)
                total = one if total is None else total + one
            for j in range(8):
                pieces[it, j, 0:5, :] = total[5 * j : 5 * j + 5]
                pieces[it, j, 5:8, :] = jnp.zeros((3, 128), F32)
            piece = pieces[it, place]
            for stage in range(4):
                grads[it, stage, places[stage]] = piece
                count = len(stages[stage])
                for d in range(count):
                    grad_copy(it, stage, d).start()
                for d in range(count):
                    grad_copy(it, stage, d).wait()
                if stage < 3:
                    piece = grads[it, stage, 0]
                    for d in range(count):
                        piece = piece + grads[it, stage, d + 1]
            total = jnp.concatenate([grads[it, 3, j][0:5] for j in range(8)], axis=0)
            mean = jnp.sum(total * total) * (1.0 / (128.0 * 36.0))
            coef[...] = coef[...] - STEP * total / jnp.sqrt(jnp.full(total.shape, mean + EPS, F32))

        transfer(keep=False)
        ratios()
        lefts, _ = adjoint_lanes(cot[0] * (0.25 / NPIX), cot[1] * (0.25 / NPIX), t2.at[3])
        objects[s] = lanes_mul(lefts[0], t1.at[2])
        for part in range(2):
            for way in range(2):
                gather_copy(part, way).start()
        for way in range(2):
            gather_copy(0, way).wait()
            gather_onward(way).start()
        for way in range(2):
            gather_copy(1, way).wait()
        for way in range(2):
            gather_onward(way).wait()

        for d in range(2):
            near_copy(d).wait()
        for d in range(2):
            wanted = near[1 - d]
            total = None
            for p in range(4):
                match = jnp.where(wanted == 4 * t + p, 1.0, 0.0)
                one = jnp.max(match[:1, :], axis=1, keepdims=True) * objects[p]
                total = one if total is None else total + one
            send[d] = total
            object_copy(d).start()
        for d in range(2):
            object_copy(d).wait()
        for j in range(4):
            source = incoming[j]
            total = jnp.where(source // 4 == (t + 31) % 32, arrive[0], arrive[1])
            for p in range(4):
                total = jnp.where(source == 4 * t + p, objects[p], total)
            out[j] = total
        coef_out[...] = coef[0:36, :]

    return kernel


def hand_on(objects, coef, out, coef_out):
    out[...] = objects[...]
    coef_out[...] = coef[...]


def per_device(observed, frame_pick, frame_count, incoming, start_coefficients, mode_basis):
    tables, mask, weight, flip = host_tables()
    vmem = pl.BlockSpec(memory_space=pltpu.VMEM)
    smem = pl.BlockSpec(memory_space=pltpu.SMEM)
    hbm = pl.BlockSpec(memory_space=pl.ANY)
    dma = pltpu.SemaphoreType.DMA
    objects, coef = pl.pallas_call(
        make_kernel(),
        out_shape=(
            jax.ShapeDtypeStruct((4, NPIX, NPIX), F32),
            jax.ShapeDtypeStruct((36, 128), F32),
        ),
        in_specs=[hbm, hbm, smem, smem, vmem, smem, vmem, vmem, vmem] + [hbm] * 6,
        out_specs=(vmem, vmem),
        scratch_shapes=[
            pltpu.VMEM((4, 8, NPIX, NPIX), BF16),
            pltpu.VMEM((2, 4, NPIX, NPIX), BF16),
            pltpu.VMEM((36, XN, NPIX), F32),
            pltpu.VMEM((MROWS * BODD, NPIX), F32),
            pltpu.VMEM((4, 8, 128), jnp.int32),
            pltpu.VMEM((4, 8, 128), jnp.int32),
            pltpu.VMEM((FR, 128), F32),
            pltpu.VMEM((8, 256), F32),
            pltpu.VMEM((MROWS, 128), F32),
            pltpu.VMEM((8, 128), jnp.int32),
            pltpu.VMEM((4, 256, 256), BF16),
            pltpu.VMEM((4, 128, 384), BF16),
            pltpu.VMEM((128, 224), BF16),
            pltpu.VMEM((80, 384), BF16),
            pltpu.VMEM((384, 256), BF16),
            pltpu.VMEM((256, 256), BF16),
            pltpu.VMEM((QUADS, 256, 256), F32),
            pltpu.VMEM((TILES, 256, 256), BF16),
            pltpu.VMEM((FR, 256), BF16),
            pltpu.VMEM((40 * ODD, 128), F32),
            pltpu.VMEM((40 * ODD, 128), F32),
            pltpu.VMEM((FR, XN, 128), F32),
            pltpu.VMEM((2 * QUADS, 256, 256), F32),
            pltpu.VMEM((QUADS, 256, 256), F32),
            pltpu.VMEM((3, 128, 128), F32),
            pltpu.VMEM((ITERS, 8, 8, 128), F32),
            pltpu.VMEM((ITERS, 4, 8, 8, 128), F32),
            pltpu.VMEM((4, 128, 128), F32),
            pltpu.VMEM((2, 8, 128), jnp.int32),
            pltpu.VMEM((2, 128, 128), F32),
            pltpu.VMEM((2, 128, 128), F32),
            dma((3, 2)),
            dma((3, 2)),
            dma((3,)),
            dma((3,)),
            dma((ITERS, 4, 7)),
            dma((ITERS, 4, 7)),
            dma((3, 2)),
            dma((3, 2)),
            dma((2, 2)),
            dma((2, 2)),
            dma((36,)),
            dma((7,)),
        ],
        compiler_params=pltpu.CompilerParams(
            collective_id=0, has_side_effects=True, vmem_limit_bytes=56 * 1024 * 1024
        ),
        cost_estimate=pl.CostEstimate(flops=30_000_000_000, bytes_accessed=10_000_000, transcendentals=0),
    )(
        observed, mode_basis, frame_pick, frame_count, start_coefficients.T, incoming,
        *[jnp.asarray(one) for one in [mask, weight, flip] + tables],
    )
    restored, coef = pl.pallas_call(
        hand_on,
        out_shape=(jax.ShapeDtypeStruct((4, NPIX, NPIX), F32), jax.ShapeDtypeStruct((36, 128), F32)),
        in_specs=[vmem, vmem],
        out_specs=(vmem, vmem),
        cost_estimate=pl.CostEstimate(flops=500_000, bytes_accessed=700_000, transcendentals=0),
    )(objects, coef)
    return restored, coef.T


def solution(mesh):
    placed = (P("tile", "spare", None, None), P("tile", "spare"), P("tile"), P("tile"), P(), P())
    return jax.shard_map(
        per_device,
        mesh=mesh,
        in_specs=placed,
        out_specs=(P("tile", None, None), P()),
        check_vma=False,
    )
```

```python
import math

import jax
import jax.numpy as jnp
import ml_dtypes
import numpy as np
from jax import lax
from jax.experimental import pallas as pl
from jax.experimental.pallas import tpu as pltpu
from jax.sharding import PartitionSpec as P

MESH = pl.DeviceIdType.MESH
F32 = jnp.float32
BF16 = jnp.bfloat16
NPIX = 128
ITERS = 2
GAMMA = 0.5
STEP = 0.25
EPS = 1e-06
X0, XN = 32, 72
MROWS = 40
FR = 32
ODD = 33
BODD = 73
QUADS = 8
PAIRS = 16
CHUNKS = 4
TILES = 17


def host_tables():
    index = np.arange(NPIX)
    angle = 2.0 * np.pi * (index[:, None] * index[None, :] % NPIX) / NPIX
    c, s = np.cos(angle), np.sin(angle)
    off = index - NPIX // 2
    disc = (off[:, None] ** 2 + off[None, :] ** 2 <= (NPIX // 4) ** 2).astype(np.float32)
    area = float(disc.sum())

    def two(table):
        high = table.astype(ml_dtypes.bfloat16)
        return high, (table - high.astype(np.float64)).astype(ml_dtypes.bfloat16)

    def wide(table, extra=0):
        high, low = two(table)
        return np.concatenate([high, high, low, np.zeros((len(table), extra), high.dtype)], axis=1)

    def tall(table):
        high, low = two(table)
        return np.concatenate([high, high, low], axis=0)

    def beside(table):
        return np.concatenate(two(table), axis=1)

    w1 = np.block([[c[32:96], -s[32:96]], [s[32:96], c[32:96]]]) / (NPIX * math.sqrt(area))
    w1t = np.concatenate([w1[64:].T, -w1[:64].T], axis=1)
    rows = np.concatenate([c[:64], c[64:65], s[1:64]], axis=0)
    order = np.concatenate([np.arange(65), 128 - np.arange(1, 64)])
    pupil = X0 + np.arange(XN)
    pupil[65] = NPIX // 2
    a2 = rows[:, pupil]
    a2t = np.concatenate([a2.T, np.zeros((8, NPIX))], axis=0)
    t2 = rows[:, order]
    cosine, sine = c[:, :64], -s[:, :64].copy()
    sine[:, 0] = c[:, 64]
    left, right = np.concatenate([cosine, sine], axis=1), np.concatenate([sine, cosine], axis=1)

    def twice(table):
        one = beside(table)
        return np.concatenate([one, one], axis=0)

    tables = [
        np.stack([twice(left), twice(right), twice(2.0 * left.T), twice(2.0 * right.T)]),
        np.stack([wide(t2), wide(t2.T), wide(rows), wide(rows.T)]),
        wide(a2, 8),
        wide(a2t),
        tall(w1),
        beside(w1t),
    ]
    mask = np.zeros((XN, 64), np.float32)
    mask[:65] = disc[X0 : X0 + 65, 32:96]
    mask[65, 0] = disc[64, 96]
    mask = np.concatenate([mask, mask], axis=1)
    weight = np.full((NPIX, NPIX), 4.0, np.float32)
    weight[:, 0] = 2.0
    weight[:, 64] = 2.0
    weight[64, 1] = 2.0
    weight[64, 65] = 2.0
    flip = np.ones((8, 256), np.float32)
    flip[1, 1::2] = -1.0
    return tables, mask, weight, flip


def split(x):
    high = x.astype(BF16)
    return high, (x - high.astype(F32)).astype(BF16)


def split3(x):
    high = x.astype(BF16).astype(F32)
    rest = x - high
    mid = rest.astype(BF16).astype(F32)
    return high, mid, rest - mid


def mm(a, b):
    return jnp.dot(a, b, preferred_element_type=F32)


def mm_nt(a, b):
    return lax.dot_general(a, b, (((1,), (1,)), ((), ())), preferred_element_type=F32)


def right_mul(x, table):
    high, low = split(x)
    return mm(jnp.concatenate([high, low, high], axis=1), table[...])


def left_mul(table, x):
    high, low = split(x)
    return mm(table[...], jnp.concatenate([high, low, high], axis=0))


def left_pupil(table, x):
    high = x.astype(BF16).astype(F32)
    zero = jnp.zeros((8, x.shape[1]), F32)
    return mm(table[...], jnp.concatenate([high, x - high, high, zero], axis=0).astype(BF16))


def lanes_mul(x, table):
    both = mm(jnp.concatenate(split(x), axis=1), table[...])
    return both[:, :128] + both[:, 128:]


def row0(v, first):
    here = lax.broadcasted_iota(jnp.int32, (8, v.shape[1]), 0) == 0
    return jnp.concatenate([jnp.where(here, first, v[:8]), v[8:]], axis=0)


def unfold(real, imag):
    cr, sr, ci, si = real[:64], real[64:], imag[:64], imag[64:]
    sr0, si0 = row0(sr, 0.0), row0(si, 0.0)
    return (
        jnp.concatenate([cr + si0, row0(cr - si0, sr[:8])], axis=0),
        jnp.concatenate([ci - sr0, row0(ci + sr0, si[:8])], axis=0),
    )


def fold(gr, gi):
    ga, gb, ha, hb = gr[:64], gr[64:], gi[:64], gi[64:]
    return (
        jnp.concatenate([row0(ga + gb, ga[:8]), row0(hb - ha, gb[:8])], axis=0),
        jnp.concatenate([row0(ha + hb, ha[:8]), row0(ga - gb, hb[:8])], axis=0),
    )


COS_POLY = (0.9999999889, -19.7392044666, 64.9391159283, -85.4501134275, 60.1674297919, -25.9668846126, 6.5277059630)


def horner(poly, z):
    total = poly[-1]
    for one in poly[-2::-1]:
        total = total * z + one
    return total


def unit_field(turns, mask):
    r = turns - jnp.floor(turns + 0.5)
    return mask * horner(COS_POLY, r * r)


def lane_mask(width, first):
    lane = lax.broadcasted_iota(jnp.int32, (8, width), 1)
    return (lane % 64) == first


def rows64(arr, fix):
    return jnp.concatenate([arr[:64], fix(arr[64:72]), arr[72:]], axis=0)


def left_half():
    return lax.broadcasted_iota(jnp.int32, (8, 128), 1)[:1] < 64


def half_spectra(lefts, rights, t2):
    low, at0 = left_half(), lane_mask(128, 0)[:1]
    lone, real, imag = [], [], []
    for one, two in zip(lefts, rights):
        di = pltpu.roll(jnp.where(low, two, one), 64, 1)
        total = jnp.sum(di, axis=0, keepdims=True)
        lone.append(pltpu.roll(jnp.broadcast_to(total, (8, 128)), 1, 1))
        real.append(jnp.where(low, one, two))
        imag.append(jnp.where(at0, 0.0, di))
    tr, ti = unfold(left_mul(t2, jnp.concatenate(real, axis=1)), left_mul(t2, jnp.concatenate(imag, axis=1)))
    here = lane_mask(256, 1) & (lax.broadcasted_iota(jnp.int32, (8, 256), 0) == 0)
    lone = jnp.concatenate(lone, axis=1)
    return rows64(tr, lambda v: jnp.where(here, lone, v)), rows64(ti, lambda v: jnp.where(here, 0.0, v))


def adjoint_lanes(gr, gi, t2t):
    width = gr.shape[1]
    here = lane_mask(width, 1) & (lax.broadcasted_iota(jnp.int32, (8, width), 0) == 0)
    lone = jnp.where(here, gr[64:72], 0.0)
    xr, xi = fold(
        rows64(gr, lambda v: jnp.where(here, 0.0, v)), rows64(gi, lambda v: jnp.where(here, 0.0, v))
    )
    dr, di = left_mul(t2t, xr), left_mul(t2t, xi)
    low, at0 = left_half(), lane_mask(128, 0)[:1]
    lefts, rights = [], []
    for i in range(width // 128):
        cols = slice(128 * i, 128 * i + 128)
        back = pltpu.roll(lone[:, cols], 127, 1)[:1]
        turned = pltpu.roll(jnp.where(at0, back, di[:, cols]), 64, 1)
        lefts.append(jnp.where(low, dr[:, cols], turned))
        rights.append(jnp.where(low, turned, dr[:, cols]))
    return lefts, rights


def rows_of(x, n):
    return x[128 * n : 128 * n + 128]


def staggered(*stages):
    for step in range(CHUNKS + len(stages) - 1):
        for k, stage in enumerate(stages):
            if 0 <= step - k < CHUNKS:
                stage(step - k)


def make_kernel():
    def prep_spectra(sources, observed, t1, t2, spec):
        lanes = []
        for source in sources:
            sides = []
            for half in range(2):
                both = [mm(observed[source, 2 * i + half], t1[half, 0:128, :]) for i in range(4)]
                sides.append([(one[:, :128] + one[:, 128:]) * (1.0 / NPIX) for one in both])
            lanes.append(sides)
        for source, sides in zip(sources, lanes):
            for j in range(2):
                real, imag = half_spectra(sides[0][2 * j : 2 * j + 2], sides[1][2 * j : 2 * j + 2], t2)
                spec[2 * source + j, :128, :] = real
                spec[2 * source + j, 128:, :] = imag

    def prep_basis(i, basis, basis6, last=False):
        lane = lax.broadcasted_iota(jnp.int32, (MROWS, 128), 1)
        halves = []
        for j in range(2):
            if last:
                rows = pltpu.roll(basis[pl.ds(64 - 32 * j, MROWS, stride=BODD), :], 96 - 64 * j, 1)
            else:
                one = pltpu.roll(basis[pl.ds(2 * i + j, MROWS, stride=BODD), :], 96, 1)
                other = pltpu.roll(basis[pl.ds(2 * i + j + 32, MROWS, stride=BODD), :], 32, 1)
                rows = jnp.where(lane < 64, one, other)
            high, mid, low = split3(rows)
            halves.append(
                jnp.concatenate([high, mid, high, low, mid, high, jnp.zeros((16, NPIX), F32)], axis=0)
            )
        basis6[i] = jnp.concatenate(halves, axis=1).astype(BF16)

    def coef_six(coef, onehot):
        high, mid, low = split3(coef[...] * (0.5 / math.pi))
        stack = jnp.concatenate([high, high, mid, high, mid, low, jnp.zeros((16, NPIX), F32)], axis=0)
        return mm_nt(onehot[...].astype(BF16), stack.astype(BF16)).astype(BF16)

    def phases(six, basis6, phi):
        for i in range(TILES):
            both = mm(six[...], basis6[i])
            phi[pl.ds(2 * i * ODD, FR), :] = both[:, :128]
            phi[pl.ds((2 * i + 1) * ODD, FR), :] = both[:, 128:]

    def frame_field(f, phi, mask):
        lane = lax.broadcasted_iota(jnp.int32, (8, 128), 1)[:1]
        packed = phi[pl.ds(f, 40, stride=ODD), :]
        turned = pltpu.roll(packed, 64, 1)
        phase = jnp.concatenate(
            [jnp.where(lane < 64, packed, turned), jnp.where(lane < 64, turned[:32], packed[:32])], axis=0
        )
        phase = jnp.concatenate([phase[:32], phase[40:], phase[32:40]], axis=0)
        return unit_field(phase - jnp.where(lane < 64, 0.0, 0.25), mask[...])

    def modes(dphi, basis6):
        total = None
        for i in range(TILES):
            a = dphi[pl.ds(2 * i * ODD, FR), :]
            b = dphi[pl.ds((2 * i + 1) * ODD, FR), :]
            high, low = split(jnp.concatenate([a, b], axis=1))
            part = mm_nt(basis6[i, 0 : 2 * MROWS, :], jnp.concatenate([high, low], axis=0))
            total = part if total is None else total + part
        return total

    def forward(phi, mask, flip, w1, a2, t1, t2, field, amp, trans, keep):
        first, second, third = {}, {}, {}

        def along_y(c):
            stack = []
            for f in range(8 * c, 8 * c + 8):
                one = frame_field(f, phi, mask)
                if keep:
                    field[f] = one
                stack.append(one)
            first[c] = right_mul(jnp.concatenate(stack, axis=0), w1)

        def along_x(c):
            b, spreads = first.pop(c), [[], []]
            for i in range(4):
                parts = []
                for half in range(2):
                    one = b[XN * (2 * i + half) : XN * (2 * i + half + 1)]
                    parts.append(jnp.concatenate([one[:64], one[64:] * flip[...]], axis=0))
                ar, ai = unfold(
                    left_pupil(a2, jnp.concatenate([parts[0][:, :128], parts[1][:, :128]], axis=1)),
                    left_pupil(a2, jnp.concatenate([parts[0][:, 128:], parts[1][:, 128:]], axis=1)),
                )
                if keep:
                    amp[4 * c + i, :128, :] = ar
                    amp[4 * c + i, 128:, :] = ai
                spread = ar * ar + ai * ai
                for half in range(2):
                    spreads[half].append(spread[:, 128 * half : 128 * half + 128])
            second[c] = spreads

        def lanes(c):
            spreads = second.pop(c)
            third[c] = [lanes_mul(jnp.concatenate(spreads[half], axis=0), t1.at[half]) for half in range(2)]

        def rows(c):
            d = third.pop(c)
            for g in range(2):
                tr, ti = half_spectra(*[[rows_of(d[half], 2 * g), rows_of(d[half], 2 * g + 1)] for half in range(2)], t2)
                trans[2 * c + g, :128, :] = tr
                trans[2 * c + g, 128:, :] = ti

        staggered(along_y, along_x, lanes, rows)

    def products(r, trans, spec, used, weight, cot):
        nr = ni = de = None
        upper, lower = pl.ds(pl.multiple_of(16 * r, 16), 16), pl.ds(pl.multiple_of(128 + 16 * r, 16), 16)
        for g in range(QUADS):
            u = used[g : g + 1, :]
            tr, ti, sr, si = trans[g, upper, :], trans[g, lower, :], spec[g, upper, :], spec[g, lower, :]
            vr, vi = tr * u, ti * u
            one = (sr * vr + si * vi, si * vr - sr * vi, tr * vr + ti * vi)
            nr, ni, de = one if g == 0 else (nr + one[0], ni + one[1], de + one[2])
        total = []
        for v in (nr, ni, de):
            v = v[:, :128] + v[:, 128:]
            total.append(v + pltpu.roll(v, 64, 1))
        scale = 1.0 / (GAMMA + total[2])
        qr, qi = total[0] * scale, total[1] * scale
        w = weight[upper, :]
        cot[0, upper, :] = w * qr
        cot[1, upper, :] = w * qi
        cot[2, upper, :] = w * (qr * qr + qi * qi)

    def backward(cot, spec, trans, used, flip, t2t, t1, a2t, w1t, amp, field, dphi):
        qr, qi, qq = [jnp.concatenate([cot[n], cot[n]], axis=1) for n in range(3)]
        lane = lax.broadcasted_iota(jnp.int32, (8, 128), 1)[:1]
        first, second, third = {}, {}, {}

        def rows(c):
            sides = [[], []]
            for g in (2 * c, 2 * c + 1):
                u = used[g : g + 1, :]
                tr, ti = trans[g, :128, :], trans[g, 128:, :]
                sr, si = spec[g, :128, :], spec[g, 128:, :]
                gr = u * (qq * tr - qr * sr - qi * si)
                gi = u * (qi * sr - qr * si + qq * ti)
                for half, one in enumerate(adjoint_lanes(gr, gi, t2t)):
                    sides[half] += one
            first[c] = sides

        def lanes(c):
            sides = first.pop(c)
            second[c] = [lanes_mul(jnp.concatenate(sides[half], axis=0), t1.at[2 + half]) for half in range(2)]

        def along_x(c):
            ds, stack = second.pop(c), []
            for i in range(4):
                one = jnp.concatenate([rows_of(ds[0], i), rows_of(ds[1], i)], axis=1)
                xr, xi = fold(amp[4 * c + i, :128, :] * one, amp[4 * c + i, 128:, :] * one)
                dbr, dbi = left_mul(a2t, xr), left_mul(a2t, xi)
                for half in range(2):
                    cols = slice(128 * half, 128 * half + 128)
                    one = jnp.concatenate([dbr[:XN, cols], dbi[:XN, cols]], axis=1)
                    stack += [one[:64], one[64:] * flip[...]]
            third[c] = stack

        def along_y(c):
            x = jnp.concatenate(third.pop(c), axis=0)
            n = x.shape[0]
            both = mm(jnp.concatenate(split(x), axis=0), w1t[...])
            d = both[:n, :128] + both[:n, 128:] + both[n:, :128] + both[n:, 128:]
            for place in range(8):
                f = 8 * c + place
                v = field[f] * d[XN * place : XN * place + XN]
                v = v + pltpu.roll(v, 64, 1)
                dphi[pl.ds(f, 40, stride=ODD), :] = jnp.concatenate(
                    [jnp.where(lane < 64, v[:32], v[32:64]), jnp.where(lane < 64, v[64:], 0.0)], axis=0
                )

        staggered(rows, lanes, along_x, along_y)

    def kernel(
        observed_h, basis_h, pick, count, coef0, incoming, mask, weight, flip,
        t1_h, t2_h, a2_h, a2t_h, w1_h, w1t_h,
        out, coef_out,
        observed, relay, window, basis, picks, picked, onehot, used, coef, own, t1, t2, a2, a2t, w1, w1t,
        spec, basis6, six, phi, dphi, field, amp, trans, cot, grads, objects, near, send, arrive,
        ob_send, ob_recv, pk_send, pk_recv, gr_send, gr_recv, ag_send, ag_recv, nb_send, nb_recv, basis_sem, load_sem,
    ):
        t, s = lax.axis_index("tile"), lax.axis_index("spare")
        tx, tz, tc = t // 8, (t // 2) % 4, t % 2
        spare_of = [(s + d) % 4 for d in (1, 2, 3)]
        groups = [
            [(t, v) for v in spare_of] + [(t + 1 - 2 * tc, (s + d) % 4) for d in range(4)],
            [(((tx + d) % 4) * 8 + tz * 2 + tc, s) for d in (1, 2, 3)],
            [(tx * 8 + ((tz + d) % 4) * 2 + tc, s) for d in (1, 2, 3)],
        ]
        places = [tc * 4 + s, tx, tz]
        beside = [((t + 1) % 32, s), ((t + 31) % 32, s)]

        barrier = pltpu.get_barrier_semaphore()
        partners = [who for group in groups for who in group] + beside
        for who in partners:
            pl.semaphore_signal(barrier, inc=1, device_id=who, device_id_type=MESH)

        loads = [
            pltpu.make_async_copy(src, dst, load_sem.at[n])
            for n, (src, dst) in enumerate(
                [(observed_h.at[s], observed.at[s]), (t1_h, t1), (t2_h, t2), (a2_h, a2), (a2t_h, a2t), (w1_h, w1), (w1t_h, w1t)]
            )
        ]
        windows = [
            pltpu.make_async_copy(
                basis_h.at[m, pl.ds(X0, XN), :], window.at[m], basis_sem.at[m]
            )
            for m in range(36)
        ]
        for one in windows + loads:
            one.start()

        def remote(src, dst, ssem, rsem, who):
            return pltpu.make_async_remote_copy(
                src_ref=src, dst_ref=dst, send_sem=ssem, recv_sem=rsem, device_id=who, device_id_type=MESH
            )

        def near_copy(d):
            return remote(own, near.at[d], nb_send.at[0, d], nb_recv.at[0, d], beside[d])

        def object_copy(d):
            return remote(send.at[d], arrive.at[d], nb_send.at[1, d], nb_recv.at[1, d], beside[d])

        ways = [(s + 1) % 4, (s + 3) % 4]
        across = (s + 2) % 4

        def frames_copy(way):
            return remote(
                observed_h.at[ways[way]], observed.at[s], ob_send.at[0, way], ob_recv.at[0, way], (t, ways[way])
            )

        def relay_copy(way):
            return remote(
                observed_h.at[across, pl.ds(4 * way, 4)], relay.at[way], ob_send.at[1, way], ob_recv.at[1, way], (t, ways[way])
            )

        def onward_copy(way):
            return remote(
                relay.at[way], observed.at[ways[1 - way], pl.ds(4 * way, 4)], ob_send.at[2, way], ob_recv.at[2, way],
                (t, ways[way]),
            )

        def picks_copy(d):
            return remote(picks.at[spare_of[d]], picked.at[s], pk_send.at[d], pk_recv.at[d], groups[0][d])

        def gather_copy(d):
            return remote(objects.at[s], objects.at[s], ag_send.at[d], ag_recv.at[d], groups[0][d])

        def grad_copy(it, stage, d):
            here = grads.at[it, stage, places[stage]]
            return remote(here, here, gr_send.at[it, stage, d], gr_recv.at[it, stage, d], groups[stage][d])

        lane = lax.broadcasted_iota(jnp.int32, (8, 128), 1)
        row = lax.broadcasted_iota(jnp.int32, (8, 128), 0)
        wanted = jnp.full((8, 128), -1, jnp.int32)
        for j in range(4):
            wanted = jnp.where(lane == j, incoming[j], wanted)
        own[...] = wanted
        for p in range(4):
            spread = jnp.full((8, 128), pick[p, 0], jnp.int32)
            for k in range(1, 8):
                spread = jnp.where(row == k, pick[p, k], spread)
            picks[p] = spread
        picked[s] = picks[s]
        pl.semaphore_wait(barrier, len(partners))
        for d in range(3):
            picks_copy(d).start()
        for way in range(2):
            relay_copy(way).start()
        for way in range(2):
            frames_copy(way).start()
        for d in range(2):
            near_copy(d).start()

        lane2 = lax.broadcasted_iota(jnp.int32, (8, 256), 1)
        row2 = lax.broadcasted_iota(jnp.int32, (8, 256), 0)
        used[...] = jnp.where(4 * (4 * (row2 % 2) + lane2 // 64) + row2 // 2 < count[s], 1.0, 0.0)
        coef[...] = jnp.zeros_like(coef)
        coef[0:36, :] = coef0[...]
        basis[pl.ds(36 * BODD, 4 * BODD), :] = jnp.zeros((4 * BODD, NPIX), F32)
        phi[...] = jnp.zeros_like(phi)
        for m in range(36):
            windows[m].wait()
            basis[pl.ds(m * BODD, XN), :] = window[m]
        for i in range(TILES):
            prep_basis(i, basis, basis6, last=i == TILES - 1)
        for d in range(3):
            picks_copy(d).wait()
        for a in range(4):
            onehot[8 * a : 8 * a + 8, :] = jnp.where(picked[a] == lane, 1.0, 0.0)
        for one in loads:
            one.wait()

        def transfer(keep, between=None):
            six[...] = coef_six(coef, onehot)
            phases(six, basis6, phi)
            if between is not None:
                between()
            forward(phi, mask, flip, w1, a2, t1, t2.at[0], field, amp, trans, keep)

        def ratios():
            pl.loop(0, 8, unroll=2)(lambda r: products(r, trans, spec, used, weight, cot))

        @pl.loop(0, ITERS)
        def iteration(it):
            def pass_on():
                @pl.when(it == 0)
                def _():
                    for way in range(2):
                        relay_copy(way).wait()
                        onward_copy(way).start()

            transfer(keep=True, between=pass_on)

            @pl.when(it == 0)
            def _():
                for way in range(2):
                    frames_copy(way).wait()
                prep_spectra([s] + ways, observed, t1, t2.at[2], spec)
                for way in range(2):
                    onward_copy(way).wait()
                prep_spectra([across], observed, t1, t2.at[2], spec)

            ratios()
            backward(cot, spec, trans, used, flip, t2.at[1], t1, a2t, w1t, amp, field, dphi)
            acc = modes(dphi, basis6)
            slot_grad = acc[:MROWS] + acc[MROWS:]
            twice = jnp.concatenate([onehot[...], onehot[...]], axis=0).astype(BF16)
            total = None
            for part in split3(slot_grad):
                one = mm(part.astype(BF16), twice)
                total = one if total is None else total + one
            for stage in range(3):
                grads[it, stage, places[stage]] = total
                count = len(groups[stage])
                for d in range(count):
                    grad_copy(it, stage, d).start()
                for d in range(count):
                    grad_copy(it, stage, d).wait()
                total = grads[it, stage, 0]
                for d in range(count):
                    total = total + grads[it, stage, d + 1]
            mean = jnp.sum(total * total) * (1.0 / (128.0 * 36.0))
            coef[...] = coef[...] - STEP * total / jnp.sqrt(jnp.full(total.shape, mean + EPS, F32))

        transfer(keep=False)
        ratios()
        lefts, _ = adjoint_lanes(cot[0] * (0.25 / NPIX), cot[1] * (0.25 / NPIX), t2.at[3])
        objects[s] = lanes_mul(lefts[0], t1.at[2])
        for d in range(3):
            gather_copy(d).start()
        for d in range(3):
            gather_copy(d).wait()

        for d in range(2):
            near_copy(d).wait()
        for d in range(2):
            wanted = near[1 - d]
            total = None
            for p in range(4):
                match = jnp.where(wanted == 4 * t + p, 1.0, 0.0)
                one = jnp.max(match[:1, :], axis=1, keepdims=True) * objects[p]
                total = one if total is None else total + one
            send[d] = total
            object_copy(d).start()
        for d in range(2):
            object_copy(d).wait()
        for j in range(4):
            source = incoming[j]
            total = jnp.where(source // 4 == (t + 31) % 32, arrive[0], arrive[1])
            for p in range(4):
                total = jnp.where(source == 4 * t + p, objects[p], total)
            out[j] = total
        coef_out[...] = coef[0:36, :]

    return kernel


def hand_on(objects, coef, out, coef_out):
    out[...] = objects[...]
    coef_out[...] = coef[...]


def per_device(observed, frame_pick, frame_count, incoming, start_coefficients, mode_basis):
    tables, mask, weight, flip = host_tables()
    vmem = pl.BlockSpec(memory_space=pltpu.VMEM)
    smem = pl.BlockSpec(memory_space=pltpu.SMEM)
    hbm = pl.BlockSpec(memory_space=pl.ANY)
    dma = pltpu.SemaphoreType.DMA
    objects, coef = pl.pallas_call(
        make_kernel(),
        out_shape=(
            jax.ShapeDtypeStruct((4, NPIX, NPIX), F32),
            jax.ShapeDtypeStruct((36, 128), F32),
        ),
        in_specs=[hbm, hbm, smem, smem, vmem, smem, vmem, vmem, vmem] + [hbm] * 6,
        out_specs=(vmem, vmem),
        scratch_shapes=[
            pltpu.VMEM((4, 8, NPIX, NPIX), BF16),
            pltpu.VMEM((2, 4, NPIX, NPIX), BF16),
            pltpu.VMEM((36, XN, NPIX), F32),
            pltpu.VMEM((MROWS * BODD, NPIX), F32),
            pltpu.VMEM((4, 8, 128), jnp.int32),
            pltpu.VMEM((4, 8, 128), jnp.int32),
            pltpu.VMEM((FR, 128), F32),
            pltpu.VMEM((8, 256), F32),
            pltpu.VMEM((MROWS, 128), F32),
            pltpu.VMEM((8, 128), jnp.int32),
            pltpu.VMEM((4, 256, 256), BF16),
            pltpu.VMEM((4, 128, 384), BF16),
            pltpu.VMEM((128, 224), BF16),
            pltpu.VMEM((80, 384), BF16),
            pltpu.VMEM((384, 256), BF16),
            pltpu.VMEM((256, 256), BF16),
            pltpu.VMEM((QUADS, 256, 256), F32),
            pltpu.VMEM((TILES, 256, 256), BF16),
            pltpu.VMEM((FR, 256), BF16),
            pltpu.VMEM((40 * ODD, 128), F32),
            pltpu.VMEM((40 * ODD, 128), F32),
            pltpu.VMEM((FR, XN, 128), F32),
            pltpu.VMEM((2 * QUADS, 256, 256), F32),
            pltpu.VMEM((QUADS, 256, 256), F32),
            pltpu.VMEM((3, 128, 128), F32),
            pltpu.VMEM((ITERS, 3, 8, MROWS, 128), F32),
            pltpu.VMEM((4, 128, 128), F32),
            pltpu.VMEM((2, 8, 128), jnp.int32),
            pltpu.VMEM((2, 128, 128), F32),
            pltpu.VMEM((2, 128, 128), F32),
            dma((3, 2)),
            dma((3, 2)),
            dma((3,)),
            dma((3,)),
            dma((ITERS, 3, 7)),
            dma((ITERS, 3, 7)),
            dma((3,)),
            dma((3,)),
            dma((2, 2)),
            dma((2, 2)),
            dma((36,)),
            dma((7,)),
        ],
        compiler_params=pltpu.CompilerParams(
            collective_id=0, has_side_effects=True, vmem_limit_bytes=56 * 1024 * 1024
        ),
        cost_estimate=pl.CostEstimate(flops=30_000_000_000, bytes_accessed=10_000_000, transcendentals=0),
    )(
        observed, mode_basis, frame_pick, frame_count, start_coefficients.T, incoming,
        *[jnp.asarray(one) for one in [mask, weight, flip] + tables],
    )
    restored, coef = pl.pallas_call(
        hand_on,
        out_shape=(jax.ShapeDtypeStruct((4, NPIX, NPIX), F32), jax.ShapeDtypeStruct((36, 128), F32)),
        in_specs=[vmem, vmem],
        out_specs=(vmem, vmem),
        cost_estimate=pl.CostEstimate(flops=500_000, bytes_accessed=700_000, transcendentals=0),
    )(objects, coef)
    return restored, coef.T


def solution(mesh):
    placed = (P("tile", "spare", None, None), P("tile", "spare"), P("tile"), P("tile"), P(), P())
    return jax.shard_map(
        per_device,
        mesh=mesh,
        in_specs=placed,
        out_specs=(P("tile", None, None), P()),
        check_vma=False,
    )
```

```python
import math

import jax
import jax.numpy as jnp
import ml_dtypes
import numpy as np
from jax import lax
from jax.experimental import pallas as pl
from jax.experimental.pallas import tpu as pltpu
from jax.sharding import PartitionSpec as P

MESH = pl.DeviceIdType.MESH
F32 = jnp.float32
BF16 = jnp.bfloat16
NPIX = 128
ITERS = 2
GAMMA = 0.5
STEP = 0.25
EPS = 1e-06
X0, XN = 32, 72
MROWS = 40
FR = 32
ODD = 33
BODD = 73
QUADS = 8
PAIRS = 16
CHUNKS = 4
TILES = 17


def host_tables():
    index = np.arange(NPIX)
    angle = 2.0 * np.pi * (index[:, None] * index[None, :] % NPIX) / NPIX
    c, s = np.cos(angle), np.sin(angle)
    off = index - NPIX // 2
    disc = (off[:, None] ** 2 + off[None, :] ** 2 <= (NPIX // 4) ** 2).astype(np.float32)
    area = float(disc.sum())

    def two(table):
        high = table.astype(ml_dtypes.bfloat16)
        return high, (table - high.astype(np.float64)).astype(ml_dtypes.bfloat16)

    def wide(table, extra=0):
        high, low = two(table)
        return np.concatenate([high, high, low, np.zeros((len(table), extra), high.dtype)], axis=1)

    def tall(table):
        high, low = two(table)
        return np.concatenate([high, high, low], axis=0)

    def beside(table):
        return np.concatenate(two(table), axis=1)

    w1 = np.block([[c[32:96], -s[32:96]], [s[32:96], c[32:96]]]) / (NPIX * math.sqrt(area))
    w1t = np.concatenate([w1[64:].T, -w1[:64].T], axis=1)
    rows = np.concatenate([c[:64], c[64:65], s[1:64]], axis=0)
    order = np.concatenate([np.arange(65), 128 - np.arange(1, 64)])
    pupil = X0 + np.arange(XN)
    pupil[65] = NPIX // 2
    a2 = rows[:, pupil]
    a2t = np.concatenate([a2.T, np.zeros((8, NPIX))], axis=0)
    t2 = rows[:, order]
    cosine, sine = c[:, :64], -s[:, :64].copy()
    sine[:, 0] = c[:, 64]
    left, right = np.concatenate([cosine, sine], axis=1), np.concatenate([sine, cosine], axis=1)

    def twice(table):
        one = beside(table)
        return np.concatenate([one, one], axis=0)

    tables = [
        np.stack([twice(left), twice(right), twice(2.0 * left.T), twice(2.0 * right.T)]),
        np.stack([wide(t2), wide(t2.T), wide(rows), wide(rows.T)]),
        wide(a2, 8),
        wide(a2t),
        tall(w1),
        beside(w1t),
    ]
    mask = np.zeros((XN, 64), np.float32)
    mask[:65] = disc[X0 : X0 + 65, 32:96]
    mask[65, 0] = disc[64, 96]
    mask = np.concatenate([mask, mask], axis=1)
    weight = np.full((NPIX, NPIX), 4.0, np.float32)
    weight[:, 0] = 2.0
    weight[:, 64] = 2.0
    weight[64, 1] = 2.0
    weight[64, 65] = 2.0
    flip = np.ones((8, 256), np.float32)
    flip[1, 1::2] = -1.0
    return tables, mask, weight, flip


def split(x):
    high = x.astype(BF16)
    return high, (x - high.astype(F32)).astype(BF16)


def split3(x):
    high = x.astype(BF16).astype(F32)
    rest = x - high
    mid = rest.astype(BF16).astype(F32)
    return high, mid, rest - mid


def mm(a, b):
    return jnp.dot(a, b, preferred_element_type=F32)


def mm_nt(a, b):
    return lax.dot_general(a, b, (((1,), (1,)), ((), ())), preferred_element_type=F32)


def right_mul(x, table):
    high, low = split(x)
    return mm(jnp.concatenate([high, low, high], axis=1), table[...])


def left_mul(table, x):
    high, low = split(x)
    return mm(table[...], jnp.concatenate([high, low, high], axis=0))


def left_pupil(table, x):
    high = x.astype(BF16).astype(F32)
    zero = jnp.zeros((8, x.shape[1]), F32)
    return mm(table[...], jnp.concatenate([high, x - high, high, zero], axis=0).astype(BF16))


def lanes_mul(x, table):
    both = mm(jnp.concatenate(split(x), axis=1), table[...])
    return both[:, :128] + both[:, 128:]


def row0(v, first):
    here = lax.broadcasted_iota(jnp.int32, (8, v.shape[1]), 0) == 0
    return jnp.concatenate([jnp.where(here, first, v[:8]), v[8:]], axis=0)


def unfold(real, imag):
    cr, sr, ci, si = real[:64], real[64:], imag[:64], imag[64:]
    sr0, si0 = row0(sr, 0.0), row0(si, 0.0)
    return (
        jnp.concatenate([cr + si0, row0(cr - si0, sr[:8])], axis=0),
        jnp.concatenate([ci - sr0, row0(ci + sr0, si[:8])], axis=0),
    )


def fold(gr, gi):
    ga, gb, ha, hb = gr[:64], gr[64:], gi[:64], gi[64:]
    return (
        jnp.concatenate([row0(ga + gb, ga[:8]), row0(hb - ha, gb[:8])], axis=0),
        jnp.concatenate([row0(ha + hb, ha[:8]), row0(ga - gb, hb[:8])], axis=0),
    )


COS_POLY = (0.9999999889, -19.7392044666, 64.9391159283, -85.4501134275, 60.1674297919, -25.9668846126, 6.5277059630)


def horner(poly, z):
    total = poly[-1]
    for one in poly[-2::-1]:
        total = total * z + one
    return total


def unit_field(turns, mask):
    r = turns - jnp.floor(turns + 0.5)
    return mask * horner(COS_POLY, r * r)


def lane_mask(width, first):
    lane = lax.broadcasted_iota(jnp.int32, (8, width), 1)
    return (lane % 64) == first


def rows64(arr, fix):
    return jnp.concatenate([arr[:64], fix(arr[64:72]), arr[72:]], axis=0)


def left_half():
    return lax.broadcasted_iota(jnp.int32, (8, 128), 1)[:1] < 64


def half_spectra(lefts, rights, t2):
    low, at0 = left_half(), lane_mask(128, 0)[:1]
    lone, real, imag = [], [], []
    for one, two in zip(lefts, rights):
        di = pltpu.roll(jnp.where(low, two, one), 64, 1)
        total = jnp.sum(di, axis=0, keepdims=True)
        lone.append(pltpu.roll(jnp.broadcast_to(total, (8, 128)), 1, 1))
        real.append(jnp.where(low, one, two))
        imag.append(jnp.where(at0, 0.0, di))
    tr, ti = unfold(left_mul(t2, jnp.concatenate(real, axis=1)), left_mul(t2, jnp.concatenate(imag, axis=1)))
    here = lane_mask(256, 1) & (lax.broadcasted_iota(jnp.int32, (8, 256), 0) == 0)
    lone = jnp.concatenate(lone, axis=1)
    return rows64(tr, lambda v: jnp.where(here, lone, v)), rows64(ti, lambda v: jnp.where(here, 0.0, v))


def adjoint_lanes(gr, gi, t2t):
    width = gr.shape[1]
    here = lane_mask(width, 1) & (lax.broadcasted_iota(jnp.int32, (8, width), 0) == 0)
    lone = jnp.where(here, gr[64:72], 0.0)
    xr, xi = fold(
        rows64(gr, lambda v: jnp.where(here, 0.0, v)), rows64(gi, lambda v: jnp.where(here, 0.0, v))
    )
    dr, di = left_mul(t2t, xr), left_mul(t2t, xi)
    low, at0 = left_half(), lane_mask(128, 0)[:1]
    lefts, rights = [], []
    for i in range(width // 128):
        cols = slice(128 * i, 128 * i + 128)
        back = pltpu.roll(lone[:, cols], 127, 1)[:1]
        turned = pltpu.roll(jnp.where(at0, back, di[:, cols]), 64, 1)
        lefts.append(jnp.where(low, dr[:, cols], turned))
        rights.append(jnp.where(low, turned, dr[:, cols]))
    return lefts, rights


def rows_of(x, n):
    return x[128 * n : 128 * n + 128]


def staggered(*stages):
    for step in range(CHUNKS + len(stages) - 1):
        for k, stage in enumerate(stages):
            if 0 <= step - k < CHUNKS:
                stage(step - k)


def make_kernel():
    def prep_spectra(sources, observed, t1, t2, spec):
        lanes = []
        for source in sources:
            sides = []
            for half in range(2):
                both = [mm(observed[source, 2 * i + half], t1[half, 0:128, :]) for i in range(4)]
                sides.append([(one[:, :128] + one[:, 128:]) * (1.0 / NPIX) for one in both])
            lanes.append(sides)
        for source, sides in zip(sources, lanes):
            for j in range(2):
                real, imag = half_spectra(sides[0][2 * j : 2 * j + 2], sides[1][2 * j : 2 * j + 2], t2)
                spec[2 * source + j, :128, :] = real
                spec[2 * source + j, 128:, :] = imag

    def prep_basis(i, basis, basis6, last=False):
        lane = lax.broadcasted_iota(jnp.int32, (MROWS, 128), 1)
        halves = []
        for j in range(2):
            if last:
                rows = pltpu.roll(basis[pl.ds(64 - 32 * j, MROWS, stride=BODD), :], 96 - 64 * j, 1)
            else:
                one = pltpu.roll(basis[pl.ds(2 * i + j, MROWS, stride=BODD), :], 96, 1)
                other = pltpu.roll(basis[pl.ds(2 * i + j + 32, MROWS, stride=BODD), :], 32, 1)
                rows = jnp.where(lane < 64, one, other)
            high, mid, low = split3(rows)
            halves.append(
                jnp.concatenate([high, mid, high, low, mid, high, jnp.zeros((16, NPIX), F32)], axis=0)
            )
        basis6[i] = jnp.concatenate(halves, axis=1).astype(BF16)

    def coef_six(coef, onehot):
        high, mid, low = split3(coef[...] * (0.5 / math.pi))
        stack = jnp.concatenate([high, high, mid, high, mid, low, jnp.zeros((16, NPIX), F32)], axis=0)
        return mm_nt(onehot[...].astype(BF16), stack.astype(BF16)).astype(BF16)

    def phases(six, basis6, phi):
        for i in range(TILES):
            both = mm(six[...], basis6[i])
            phi[pl.ds(2 * i * ODD, FR), :] = both[:, :128]
            phi[pl.ds((2 * i + 1) * ODD, FR), :] = both[:, 128:]

    def frame_field(f, phi, mask):
        lane = lax.broadcasted_iota(jnp.int32, (8, 128), 1)[:1]
        packed = phi[pl.ds(f, 40, stride=ODD), :]
        turned = pltpu.roll(packed, 64, 1)
        phase = jnp.concatenate(
            [jnp.where(lane < 64, packed, turned), jnp.where(lane < 64, turned[:32], packed[:32])], axis=0
        )
        phase = jnp.concatenate([phase[:32], phase[40:], phase[32:40]], axis=0)
        return unit_field(phase - jnp.where(lane < 64, 0.0, 0.25), mask[...])

    def modes(dphi, basis6):
        total = None
        for i in range(TILES):
            a = dphi[pl.ds(2 * i * ODD, FR), :]
            b = dphi[pl.ds((2 * i + 1) * ODD, FR), :]
            high, low = split(jnp.concatenate([a, b], axis=1))
            part = mm_nt(basis6[i, 0 : 2 * MROWS, :], jnp.concatenate([high, low], axis=0))
            total = part if total is None else total + part
        return total

    def forward(phi, mask, flip, w1, a2, t1, t2, field, amp, trans, keep):
        first, second, third = {}, {}, {}

        def along_y(c):
            stack = []
            for f in range(8 * c, 8 * c + 8):
                one = frame_field(f, phi, mask)
                if keep:
                    field[f] = one
                stack.append(one)
            first[c] = right_mul(jnp.concatenate(stack, axis=0), w1)

        def along_x(c):
            b, spreads = first.pop(c), [[], []]
            for i in range(4):
                parts = []
                for half in range(2):
                    one = b[XN * (2 * i + half) : XN * (2 * i + half + 1)]
                    parts.append(jnp.concatenate([one[:64], one[64:] * flip[...]], axis=0))
                ar, ai = unfold(
                    left_pupil(a2, jnp.concatenate([parts[0][:, :128], parts[1][:, :128]], axis=1)),
                    left_pupil(a2, jnp.concatenate([parts[0][:, 128:], parts[1][:, 128:]], axis=1)),
                )
                if keep:
                    amp[4 * c + i, :128, :] = ar
                    amp[4 * c + i, 128:, :] = ai
                spread = ar * ar + ai * ai
                for half in range(2):
                    spreads[half].append(spread[:, 128 * half : 128 * half + 128])
            second[c] = spreads

        def lanes(c):
            spreads = second.pop(c)
            third[c] = [lanes_mul(jnp.concatenate(spreads[half], axis=0), t1.at[half]) for half in range(2)]

        def rows(c):
            d = third.pop(c)
            for g in range(2):
                tr, ti = half_spectra(*[[rows_of(d[half], 2 * g), rows_of(d[half], 2 * g + 1)] for half in range(2)], t2)
                trans[2 * c + g, :128, :] = tr
                trans[2 * c + g, 128:, :] = ti

        staggered(along_y, along_x, lanes, rows)

    def products(r, trans, spec, used, weight, cot):
        nr = ni = de = None
        upper, lower = pl.ds(pl.multiple_of(16 * r, 16), 16), pl.ds(pl.multiple_of(128 + 16 * r, 16), 16)
        for g in range(QUADS):
            u = used[g : g + 1, :]
            tr, ti, sr, si = trans[g, upper, :], trans[g, lower, :], spec[g, upper, :], spec[g, lower, :]
            vr, vi = tr * u, ti * u
            one = (sr * vr + si * vi, si * vr - sr * vi, tr * vr + ti * vi)
            nr, ni, de = one if g == 0 else (nr + one[0], ni + one[1], de + one[2])
        total = []
        for v in (nr, ni, de):
            v = v[:, :128] + v[:, 128:]
            total.append(v + pltpu.roll(v, 64, 1))
        scale = 1.0 / (GAMMA + total[2])
        qr, qi = total[0] * scale, total[1] * scale
        w = weight[upper, :]
        cot[0, upper, :] = w * qr
        cot[1, upper, :] = w * qi
        cot[2, upper, :] = w * (qr * qr + qi * qi)

    def backward(cot, spec, trans, used, flip, t2t, t1, a2t, w1t, amp, field, dphi):
        qr, qi, qq = [jnp.concatenate([cot[n], cot[n]], axis=1) for n in range(3)]
        lane = lax.broadcasted_iota(jnp.int32, (8, 128), 1)[:1]
        first, second, third = {}, {}, {}

        def rows(c):
            sides = [[], []]
            for g in (2 * c, 2 * c + 1):
                u = used[g : g + 1, :]
                tr, ti = trans[g, :128, :], trans[g, 128:, :]
                sr, si = spec[g, :128, :], spec[g, 128:, :]
                gr = u * (qq * tr - qr * sr - qi * si)
                gi = u * (qi * sr - qr * si + qq * ti)
                for half, one in enumerate(adjoint_lanes(gr, gi, t2t)):
                    sides[half] += one
            first[c] = sides

        def lanes(c):
            sides = first.pop(c)
            second[c] = [lanes_mul(jnp.concatenate(sides[half], axis=0), t1.at[2 + half]) for half in range(2)]

        def along_x(c):
            ds, stack = second.pop(c), []
            for i in range(4):
                one = jnp.concatenate([rows_of(ds[0], i), rows_of(ds[1], i)], axis=1)
                xr, xi = fold(amp[4 * c + i, :128, :] * one, amp[4 * c + i, 128:, :] * one)
                dbr, dbi = left_mul(a2t, xr), left_mul(a2t, xi)
                for half in range(2):
                    cols = slice(128 * half, 128 * half + 128)
                    one = jnp.concatenate([dbr[:XN, cols], dbi[:XN, cols]], axis=1)
                    stack += [one[:64], one[64:] * flip[...]]
            third[c] = stack

        def along_y(c):
            x = jnp.concatenate(third.pop(c), axis=0)
            n = x.shape[0]
            both = mm(jnp.concatenate(split(x), axis=0), w1t[...])
            d = both[:n, :128] + both[:n, 128:] + both[n:, :128] + both[n:, 128:]
            for place in range(8):
                f = 8 * c + place
                v = field[f] * d[XN * place : XN * place + XN]
                v = v + pltpu.roll(v, 64, 1)
                dphi[pl.ds(f, 40, stride=ODD), :] = jnp.concatenate(
                    [jnp.where(lane < 64, v[:32], v[32:64]), jnp.where(lane < 64, v[64:], 0.0)], axis=0
                )

        staggered(rows, lanes, along_x, along_y)

    def kernel(
        observed_h, basis_h, pick, count, coef0, incoming, mask, weight, flip,
        t1_h, t2_h, a2_h, a2t_h, w1_h, w1t_h,
        out, coef_out,
        observed, relay, window, basis, picks, picked, onehot, used, coef, own, t1, t2, a2, a2t, w1, w1t,
        spec, basis6, six, phi, dphi, field, amp, trans, cot, halves, grads, objects, near, send, arrive,
        ob_send, ob_recv, pk_send, pk_recv, gr_send, gr_recv, ag_send, ag_recv, nb_send, nb_recv, basis_sem, load_sem,
    ):
        t, s = lax.axis_index("tile"), lax.axis_index("spare")
        tx, tz, tc = t // 8, (t // 2) % 4, t % 2
        spare_of = [(s + d) % 4 for d in (1, 2, 3)]
        groups = [
            [(t, v) for v in spare_of] + [(t + 1 - 2 * tc, (s + d) % 4) for d in range(4)],
            [(((tx + d) % 4) * 8 + tz * 2 + tc, s) for d in (1, 2, 3)],
            [(tx * 8 + ((tz + d) % 4) * 2 + tc, s) for d in (1, 2, 3)]
            + [(tx * 8 + ((tz + d) % 4) * 2 + 1 - tc, s) for d in range(4)],
        ]
        places = [tc * 4 + s, tx, tc * 4 + tz]
        beside = [((t + 1) % 32, s), ((t + 31) % 32, s)]

        barrier = pltpu.get_barrier_semaphore()
        partners = [who for group in groups for who in group] + beside
        for who in partners:
            pl.semaphore_signal(barrier, inc=1, device_id=who, device_id_type=MESH)

        loads = [
            pltpu.make_async_copy(src, dst, load_sem.at[n])
            for n, (src, dst) in enumerate(
                [(observed_h.at[s], observed.at[s]), (t1_h, t1), (t2_h, t2), (a2_h, a2), (a2t_h, a2t), (w1_h, w1), (w1t_h, w1t)]
            )
        ]
        windows = [
            pltpu.make_async_copy(
                basis_h.at[m, pl.ds(X0, XN), :], window.at[m], basis_sem.at[m]
            )
            for m in range(36)
        ]
        for one in windows + loads:
            one.start()

        def remote(src, dst, ssem, rsem, who):
            return pltpu.make_async_remote_copy(
                src_ref=src, dst_ref=dst, send_sem=ssem, recv_sem=rsem, device_id=who, device_id_type=MESH
            )

        def near_copy(d):
            return remote(own, near.at[d], nb_send.at[0, d], nb_recv.at[0, d], beside[d])

        def object_copy(d):
            return remote(send.at[d], arrive.at[d], nb_send.at[1, d], nb_recv.at[1, d], beside[d])

        ways = [(s + 1) % 4, (s + 3) % 4]
        across = (s + 2) % 4

        def frames_copy(way):
            return remote(
                observed_h.at[ways[way]], observed.at[s], ob_send.at[0, way], ob_recv.at[0, way], (t, ways[way])
            )

        def relay_copy(way):
            return remote(
                observed_h.at[across, pl.ds(4 * way, 4)], relay.at[way], ob_send.at[1, way], ob_recv.at[1, way], (t, ways[way])
            )

        def onward_copy(way):
            return remote(
                relay.at[way], observed.at[ways[1 - way], pl.ds(4 * way, 4)], ob_send.at[2, way], ob_recv.at[2, way],
                (t, ways[way]),
            )

        def picks_copy(d):
            return remote(picks.at[spare_of[d]], picked.at[s], pk_send.at[d], pk_recv.at[d], groups[0][d])

        def gather_copy(d):
            return remote(objects.at[s], objects.at[s], ag_send.at[d], ag_recv.at[d], groups[0][d])

        def grad_copy(it, stage, d):
            here = grads.at[it, stage, places[stage]]
            src = halves.at[it, tc if d < 3 else 1 - tc] if stage == 0 else here
            return remote(src, here, gr_send.at[it, stage, d], gr_recv.at[it, stage, d], groups[stage][d])

        lane = lax.broadcasted_iota(jnp.int32, (8, 128), 1)
        row = lax.broadcasted_iota(jnp.int32, (8, 128), 0)
        wanted = jnp.full((8, 128), -1, jnp.int32)
        for j in range(4):
            wanted = jnp.where(lane == j, incoming[j], wanted)
        own[...] = wanted
        for p in range(4):
            spread = jnp.full((8, 128), pick[p, 0], jnp.int32)
            for k in range(1, 8):
                spread = jnp.where(row == k, pick[p, k], spread)
            picks[p] = spread
        picked[s] = picks[s]
        pl.semaphore_wait(barrier, len(partners))
        for d in range(3):
            picks_copy(d).start()
        for way in range(2):
            relay_copy(way).start()
        for way in range(2):
            frames_copy(way).start()
        for d in range(2):
            near_copy(d).start()

        lane2 = lax.broadcasted_iota(jnp.int32, (8, 256), 1)
        row2 = lax.broadcasted_iota(jnp.int32, (8, 256), 0)
        used[...] = jnp.where(4 * (4 * (row2 % 2) + lane2 // 64) + row2 // 2 < count[s], 1.0, 0.0)
        coef[...] = jnp.zeros_like(coef)
        coef[0:36, :] = coef0[...]
        basis[pl.ds(36 * BODD, 4 * BODD), :] = jnp.zeros((4 * BODD, NPIX), F32)
        phi[...] = jnp.zeros_like(phi)
        for m in range(36):
            windows[m].wait()
            basis[pl.ds(m * BODD, XN), :] = window[m]
        for i in range(TILES):
            prep_basis(i, basis, basis6, last=i == TILES - 1)
        for d in range(3):
            picks_copy(d).wait()
        for a in range(4):
            onehot[8 * a : 8 * a + 8, :] = jnp.where(picked[a] == lane, 1.0, 0.0)
        for one in loads:
            one.wait()

        def transfer(keep, between=None):
            six[...] = coef_six(coef, onehot)
            phases(six, basis6, phi)
            if between is not None:
                between()
            forward(phi, mask, flip, w1, a2, t1, t2.at[0], field, amp, trans, keep)

        def ratios():
            pl.loop(0, 8, unroll=2)(lambda r: products(r, trans, spec, used, weight, cot))

        @pl.loop(0, ITERS)
        def iteration(it):
            def pass_on():
                @pl.when(it == 0)
                def _():
                    for way in range(2):
                        relay_copy(way).wait()
                        onward_copy(way).start()

            transfer(keep=True, between=pass_on)

            @pl.when(it == 0)
            def _():
                for way in range(2):
                    frames_copy(way).wait()
                prep_spectra([s] + ways, observed, t1, t2.at[2], spec)
                for way in range(2):
                    onward_copy(way).wait()
                prep_spectra([across], observed, t1, t2.at[2], spec)

            ratios()
            backward(cot, spec, trans, used, flip, t2.at[1], t1, a2t, w1t, amp, field, dphi)
            acc = modes(dphi, basis6)
            slot_grad = acc[:MROWS] + acc[MROWS:]
            twice = jnp.concatenate([onehot[...], onehot[...]], axis=0).astype(BF16)
            total = None
            for part in split3(slot_grad):
                one = mm(part.astype(BF16), twice)
                total = one if total is None else total + one
            halves[it, 0] = total[:24]
            halves[it, 1] = jnp.concatenate([total[24:], jnp.zeros((8, 128), F32)], axis=0)
            half = halves[it, tc]
            for stage in range(3):
                grads[it, stage, places[stage]] = half
                count = len(groups[stage])
                for d in range(count):
                    grad_copy(it, stage, d).start()
                for d in range(count):
                    grad_copy(it, stage, d).wait()
                if stage < 2:
                    half = grads[it, stage, 0]
                    for d in range(count):
                        half = half + grads[it, stage, d + 1]
            both = [
                grads[it, 2, 4 * c] + grads[it, 2, 4 * c + 1] + grads[it, 2, 4 * c + 2] + grads[it, 2, 4 * c + 3]
                for c in range(2)
            ]
            total = jnp.concatenate([both[0], both[1][:16]], axis=0)
            mean = jnp.sum(total * total) * (1.0 / (128.0 * 36.0))
            coef[...] = coef[...] - STEP * total / jnp.sqrt(jnp.full(total.shape, mean + EPS, F32))

        transfer(keep=False)
        ratios()
        lefts, _ = adjoint_lanes(cot[0] * (0.25 / NPIX), cot[1] * (0.25 / NPIX), t2.at[3])
        objects[s] = lanes_mul(lefts[0], t1.at[2])
        for d in range(3):
            gather_copy(d).start()
        for d in range(3):
            gather_copy(d).wait()

        for d in range(2):
            near_copy(d).wait()
        for d in range(2):
            wanted = near[1 - d]
            total = None
            for p in range(4):
                match = jnp.where(wanted == 4 * t + p, 1.0, 0.0)
                one = jnp.max(match[:1, :], axis=1, keepdims=True) * objects[p]
                total = one if total is None else total + one
            send[d] = total
            object_copy(d).start()
        for d in range(2):
            object_copy(d).wait()
        for j in range(4):
            source = incoming[j]
            total = jnp.where(source // 4 == (t + 31) % 32, arrive[0], arrive[1])
            for p in range(4):
                total = jnp.where(source == 4 * t + p, objects[p], total)
            out[j] = total
        coef_out[...] = coef[0:36, :]

    return kernel


def hand_on(objects, coef, out, coef_out):
    out[...] = objects[...]
    coef_out[...] = coef[...]


def per_device(observed, frame_pick, frame_count, incoming, start_coefficients, mode_basis):
    tables, mask, weight, flip = host_tables()
    vmem = pl.BlockSpec(memory_space=pltpu.VMEM)
    smem = pl.BlockSpec(memory_space=pltpu.SMEM)
    hbm = pl.BlockSpec(memory_space=pl.ANY)
    dma = pltpu.SemaphoreType.DMA
    objects, coef = pl.pallas_call(
        make_kernel(),
        out_shape=(
            jax.ShapeDtypeStruct((4, NPIX, NPIX), F32),
            jax.ShapeDtypeStruct((36, 128), F32),
        ),
        in_specs=[hbm, hbm, smem, smem, vmem, smem, vmem, vmem, vmem] + [hbm] * 6,
        out_specs=(vmem, vmem),
        scratch_shapes=[
            pltpu.VMEM((4, 8, NPIX, NPIX), BF16),
            pltpu.VMEM((2, 4, NPIX, NPIX), BF16),
            pltpu.VMEM((36, XN, NPIX), F32),
            pltpu.VMEM((MROWS * BODD, NPIX), F32),
            pltpu.VMEM((4, 8, 128), jnp.int32),
            pltpu.VMEM((4, 8, 128), jnp.int32),
            pltpu.VMEM((FR, 128), F32),
            pltpu.VMEM((8, 256), F32),
            pltpu.VMEM((MROWS, 128), F32),
            pltpu.VMEM((8, 128), jnp.int32),
            pltpu.VMEM((4, 256, 256), BF16),
            pltpu.VMEM((4, 128, 384), BF16),
            pltpu.VMEM((128, 224), BF16),
            pltpu.VMEM((80, 384), BF16),
            pltpu.VMEM((384, 256), BF16),
            pltpu.VMEM((256, 256), BF16),
            pltpu.VMEM((QUADS, 256, 256), F32),
            pltpu.VMEM((TILES, 256, 256), BF16),
            pltpu.VMEM((FR, 256), BF16),
            pltpu.VMEM((40 * ODD, 128), F32),
            pltpu.VMEM((40 * ODD, 128), F32),
            pltpu.VMEM((FR, XN, 128), F32),
            pltpu.VMEM((2 * QUADS, 256, 256), F32),
            pltpu.VMEM((QUADS, 256, 256), F32),
            pltpu.VMEM((3, 128, 128), F32),
            pltpu.VMEM((ITERS, 2, 24, 128), F32),
            pltpu.VMEM((ITERS, 3, 8, 24, 128), F32),
            pltpu.VMEM((4, 128, 128), F32),
            pltpu.VMEM((2, 8, 128), jnp.int32),
            pltpu.VMEM((2, 128, 128), F32),
            pltpu.VMEM((2, 128, 128), F32),
            dma((3, 2)),
            dma((3, 2)),
            dma((3,)),
            dma((3,)),
            dma((ITERS, 3, 7)),
            dma((ITERS, 3, 7)),
            dma((3,)),
            dma((3,)),
            dma((2, 2)),
            dma((2, 2)),
            dma((36,)),
            dma((7,)),
        ],
        compiler_params=pltpu.CompilerParams(
            collective_id=0, has_side_effects=True, vmem_limit_bytes=56 * 1024 * 1024
        ),
        cost_estimate=pl.CostEstimate(flops=30_000_000_000, bytes_accessed=10_000_000, transcendentals=0),
    )(
        observed, mode_basis, frame_pick, frame_count, start_coefficients.T, incoming,
        *[jnp.asarray(one) for one in [mask, weight, flip] + tables],
    )
    restored, coef = pl.pallas_call(
        hand_on,
        out_shape=(jax.ShapeDtypeStruct((4, NPIX, NPIX), F32), jax.ShapeDtypeStruct((36, 128), F32)),
        in_specs=[vmem, vmem],
        out_specs=(vmem, vmem),
        cost_estimate=pl.CostEstimate(flops=500_000, bytes_accessed=700_000, transcendentals=0),
    )(objects, coef)
    return restored, coef.T


def solution(mesh):
    placed = (P("tile", "spare", None, None), P("tile", "spare"), P("tile"), P("tile"), P(), P())
    return jax.shard_map(
        per_device,
        mesh=mesh,
        in_specs=placed,
        out_specs=(P("tile", None, None), P()),
        check_vma=False,
    )
```

```python
import math

import jax
import jax.numpy as jnp
import ml_dtypes
import numpy as np
from jax import lax
from jax.experimental import pallas as pl
from jax.experimental.pallas import tpu as pltpu
from jax.sharding import PartitionSpec as P

MESH = pl.DeviceIdType.MESH
F32 = jnp.float32
BF16 = jnp.bfloat16
NPIX = 128
ITERS = 2
GAMMA = 0.5
STEP = 0.25
EPS = 1e-06
X0, XN = 32, 72
MROWS = 40
FR = 32
ODD = 33
BODD = 73
QUADS = 8
PAIRS = 16
CHUNKS = 4
TILES = 17


def host_tables():
    index = np.arange(NPIX)
    angle = 2.0 * np.pi * (index[:, None] * index[None, :] % NPIX) / NPIX
    c, s = np.cos(angle), np.sin(angle)
    off = index - NPIX // 2
    disc = (off[:, None] ** 2 + off[None, :] ** 2 <= (NPIX // 4) ** 2).astype(np.float32)
    area = float(disc.sum())

    def two(table):
        high = table.astype(ml_dtypes.bfloat16)
        return high, (table - high.astype(np.float64)).astype(ml_dtypes.bfloat16)

    def wide(table, extra=0):
        high, low = two(table)
        return np.concatenate([high, high, low, np.zeros((len(table), extra), high.dtype)], axis=1)

    def tall(table):
        high, low = two(table)
        return np.concatenate([high, high, low], axis=0)

    def beside(table):
        return np.concatenate(two(table), axis=1)

    w1 = np.block([[c[32:96], -s[32:96]], [s[32:96], c[32:96]]]) / (NPIX * math.sqrt(area))
    w1t = np.concatenate([w1[64:].T, -w1[:64].T], axis=1)
    rows = np.concatenate([c[:64], c[64:65], s[1:64]], axis=0)
    order = np.concatenate([np.arange(65), 128 - np.arange(1, 64)])
    pupil = X0 + np.arange(XN)
    pupil[65] = NPIX // 2
    a2 = rows[:, pupil]
    a2t = np.concatenate([a2.T, np.zeros((8, NPIX))], axis=0)
    t2 = rows[:, order]
    cosine, sine = c[:, :64], -s[:, :64].copy()
    sine[:, 0] = c[:, 64]
    left, right = np.concatenate([cosine, sine], axis=1), np.concatenate([sine, cosine], axis=1)

    def twice(table):
        one = beside(table)
        return np.concatenate([one, one], axis=0)

    tables = [
        np.stack([twice(left), twice(right), twice(2.0 * left.T), twice(2.0 * right.T)]),
        np.stack([wide(t2), wide(t2.T), wide(rows), wide(rows.T)]),
        wide(a2, 8),
        wide(a2t),
        tall(w1),
        beside(w1t),
    ]
    mask = np.zeros((XN, 64), np.float32)
    mask[:65] = disc[X0 : X0 + 65, 32:96]
    mask[65, 0] = disc[64, 96]
    mask = np.concatenate([mask, mask], axis=1)
    weight = np.full((NPIX, NPIX), 4.0, np.float32)
    weight[:, 0] = 2.0
    weight[:, 64] = 2.0
    weight[64, 1] = 2.0
    weight[64, 65] = 2.0
    flip = np.ones((8, 256), np.float32)
    flip[1, 1::2] = -1.0
    return tables, mask, weight, flip


def split(x):
    high = x.astype(BF16)
    return high, (x - high.astype(F32)).astype(BF16)


def split3(x):
    high = x.astype(BF16).astype(F32)
    rest = x - high
    mid = rest.astype(BF16).astype(F32)
    return high, mid, rest - mid


def mm(a, b):
    return jnp.dot(a, b, preferred_element_type=F32)


def mm_nt(a, b):
    return lax.dot_general(a, b, (((1,), (1,)), ((), ())), preferred_element_type=F32)


def right_mul(x, table):
    high, low = split(x)
    return mm(jnp.concatenate([high, low, high], axis=1), table[...])


def left_mul(table, x):
    high, low = split(x)
    return mm(table[...], jnp.concatenate([high, low, high], axis=0))


def left_pupil(table, x):
    high = x.astype(BF16).astype(F32)
    zero = jnp.zeros((8, x.shape[1]), F32)
    return mm(table[...], jnp.concatenate([high, x - high, high, zero], axis=0).astype(BF16))


def lanes_mul(x, table):
    both = mm(jnp.concatenate(split(x), axis=1), table[...])
    return both[:, :128] + both[:, 128:]


def row0(v, first):
    here = lax.broadcasted_iota(jnp.int32, (8, v.shape[1]), 0) == 0
    return jnp.concatenate([jnp.where(here, first, v[:8]), v[8:]], axis=0)


def unfold(real, imag):
    cr, sr, ci, si = real[:64], real[64:], imag[:64], imag[64:]
    sr0, si0 = row0(sr, 0.0), row0(si, 0.0)
    return (
        jnp.concatenate([cr + si0, row0(cr - si0, sr[:8])], axis=0),
        jnp.concatenate([ci - sr0, row0(ci + sr0, si[:8])], axis=0),
    )


def fold(gr, gi):
    ga, gb, ha, hb = gr[:64], gr[64:], gi[:64], gi[64:]
    return (
        jnp.concatenate([row0(ga + gb, ga[:8]), row0(hb - ha, gb[:8])], axis=0),
        jnp.concatenate([row0(ha + hb, ha[:8]), row0(ga - gb, hb[:8])], axis=0),
    )


COS_POLY = (0.9999999889, -19.7392044666, 64.9391159283, -85.4501134275, 60.1674297919, -25.9668846126, 6.5277059630)


def horner(poly, z):
    total = poly[-1]
    for one in poly[-2::-1]:
        total = total * z + one
    return total


def unit_field(turns, mask):
    r = turns - jnp.floor(turns + 0.5)
    return mask * horner(COS_POLY, r * r)


def lane_mask(width, first):
    lane = lax.broadcasted_iota(jnp.int32, (8, width), 1)
    return (lane % 64) == first


def rows64(arr, fix):
    return jnp.concatenate([arr[:64], fix(arr[64:72]), arr[72:]], axis=0)


def left_half():
    return lax.broadcasted_iota(jnp.int32, (8, 128), 1)[:1] < 64


def half_spectra(lefts, rights, t2):
    low, at0 = left_half(), lane_mask(128, 0)[:1]
    lone, real, imag = [], [], []
    for one, two in zip(lefts, rights):
        di = pltpu.roll(jnp.where(low, two, one), 64, 1)
        total = jnp.sum(di, axis=0, keepdims=True)
        lone.append(pltpu.roll(jnp.broadcast_to(total, (8, 128)), 1, 1))
        real.append(jnp.where(low, one, two))
        imag.append(jnp.where(at0, 0.0, di))
    tr, ti = unfold(left_mul(t2, jnp.concatenate(real, axis=1)), left_mul(t2, jnp.concatenate(imag, axis=1)))
    here = lane_mask(256, 1) & (lax.broadcasted_iota(jnp.int32, (8, 256), 0) == 0)
    lone = jnp.concatenate(lone, axis=1)
    return rows64(tr, lambda v: jnp.where(here, lone, v)), rows64(ti, lambda v: jnp.where(here, 0.0, v))


def adjoint_lanes(gr, gi, t2t):
    width = gr.shape[1]
    here = lane_mask(width, 1) & (lax.broadcasted_iota(jnp.int32, (8, width), 0) == 0)
    lone = jnp.where(here, gr[64:72], 0.0)
    xr, xi = fold(
        rows64(gr, lambda v: jnp.where(here, 0.0, v)), rows64(gi, lambda v: jnp.where(here, 0.0, v))
    )
    dr, di = left_mul(t2t, xr), left_mul(t2t, xi)
    low, at0 = left_half(), lane_mask(128, 0)[:1]
    lefts, rights = [], []
    for i in range(width // 128):
        cols = slice(128 * i, 128 * i + 128)
        back = pltpu.roll(lone[:, cols], 127, 1)[:1]
        turned = pltpu.roll(jnp.where(at0, back, di[:, cols]), 64, 1)
        lefts.append(jnp.where(low, dr[:, cols], turned))
        rights.append(jnp.where(low, turned, dr[:, cols]))
    return lefts, rights


def rows_of(x, n):
    return x[128 * n : 128 * n + 128]


def staggered(*stages):
    for step in range(CHUNKS + len(stages) - 1):
        for k, stage in enumerate(stages):
            if 0 <= step - k < CHUNKS:
                stage(step - k)


def make_kernel():
    def prep_spectra(sources, observed, t1, t2, spec):
        lanes = []
        for source in sources:
            sides = []
            for half in range(2):
                both = [mm(observed[source, 2 * i + half], t1[half, 0:128, :]) for i in range(4)]
                sides.append([(one[:, :128] + one[:, 128:]) * (1.0 / NPIX) for one in both])
            lanes.append(sides)
        for source, sides in zip(sources, lanes):
            for j in range(2):
                real, imag = half_spectra(sides[0][2 * j : 2 * j + 2], sides[1][2 * j : 2 * j + 2], t2)
                spec[2 * source + j, :128, :] = real
                spec[2 * source + j, 128:, :] = imag

    def prep_basis(i, basis, basis6, last=False):
        lane = lax.broadcasted_iota(jnp.int32, (MROWS, 128), 1)
        halves = []
        for j in range(2):
            if last:
                rows = pltpu.roll(basis[pl.ds(64 - 32 * j, MROWS, stride=BODD), :], 96 - 64 * j, 1)
            else:
                one = pltpu.roll(basis[pl.ds(2 * i + j, MROWS, stride=BODD), :], 96, 1)
                other = pltpu.roll(basis[pl.ds(2 * i + j + 32, MROWS, stride=BODD), :], 32, 1)
                rows = jnp.where(lane < 64, one, other)
            high, mid, low = split3(rows)
            halves.append(
                jnp.concatenate([high, mid, high, low, mid, high, jnp.zeros((16, NPIX), F32)], axis=0)
            )
        basis6[i] = jnp.concatenate(halves, axis=1).astype(BF16)

    def coef_six(coef, onehot):
        high, mid, low = split3(coef[...] * (0.5 / math.pi))
        stack = jnp.concatenate([high, high, mid, high, mid, low, jnp.zeros((16, NPIX), F32)], axis=0)
        return mm_nt(onehot[...].astype(BF16), stack.astype(BF16)).astype(BF16)

    def phases(six, basis6, phi):
        for i in range(TILES):
            both = mm(six[...], basis6[i])
            phi[pl.ds(2 * i * ODD, FR), :] = both[:, :128]
            phi[pl.ds((2 * i + 1) * ODD, FR), :] = both[:, 128:]

    def frame_field(f, phi, mask):
        lane = lax.broadcasted_iota(jnp.int32, (8, 128), 1)[:1]
        packed = phi[pl.ds(f, 40, stride=ODD), :]
        turned = pltpu.roll(packed, 64, 1)
        phase = jnp.concatenate(
            [jnp.where(lane < 64, packed, turned), jnp.where(lane < 64, turned[:32], packed[:32])], axis=0
        )
        phase = jnp.concatenate([phase[:32], phase[40:], phase[32:40]], axis=0)
        return unit_field(phase - jnp.where(lane < 64, 0.0, 0.25), mask[...])

    def modes(dphi, basis6):
        total = None
        for i in range(TILES):
            a = dphi[pl.ds(2 * i * ODD, FR), :]
            b = dphi[pl.ds((2 * i + 1) * ODD, FR), :]
            high, low = split(jnp.concatenate([a, b], axis=1))
            part = mm_nt(basis6[i, 0 : 2 * MROWS, :], jnp.concatenate([high, low], axis=0))
            total = part if total is None else total + part
        return total

    def forward(phi, mask, flip, w1, a2, t1, t2, field, amp, trans, keep):
        first, second, third = {}, {}, {}

        def along_y(c):
            stack = []
            for f in range(8 * c, 8 * c + 8):
                one = frame_field(f, phi, mask)
                if keep:
                    field[f] = one
                stack.append(one)
            first[c] = right_mul(jnp.concatenate(stack, axis=0), w1)

        def along_x(c):
            b, spreads = first.pop(c), [[], []]
            for i in range(4):
                parts = []
                for half in range(2):
                    one = b[XN * (2 * i + half) : XN * (2 * i + half + 1)]
                    parts.append(jnp.concatenate([one[:64], one[64:] * flip[...]], axis=0))
                ar, ai = unfold(
                    left_pupil(a2, jnp.concatenate([parts[0][:, :128], parts[1][:, :128]], axis=1)),
                    left_pupil(a2, jnp.concatenate([parts[0][:, 128:], parts[1][:, 128:]], axis=1)),
                )
                if keep:
                    amp[4 * c + i, :128, :] = ar
                    amp[4 * c + i, 128:, :] = ai
                spread = ar * ar + ai * ai
                for half in range(2):
                    spreads[half].append(spread[:, 128 * half : 128 * half + 128])
            second[c] = spreads

        def lanes(c):
            spreads = second.pop(c)
            third[c] = [lanes_mul(jnp.concatenate(spreads[half], axis=0), t1.at[half]) for half in range(2)]

        def rows(c):
            d = third.pop(c)
            for g in range(2):
                tr, ti = half_spectra(*[[rows_of(d[half], 2 * g), rows_of(d[half], 2 * g + 1)] for half in range(2)], t2)
                trans[2 * c + g, :128, :] = tr
                trans[2 * c + g, 128:, :] = ti

        staggered(along_y, along_x, lanes, rows)

    def products(r, trans, spec, used, weight, cot):
        nr = ni = de = None
        upper, lower = pl.ds(pl.multiple_of(16 * r, 16), 16), pl.ds(pl.multiple_of(128 + 16 * r, 16), 16)
        for g in range(QUADS):
            u = used[g : g + 1, :]
            tr, ti, sr, si = trans[g, upper, :], trans[g, lower, :], spec[g, upper, :], spec[g, lower, :]
            vr, vi = tr * u, ti * u
            one = (sr * vr + si * vi, si * vr - sr * vi, tr * vr + ti * vi)
            nr, ni, de = one if g == 0 else (nr + one[0], ni + one[1], de + one[2])
        total = []
        for v in (nr, ni, de):
            v = v[:, :128] + v[:, 128:]
            total.append(v + pltpu.roll(v, 64, 1))
        scale = 1.0 / (GAMMA + total[2])
        qr, qi = total[0] * scale, total[1] * scale
        w = weight[upper, :]
        cot[0, upper, :] = w * qr
        cot[1, upper, :] = w * qi
        cot[2, upper, :] = w * (qr * qr + qi * qi)

    def backward(cot, spec, trans, used, flip, t2t, t1, a2t, w1t, amp, field, dphi):
        qr, qi, qq = [jnp.concatenate([cot[n], cot[n]], axis=1) for n in range(3)]
        lane = lax.broadcasted_iota(jnp.int32, (8, 128), 1)[:1]
        first, second, third = {}, {}, {}

        def rows(c):
            sides = [[], []]
            for g in (2 * c, 2 * c + 1):
                u = used[g : g + 1, :]
                tr, ti = trans[g, :128, :], trans[g, 128:, :]
                sr, si = spec[g, :128, :], spec[g, 128:, :]
                gr = u * (qq * tr - qr * sr - qi * si)
                gi = u * (qi * sr - qr * si + qq * ti)
                for half, one in enumerate(adjoint_lanes(gr, gi, t2t)):
                    sides[half] += one
            first[c] = sides

        def lanes(c):
            sides = first.pop(c)
            second[c] = [lanes_mul(jnp.concatenate(sides[half], axis=0), t1.at[2 + half]) for half in range(2)]

        def along_x(c):
            ds, stack = second.pop(c), []
            for i in range(4):
                one = jnp.concatenate([rows_of(ds[0], i), rows_of(ds[1], i)], axis=1)
                xr, xi = fold(amp[4 * c + i, :128, :] * one, amp[4 * c + i, 128:, :] * one)
                dbr, dbi = left_mul(a2t, xr), left_mul(a2t, xi)
                for half in range(2):
                    cols = slice(128 * half, 128 * half + 128)
                    one = jnp.concatenate([dbr[:XN, cols], dbi[:XN, cols]], axis=1)
                    stack += [one[:64], one[64:] * flip[...]]
            third[c] = stack

        def along_y(c):
            x = jnp.concatenate(third.pop(c), axis=0)
            n = x.shape[0]
            both = mm(jnp.concatenate(split(x), axis=0), w1t[...])
            d = both[:n, :128] + both[:n, 128:] + both[n:, :128] + both[n:, 128:]
            for place in range(8):
                f = 8 * c + place
                v = field[f] * d[XN * place : XN * place + XN]
                v = v + pltpu.roll(v, 64, 1)
                dphi[pl.ds(f, 40, stride=ODD), :] = jnp.concatenate(
                    [jnp.where(lane < 64, v[:32], v[32:64]), jnp.where(lane < 64, v[64:], 0.0)], axis=0
                )

        staggered(rows, lanes, along_x, along_y)

    def kernel(
        observed_h, basis_h, pick, count, coef0, incoming, mask, weight, flip,
        t1_h, t2_h, a2_h, a2t_h, w1_h, w1t_h,
        out, coef_out,
        observed, relay, window, basis, picks, picked, onehot, used, coef, own, t1, t2, a2, a2t, w1, w1t,
        spec, basis6, six, phi, dphi, field, amp, trans, cot, grads, objects, near, send, arrive,
        ob_send, ob_recv, pk_send, pk_recv, gr_send, gr_recv, ag_send, ag_recv, nb_send, nb_recv, basis_sem, load_sem,
    ):
        t, s = lax.axis_index("tile"), lax.axis_index("spare")
        tx, tz, tc = t // 8, (t // 2) % 4, t % 2
        spare_of = [(s + d) % 4 for d in (1, 2, 3)]
        groups = [
            [(t, v) for v in spare_of] + [(t + 1 - 2 * tc, (s + d) % 4) for d in range(4)],
            [
                (((tx + dx) % 4) * 8 + ((tz + dz) % 4) * 2 + tc, s)
                for dx, dz in [(1, 0), (0, 1), (3, 0), (0, 3), (1, 1), (3, 3), (1, 3), (3, 1), (2, 0), (0, 2)]
                + [(2, 1), (1, 2), (2, 3), (3, 2), (2, 2)]
            ],
        ]
        places = [tc * 4 + s, 4 * tx + tz]
        beside = [((t + 1) % 32, s), ((t + 31) % 32, s)]

        barrier = pltpu.get_barrier_semaphore()
        partners = [who for group in groups for who in group] + beside
        for who in partners:
            pl.semaphore_signal(barrier, inc=1, device_id=who, device_id_type=MESH)

        loads = [
            pltpu.make_async_copy(src, dst, load_sem.at[n])
            for n, (src, dst) in enumerate(
                [(observed_h.at[s], observed.at[s]), (t1_h, t1), (t2_h, t2), (a2_h, a2), (a2t_h, a2t), (w1_h, w1), (w1t_h, w1t)]
            )
        ]
        windows = [
            pltpu.make_async_copy(
                basis_h.at[m, pl.ds(X0, XN), :], window.at[m], basis_sem.at[m]
            )
            for m in range(36)
        ]
        for one in windows + loads:
            one.start()

        def remote(src, dst, ssem, rsem, who):
            return pltpu.make_async_remote_copy(
                src_ref=src, dst_ref=dst, send_sem=ssem, recv_sem=rsem, device_id=who, device_id_type=MESH
            )

        def near_copy(d):
            return remote(own, near.at[d], nb_send.at[0, d], nb_recv.at[0, d], beside[d])

        def object_copy(d):
            return remote(send.at[d], arrive.at[d], nb_send.at[1, d], nb_recv.at[1, d], beside[d])

        ways = [(s + 1) % 4, (s + 3) % 4]
        across = (s + 2) % 4

        def frames_copy(way):
            return remote(
                observed_h.at[ways[way]], observed.at[s], ob_send.at[0, way], ob_recv.at[0, way], (t, ways[way])
            )

        def relay_copy(way):
            return remote(
                observed_h.at[across, pl.ds(4 * way, 4)], relay.at[way], ob_send.at[1, way], ob_recv.at[1, way], (t, ways[way])
            )

        def onward_copy(way):
            return remote(
                relay.at[way], observed.at[ways[1 - way], pl.ds(4 * way, 4)], ob_send.at[2, way], ob_recv.at[2, way],
                (t, ways[way]),
            )

        def picks_copy(d):
            return remote(picks.at[spare_of[d]], picked.at[s], pk_send.at[d], pk_recv.at[d], groups[0][d])

        def gather_copy(d):
            return remote(objects.at[s], objects.at[s], ag_send.at[d], ag_recv.at[d], groups[0][d])

        def grad_copy(it, stage, d):
            here = grads.at[it, stage, places[stage]]
            return remote(here, here, gr_send.at[it, stage, d], gr_recv.at[it, stage, d], groups[stage][d])

        lane = lax.broadcasted_iota(jnp.int32, (8, 128), 1)
        row = lax.broadcasted_iota(jnp.int32, (8, 128), 0)
        wanted = jnp.full((8, 128), -1, jnp.int32)
        for j in range(4):
            wanted = jnp.where(lane == j, incoming[j], wanted)
        own[...] = wanted
        for p in range(4):
            spread = jnp.full((8, 128), pick[p, 0], jnp.int32)
            for k in range(1, 8):
                spread = jnp.where(row == k, pick[p, k], spread)
            picks[p] = spread
        picked[s] = picks[s]
        pl.semaphore_wait(barrier, len(partners))
        for d in range(3):
            picks_copy(d).start()
        for way in range(2):
            relay_copy(way).start()
        for way in range(2):
            frames_copy(way).start()
        for d in range(2):
            near_copy(d).start()

        lane2 = lax.broadcasted_iota(jnp.int32, (8, 256), 1)
        row2 = lax.broadcasted_iota(jnp.int32, (8, 256), 0)
        used[...] = jnp.where(4 * (4 * (row2 % 2) + lane2 // 64) + row2 // 2 < count[s], 1.0, 0.0)
        coef[...] = jnp.zeros_like(coef)
        coef[0:36, :] = coef0[...]
        basis[pl.ds(36 * BODD, 4 * BODD), :] = jnp.zeros((4 * BODD, NPIX), F32)
        phi[...] = jnp.zeros_like(phi)
        for m in range(36):
            windows[m].wait()
            basis[pl.ds(m * BODD, XN), :] = window[m]
        for i in range(TILES):
            prep_basis(i, basis, basis6, last=i == TILES - 1)
        for d in range(3):
            picks_copy(d).wait()
        for a in range(4):
            onehot[8 * a : 8 * a + 8, :] = jnp.where(picked[a] == lane, 1.0, 0.0)
        for one in loads:
            one.wait()

        def transfer(keep, between=None):
            six[...] = coef_six(coef, onehot)
            phases(six, basis6, phi)
            if between is not None:
                between()
            forward(phi, mask, flip, w1, a2, t1, t2.at[0], field, amp, trans, keep)

        def ratios():
            pl.loop(0, 8, unroll=2)(lambda r: products(r, trans, spec, used, weight, cot))

        @pl.loop(0, ITERS)
        def iteration(it):
            def pass_on():
                @pl.when(it == 0)
                def _():
                    for way in range(2):
                        relay_copy(way).wait()
                        onward_copy(way).start()

            transfer(keep=True, between=pass_on)

            @pl.when(it == 0)
            def _():
                for way in range(2):
                    frames_copy(way).wait()
                prep_spectra([s] + ways, observed, t1, t2.at[2], spec)
                for way in range(2):
                    onward_copy(way).wait()
                prep_spectra([across], observed, t1, t2.at[2], spec)

            ratios()
            backward(cot, spec, trans, used, flip, t2.at[1], t1, a2t, w1t, amp, field, dphi)
            acc = modes(dphi, basis6)
            slot_grad = acc[:MROWS] + acc[MROWS:]
            twice = jnp.concatenate([onehot[...], onehot[...]], axis=0).astype(BF16)
            total = None
            for part in split3(slot_grad):
                one = mm(part.astype(BF16), twice)
                total = one if total is None else total + one
            for stage in range(2):
                grads[it, stage, places[stage]] = total
                count = len(groups[stage])
                for d in range(count):
                    grad_copy(it, stage, d).start()
                for d in range(count):
                    grad_copy(it, stage, d).wait()
                total = grads[it, stage, 0]
                for d in range(count):
                    total = total + grads[it, stage, d + 1]
            mean = jnp.sum(total * total) * (1.0 / (128.0 * 36.0))
            coef[...] = coef[...] - STEP * total / jnp.sqrt(jnp.full(total.shape, mean + EPS, F32))

        transfer(keep=False)
        ratios()
        lefts, _ = adjoint_lanes(cot[0] * (0.25 / NPIX), cot[1] * (0.25 / NPIX), t2.at[3])
        objects[s] = lanes_mul(lefts[0], t1.at[2])
        for d in range(3):
            gather_copy(d).start()
        for d in range(3):
            gather_copy(d).wait()

        for d in range(2):
            near_copy(d).wait()
        for d in range(2):
            wanted = near[1 - d]
            total = None
            for p in range(4):
                match = jnp.where(wanted == 4 * t + p, 1.0, 0.0)
                one = jnp.max(match[:1, :], axis=1, keepdims=True) * objects[p]
                total = one if total is None else total + one
            send[d] = total
            object_copy(d).start()
        for d in range(2):
            object_copy(d).wait()
        for j in range(4):
            source = incoming[j]
            total = jnp.where(source // 4 == (t + 31) % 32, arrive[0], arrive[1])
            for p in range(4):
                total = jnp.where(source == 4 * t + p, objects[p], total)
            out[j] = total
        coef_out[...] = coef[0:36, :]

    return kernel


def hand_on(objects, coef, out, coef_out):
    out[...] = objects[...]
    coef_out[...] = coef[...]


def per_device(observed, frame_pick, frame_count, incoming, start_coefficients, mode_basis):
    tables, mask, weight, flip = host_tables()
    vmem = pl.BlockSpec(memory_space=pltpu.VMEM)
    smem = pl.BlockSpec(memory_space=pltpu.SMEM)
    hbm = pl.BlockSpec(memory_space=pl.ANY)
    dma = pltpu.SemaphoreType.DMA
    objects, coef = pl.pallas_call(
        make_kernel(),
        out_shape=(
            jax.ShapeDtypeStruct((4, NPIX, NPIX), F32),
            jax.ShapeDtypeStruct((36, 128), F32),
        ),
        in_specs=[hbm, hbm, smem, smem, vmem, smem, vmem, vmem, vmem] + [hbm] * 6,
        out_specs=(vmem, vmem),
        scratch_shapes=[
            pltpu.VMEM((4, 8, NPIX, NPIX), BF16),
            pltpu.VMEM((2, 4, NPIX, NPIX), BF16),
            pltpu.VMEM((36, XN, NPIX), F32),
            pltpu.VMEM((MROWS * BODD, NPIX), F32),
            pltpu.VMEM((4, 8, 128), jnp.int32),
            pltpu.VMEM((4, 8, 128), jnp.int32),
            pltpu.VMEM((FR, 128), F32),
            pltpu.VMEM((8, 256), F32),
            pltpu.VMEM((MROWS, 128), F32),
            pltpu.VMEM((8, 128), jnp.int32),
            pltpu.VMEM((4, 256, 256), BF16),
            pltpu.VMEM((4, 128, 384), BF16),
            pltpu.VMEM((128, 224), BF16),
            pltpu.VMEM((80, 384), BF16),
            pltpu.VMEM((384, 256), BF16),
            pltpu.VMEM((256, 256), BF16),
            pltpu.VMEM((QUADS, 256, 256), F32),
            pltpu.VMEM((TILES, 256, 256), BF16),
            pltpu.VMEM((FR, 256), BF16),
            pltpu.VMEM((40 * ODD, 128), F32),
            pltpu.VMEM((40 * ODD, 128), F32),
            pltpu.VMEM((FR, XN, 128), F32),
            pltpu.VMEM((2 * QUADS, 256, 256), F32),
            pltpu.VMEM((QUADS, 256, 256), F32),
            pltpu.VMEM((3, 128, 128), F32),
            pltpu.VMEM((ITERS, 2, 16, MROWS, 128), F32),
            pltpu.VMEM((4, 128, 128), F32),
            pltpu.VMEM((2, 8, 128), jnp.int32),
            pltpu.VMEM((2, 128, 128), F32),
            pltpu.VMEM((2, 128, 128), F32),
            dma((3, 2)),
            dma((3, 2)),
            dma((3,)),
            dma((3,)),
            dma((ITERS, 2, 15)),
            dma((ITERS, 2, 15)),
            dma((3,)),
            dma((3,)),
            dma((2, 2)),
            dma((2, 2)),
            dma((36,)),
            dma((7,)),
        ],
        compiler_params=pltpu.CompilerParams(
            collective_id=0, has_side_effects=True, vmem_limit_bytes=56 * 1024 * 1024
        ),
        cost_estimate=pl.CostEstimate(flops=30_000_000_000, bytes_accessed=10_000_000, transcendentals=0),
    )(
        observed, mode_basis, frame_pick, frame_count, start_coefficients.T, incoming,
        *[jnp.asarray(one) for one in [mask, weight, flip] + tables],
    )
    restored, coef = pl.pallas_call(
        hand_on,
        out_shape=(jax.ShapeDtypeStruct((4, NPIX, NPIX), F32), jax.ShapeDtypeStruct((36, 128), F32)),
        in_specs=[vmem, vmem],
        out_specs=(vmem, vmem),
        cost_estimate=pl.CostEstimate(flops=500_000, bytes_accessed=700_000, transcendentals=0),
    )(objects, coef)
    return restored, coef.T


def solution(mesh):
    placed = (P("tile", "spare", None, None), P("tile", "spare"), P("tile"), P("tile"), P(), P())
    return jax.shard_map(
        per_device,
        mesh=mesh,
        in_specs=placed,
        out_specs=(P("tile", None, None), P()),
        check_vma=False,
    )
```
